32 devices in a mesh: blk: 16 (over z, y, core), lay: 2 (over x).
Axes of the slice: x: 2, y: 2, z: 4, core: 2. Of those that a mesh axis runs over, the one named last changes fastest.
Arguments:
- spectra: bfloat16 [2, 64, 4, 1024], P(None, 'blk'), may hold values from -6 to 6
- model_corr: bfloat16 [16, 8, 4, 4, 1024], P('blk', 'lay'), may hold values from -6 to 6
- window_start: int32 [16, 8], P('blk', 'lay'), may hold values from 0 to 511
- window_end: int32 [16, 8], P('blk', 'lay'), may hold values from 513 to 1024
- station_slot: int32 [16, 4], P('blk'), may hold values from 0 to 3, each once within a row
Outputs:
- adjoint: float32 [2, 64, 4, 1024], P(None, 'blk', None, 'lay')
The draws below stay inside these ranges and needn't reach their ends.
Inputs may be any that keep to these rules, and one draw needn't show every extreme that they name: `station_slot`: each row lists every number from 0 to 3 once. `window_start`: every taper starts before the middle lag sample. `window_end`: every taper ends after the middle lag sample.
All inputs are finite; a program needn't handle non-finite values.
Results may differ from the reference program's by a relative error of at most 0.0022.
Values may be sent and summed in bfloat16 or wider, within the bound.
No kernel may reach another device: no remote copies, remote signals or barrier semaphores. Data moves between devices by JAX's collectives and lax.ppermute only.
A program may use at most 64 MiB of HBM per device.

```python
import functools
import math
import jax
import jax.numpy as jnp
from jax import lax

STA = 4
WIN = 4
FREQ = 1024
LAGS = 1024
NBLK = 16
OFFSETS = 8
NSTA = 64


def plant(array, stream_key, low, top_value):
    spot = [jax.random.randint(jax.random.fold_in(stream_key, axis), (), 0, length) for axis, length in enumerate(array.shape)]
    main_axis = array.shape.index(max(array.shape))
    beside = spot[:main_axis] + [(spot[main_axis] + 1) % array.shape[main_axis]] + spot[main_axis + 1:]
    return array.at[tuple(spot)].set(low).at[tuple(beside)].set(top_value)


def levels(own_key, shape, pieces, least, high):
    def one(position, blocks):
        heights = jax.random.uniform(jax.random.fold_in(jax.random.fold_in(own_key, 6), position), (blocks,), jnp.float32, least / len(pieces), high / len(pieces))
        return jnp.repeat(jnp.exp(heights), shape[position] // blocks).reshape((-1,) + (1,) * (len(shape) - position - 1))

    level = one(*pieces[0])
    for cut in pieces[1:]:
        level = level * one(*cut)
    return level


def noise(rng, shape, deviation, most, shards=(), kind=jnp.bfloat16):
    values = jax.random.normal(rng, shape, jnp.float32) * deviation
    if len(shards) > 0:
        values = levels(rng, shape, shards, -0.22, 0.18) * values
    return jnp.clip(values, min=-most, max=most).astype(kind)


def setup_inputs(seed: int = 0) -> dict:
    streams_of = jax.random.split(jax.random.key(seed), 6)
    return {
        "spectra": noise(streams_of[0], (2, NSTA, WIN, FREQ), 1.0, 6.0, ((1, 16),)),
        "model_corr": noise(streams_of[1], (NBLK, OFFSETS, STA, STA, LAGS), 1.0, 6.0, ((0, 16), (1, 2))),
        "window_start": plant(jax.random.randint(streams_of[2], (NBLK, OFFSETS), 0, LAGS // 2), jax.random.fold_in(streams_of[2], 1), 0, (LAGS // 2) - 1).astype(jnp.int32),
        "window_end": plant(jax.random.randint(streams_of[3], (NBLK, OFFSETS), LAGS // 2 + 1, LAGS + 1), jax.random.fold_in(streams_of[3], 1), LAGS // 2 + 1, LAGS).astype(jnp.int32),
        "station_slot": jax.vmap(lambda own: jax.random.permutation(own, STA))(jax.random.split(streams_of[4], NBLK)).reshape((NBLK, STA)).astype(jnp.int32),
    }


def lag_table(freq_count, lag_count, window_count):
    freq_index = jnp.arange(freq_count, dtype=jnp.int32)
    lag_index = jnp.arange(lag_count, dtype=jnp.int32) - lag_count // 2
    phase_index = freq_index[:, None] * lag_index[None, :] % (2 * freq_count)
    angle = phase_index.astype(jnp.float32) * (math.pi / freq_count)
    factor = 1.0 / math.sqrt(2.0 * freq_count * window_count)
    cosine = (jnp.cos(angle) * factor).astype(jnp.bfloat16)
    sine = (-jnp.sin(angle) * factor).astype(jnp.bfloat16)
    return jnp.concatenate([cosine, sine], axis=0)

def reference(spectra, model_corr, window_start, window_end, station_slot):
    blocked = spectra.reshape(2, NBLK, STA, WIN, FREQ)
    slot_index = jnp.broadcast_to(station_slot.astype(jnp.int32)[None, :, :, None, None], blocked.shape)
    ordered = jnp.take_along_axis(blocked, slot_index, axis=2)
    table = lag_table(FREQ, LAGS, WIN).astype(jnp.float32)
    lag_pos = jnp.arange(LAGS, dtype=jnp.int32)
    station_pos = jnp.arange(STA, dtype=jnp.int32)
    diagonal = station_pos[:, None] == station_pos[None, :]
    einsum_high = functools.partial(jnp.einsum, precision=lax.Precision.HIGHEST)
    first = ordered.astype(jnp.float32)

    def one_offset(summed, offset):
        second = jnp.roll(ordered, -offset, axis=1).astype(jnp.float32)
        cross_re = einsum_high('bitf,bjtf->bijf', first[0], second[0]) + einsum_high('bitf,bjtf->bijf', first[1], second[1])
        cross_im = einsum_high('bitf,bjtf->bijf', first[1], second[0]) - einsum_high('bitf,bjtf->bijf', first[0], second[1])
        cross = jnp.concatenate([cross_re.astype(jnp.bfloat16), cross_im.astype(jnp.bfloat16)], axis=3)
        cross = lax.optimization_barrier(cross).astype(jnp.float32)
        lagged = jnp.dot(cross.reshape(-1, 2 * FREQ), table, precision=lax.Precision.HIGHEST)
        lagged = lagged.reshape(NBLK, STA, STA, LAGS)
        model = lax.dynamic_index_in_dim(model_corr, offset, 1, keepdims=False).astype(jnp.float32)
        starts = lax.dynamic_index_in_dim(window_start, offset, 1, keepdims=False)
        ends = lax.dynamic_index_in_dim(window_end, offset, 1, keepdims=False)
        inside = (lag_pos[None, :] >= starts[:, None]) & (lag_pos[None, :] < ends[:, None])
        paired = jnp.logical_not((offset == 0) & diagonal)
        keep = inside[:, None, None, :] & paired[None, :, :, None]
        misfit = jnp.where(keep, lagged - model, 0.0).astype(jnp.bfloat16)
        misfit = lax.optimization_barrier(misfit).astype(jnp.float32)
        response = jnp.dot(misfit.reshape(-1, LAGS), table.T, precision=lax.Precision.HIGHEST).astype(jnp.bfloat16)
        response = lax.optimization_barrier(response).astype(jnp.float32).reshape(NBLK, STA, STA, 2 * FREQ)
        resp_re = response[..., :FREQ]
        resp_im = response[..., FREQ:]
        own_re = einsum_high('bijf,bjtf->bitf', resp_re, second[0]) - einsum_high('bijf,bjtf->bitf', resp_im, second[1])
        own_im = einsum_high('bijf,bjtf->bitf', resp_re, second[1]) + einsum_high('bijf,bjtf->bitf', resp_im, second[0])
        part_re = einsum_high('bijf,bitf->bjtf', resp_re, first[0]) + einsum_high('bijf,bitf->bjtf', resp_im, first[1])
        part_im = einsum_high('bijf,bitf->bjtf', resp_re, first[1]) - einsum_high('bijf,bitf->bjtf', resp_im, first[0])
        own_side = jnp.stack([own_re, own_im])
        partner_side = jnp.stack([part_re, part_im])
        summed = summed + own_side + jnp.roll(partner_side, offset, axis=1)
        return (summed, None)
    start_sum = jnp.zeros((2, NBLK, STA, WIN, FREQ), jnp.float32)
    summed, _ = lax.scan(one_offset, start_sum, jnp.arange(OFFSETS, dtype=jnp.int32))
    scaled = summed * (1.0 / math.sqrt(NSTA))
    block_rows = jnp.arange(NBLK, dtype=jnp.int32)[:, None]
    result = jnp.zeros_like(scaled).at[:, block_rows, station_slot.astype(jnp.int32)].set(scaled)
    return result.reshape(2, NSTA, WIN, FREQ)
```

```python
import math

import jax
import jax.numpy as jnp
import ml_dtypes
import numpy as np
from jax import lax
from jax.sharding import PartitionSpec as P


def from_behind(value, axis, steps):
    count = lax.axis_size(axis)
    pairs = [(source, (source + steps) % count) for source in range(count)]
    return lax.ppermute(value, axis, pairs)


def lag_table(freq_count, lag_count, window_count):
    freq_index = np.arange(freq_count, dtype=np.int64)
    lag_index = np.arange(lag_count, dtype=np.int64) - lag_count // 2
    phase_index = freq_index[:, None] * lag_index[None, :] % (2 * freq_count)
    angle = phase_index.astype(np.float64) * (math.pi / freq_count)
    factor = 1.0 / math.sqrt(2.0 * freq_count * window_count)
    table = np.concatenate([np.cos(angle) * factor, -np.sin(angle) * factor], axis=0)
    return jnp.asarray(table.astype(ml_dtypes.bfloat16))


def summed_over_layers(value, layer_index, layer_count):
    width = value.shape[3] // layer_count
    own_part = lax.dynamic_slice_in_dim(value, layer_index * width, width, axis=3)
    for step in range(1, layer_count):
        target = (layer_index + step) % layer_count
        part = lax.dynamic_slice_in_dim(value, target * width, width, axis=3)
        own_part = own_part + from_behind(part, "lay", step)
    return own_part


def cross_of(ordered, partner):
    first = ordered.astype(jnp.float32)
    second = partner.astype(jnp.float32)
    cross_re = jnp.sum(
        first[0][:, None] * second[0][None] + first[1][:, None] * second[1][None], axis=2
    )
    cross_im = jnp.sum(
        first[1][:, None] * second[0][None] - first[0][:, None] * second[1][None], axis=2
    )
    return jnp.concatenate([cross_re.astype(jnp.bfloat16), cross_im.astype(jnp.bfloat16)], axis=2)


def terms_of(response, ordered, partner):
    freq_count = ordered.shape[3]
    first = ordered.astype(jnp.float32)
    second = partner.astype(jnp.float32)
    resp = response.astype(jnp.float32)
    resp_re = resp[:, :, None, :freq_count]
    resp_im = resp[:, :, None, freq_count:]
    own_re = jnp.sum(resp_re * second[0][None] - resp_im * second[1][None], axis=1)
    own_im = jnp.sum(resp_re * second[1][None] + resp_im * second[0][None], axis=1)
    part_re = jnp.sum(resp_re * first[0][:, None] + resp_im * first[1][:, None], axis=0)
    part_im = jnp.sum(resp_re * first[1][:, None] - resp_im * first[0][:, None], axis=0)
    return (jnp.stack([own_re, own_im]), jnp.stack([part_re, part_im]))


def local(spectra, model_corr, window_start, window_end, station_slot):
    station_count = spectra.shape[1]
    window_count = spectra.shape[2]
    freq_count = spectra.shape[3]
    offset_count = model_corr.shape[1]
    lag_count = model_corr.shape[4]
    layer_count = lax.axis_size("lay")
    block_count = lax.axis_size("blk")
    layer_index = lax.axis_index("lay")
    base_offset = layer_index * offset_count
    placing = (
        station_slot[0][:, None] == jnp.arange(station_count, dtype=jnp.int32)[None, :]
    ).astype(jnp.float32)
    ordered = jnp.sum(
        placing[None, :, :, None, None] * spectra.astype(jnp.float32)[:, None], axis=2
    ).astype(jnp.bfloat16)
    table = lag_table(freq_count, lag_count, window_count)
    bit_total = (layer_count - 1).bit_length()
    partner = ordered
    for bit_place in range(bit_total):
        shifted = from_behind(partner, "blk", -(offset_count << bit_place))
        partner = jnp.where((layer_index >> bit_place) % 2 == 1, shifted, partner)
    partners = []
    crosses = []
    for step_index in range(offset_count):
        partners.append(partner)
        crosses.append(cross_of(ordered, partner))
        if step_index + 1 < offset_count:
            partner = from_behind(partner, "blk", -1)
    pair_rows = station_count * station_count
    cross_all = jnp.stack(crosses).reshape(-1, 2 * freq_count)
    lagged = jnp.dot(cross_all, table, preferred_element_type=jnp.float32).reshape(
        offset_count, pair_rows, lag_count
    )
    lag_pos = jnp.arange(lag_count, dtype=jnp.int32)
    inside = (lag_pos[None, :] >= window_start[0][:, None]) & (
        lag_pos[None, :] < window_end[0][:, None]
    )
    station_pos = jnp.arange(station_count, dtype=jnp.int32)
    diagonal = (station_pos[:, None] == station_pos[None, :]).reshape(-1)
    offsets = base_offset + jnp.arange(offset_count, dtype=jnp.int32)
    paired = jnp.logical_not((offsets[:, None] == 0) & diagonal[None, :])
    keep = paired[:, :, None] & inside[:, None, :]
    model_rows = model_corr[0].reshape(offset_count, pair_rows, lag_count).astype(jnp.float32)
    misfit = jnp.where(keep, lagged - model_rows, 0.0).astype(jnp.bfloat16).reshape(-1, lag_count)
    response = lax.dot_general(
        misfit, table, (((1,), (1,)), ((), ())), preferred_element_type=jnp.float32
    )
    response = response.astype(jnp.bfloat16).reshape(
        offset_count, station_count, station_count, 2 * freq_count
    )
    own_sum = jnp.zeros((2, station_count, window_count, freq_count), jnp.float32)
    partner_list = []
    for step_index in range(offset_count):
        own_side, partner_side = terms_of(response[step_index], ordered, partners[step_index])
        own_sum = own_sum + own_side
        partner_list.append(partner_side)
    home_sum = partner_list[0]
    for step_index in range(1, offset_count):
        home_sum = home_sum + from_behind(
            partner_list[step_index].astype(jnp.bfloat16), "blk", step_index
        ).astype(jnp.float32)
    for bit_place in range(bit_total):
        shifted = from_behind(home_sum, "blk", offset_count << bit_place)
        home_sum = jnp.where((layer_index >> bit_place) % 2 == 1, shifted, home_sum)
    combined = own_sum + home_sum
    reduced = summed_over_layers(combined, layer_index, layer_count)
    scaled = reduced * (1.0 / math.sqrt(block_count * station_count))
    return jnp.sum(placing[None, :, :, None, None] * scaled[:, :, None], axis=1)


def solution(mesh):
    in_specs = (
        P(None, "blk", None, None),
        P("blk", "lay", None, None, None),
        P("blk", "lay"),
        P("blk", "lay"),
        P("blk", None),
    )
    out_specs = P(None, "blk", None, "lay")
    return jax.shard_map(local, mesh=mesh, in_specs=in_specs, out_specs=out_specs, check_vma=False)
```

```python
import functools
import math

import jax
import jax.numpy as jnp
import ml_dtypes
import numpy as np
from jax import lax
from jax.experimental import pallas as pl
from jax.experimental.pallas import tpu as pltpu
from jax.sharding import PartitionSpec as P


LANES = 128
AXES = ("blk", "lay")
OUTSIDE = 2.0**100


def lag_table(freq_count, lag_count, window_count):
    freq_index = np.arange(freq_count, dtype=np.int64)
    lag_index = np.arange(lag_count, dtype=np.int64) - lag_count // 2
    phase_index = freq_index[:, None] * lag_index[None, :] % (2 * freq_count)
    angle = phase_index.astype(np.float64) * (math.pi / freq_count)
    factor = 1.0 / math.sqrt(2.0 * freq_count * window_count)
    table = np.concatenate([np.cos(angle) * factor, -np.sin(angle) * factor], axis=0)
    return jnp.asarray(table.astype(ml_dtypes.bfloat16))


def order_kernel(slot_ref, spectra_ref, out_ref, spread):
    parts, stations, windows, freq = spectra_ref.shape
    chunks = freq // LANES
    for part in range(parts):
        for place in range(stations):
            rows = spectra_ref[part, slot_ref[0, place]].astype(jnp.float32)
            base = (part * stations + place) * windows * chunks
            for chunk in range(chunks):
                spread[pl.ds(base + chunk, windows, stride=chunks), :] = rows[
                    :, chunk * LANES : (chunk + 1) * LANES
                ]
    out_ref[...] = spread[...].astype(jnp.bfloat16)


def mask_kernel(start_ref, end_ref, model_ref, near_ref, last_ref, pass_ref, rows):
    core = lax.axis_index("blk") % 2
    layer = lax.axis_index("lay")
    stations, lags = model_ref.shape[3:]
    shape = (stations * stations, lags)
    lag = lax.broadcasted_iota(jnp.int32, shape, 1)
    row = lax.broadcasted_iota(jnp.int32, shape, 0)
    diagonal = row % (stations + 1) == 0

    def masked(offset):
        for first in range(stations):
            rows[first * stations : (first + 1) * stations, :] = model_ref[
                0, offset, first
            ].astype(jnp.float32)
        keep = (lag >= start_ref[0, offset]) & (lag < end_ref[0, offset])
        same = (layer == 0) & (offset == 0)
        keep = keep & jnp.logical_not(diagonal & same)
        return jnp.where(keep, rows[...], OUTSIDE).astype(jnp.bfloat16)

    near_ref[...] = masked(2 - 2 * core)
    last_ref[...] = masked(3)
    pass_ref[0] = masked(1)
    pass_ref[1] = masked(2 * core)


def pair_kernel(
    layers,
    stations,
    windows,
    mine_ref,
    other_ref,
    near_ref,
    cross_ref,
    model_near_ref,
    model_last_ref,
    model_moved_ref,
    model_pass_ref,
    table_ref,
    *rest,
):
    keep_ref = rest[0]
    own_refs = rest[1 : 1 + layers - 1]
    far_refs = rest[layers : 2 * layers]
    spec, cross_rows, resp_rows, sums = rest[2 * layers :]
    core = lax.axis_index("blk") % 2
    layer = lax.axis_index("lay")
    home = (layer == 0) & (core == 1)
    chunks = table_ref.shape[0] // 2 // LANES
    block_rows = 2 * stations * windows
    pair_rows = stations * stations
    total = 4 * pair_rows
    size = block_rows * chunks

    mine = mine_ref[...].astype(jnp.float32)
    other = other_ref[...].astype(jnp.float32)
    near = near_ref[...].astype(jnp.float32)
    cross = cross_ref[...].astype(jnp.float32)
    spec[0 * size : 1 * size, :] = mine
    spec[1 * size : 2 * size, :] = other
    spec[2 * size : 3 * size, :] = jnp.where(home, mine, near)
    spec[3 * size : 4 * size, :] = cross
    spec[4 * size : 5 * size, :] = jnp.where(home, other, cross)
    pairs = ((0, 2), (0, 3), (1, 2), (1, 4))

    def row_of(ref, index):
        return ref[index * chunks : (index + 1) * chunks, :]

    def spectrum(block, window):
        base = block * block_rows
        return [
            [row_of(spec, base + (part * stations + s) * windows + window) for s in range(stations)]
            for part in range(2)
        ]

    for pair, (first, second) in enumerate(pairs):
        real = [[None] * stations for _ in range(stations)]
        imag = [[None] * stations for _ in range(stations)]
        for window in range(windows):
            u = spectrum(first, window)
            v = spectrum(second, window)
            for i in range(stations):
                for j in range(stations):
                    re = u[0][i] * v[0][j] + u[1][i] * v[1][j]
                    im = u[1][i] * v[0][j] - u[0][i] * v[1][j]
                    real[i][j] = re if window == 0 else real[i][j] + re
                    imag[i][j] = im if window == 0 else imag[i][j] + im
        for i in range(stations):
            for j in range(stations):
                row = pair * pair_rows + i * stations + j
                cross_rows[row * chunks : (row + 1) * chunks, :] = real[i][j]
                row = row + total
                cross_rows[row * chunks : (row + 1) * chunks, :] = imag[i][j]

    left = jnp.concatenate(
        [
            cross_rows[pl.ds(part * total * chunks + chunk, total, stride=chunks), :].astype(
                jnp.bfloat16
            )
            for part in range(2)
            for chunk in range(chunks)
        ],
        axis=1,
    )
    lags = table_ref.shape[1]
    tile = 256
    misfit = []
    for place in range(lags // tile):
        span = slice(place * tile, (place + 1) * tile)
        lagged = jnp.dot(left, table_ref[:, span], preferred_element_type=jnp.float32)
        last = jnp.where(core == 0, model_last_ref[:, span].astype(jnp.float32), model_moved_ref[:, span].astype(jnp.float32))
        model = jnp.concatenate(
            [
                model_near_ref[:, span].astype(jnp.float32),
                last,
                model_pass_ref[0, :, span].astype(jnp.float32),
                model_pass_ref[1, :, span].astype(jnp.float32),
            ],
            axis=0,
        )
        misfit.append(jnp.where(model == OUTSIDE, 0.0, lagged - model).astype(jnp.bfloat16))
    misfit = jnp.concatenate(misfit, axis=1)
    per_tile = tile // LANES
    for place in range(2 * chunks // per_tile):
        response = lax.dot_general(
            misfit,
            table_ref[place * tile : (place + 1) * tile, :],
            (((1,), (1,)), ((), ())),
            preferred_element_type=jnp.float32,
        )
        response = response.astype(jnp.bfloat16).astype(jnp.float32)
        for inner in range(per_tile):
            part, chunk = divmod(place * per_tile + inner, chunks)
            resp_rows[pl.ds(part * total * chunks + chunk, total, stride=chunks), :] = response[
                :, inner * LANES : (inner + 1) * LANES
            ]

    written = set()

    def add(block, part, station, window, value):
        index = block * block_rows + (part * stations + station) * windows + window
        rows = slice(index * chunks, (index + 1) * chunks)
        if index in written:
            value = value + sums[rows, :]
        written.add(index)
        sums[rows, :] = value

    for pair, (first, second) in enumerate(pairs):
        base = pair * pair_rows
        r = [
            [row_of(resp_rows, part * total + base + n) for n in range(pair_rows)]
            for part in range(2)
        ]
        for window in range(windows):
            u = spectrum(first, window)
            v = spectrum(second, window)
            for i in range(stations):
                terms_re, terms_im = [], []
                for j in range(stations):
                    re, im = r[0][i * stations + j], r[1][i * stations + j]
                    terms_re.append(re * v[0][j] - im * v[1][j])
                    terms_im.append(re * v[1][j] + im * v[0][j])
                add(first, 0, i, window, sum(terms_re[1:], terms_re[0]))
                add(first, 1, i, window, sum(terms_im[1:], terms_im[0]))
            for j in range(stations):
                terms_re, terms_im = [], []
                for i in range(stations):
                    re, im = r[0][i * stations + j], r[1][i * stations + j]
                    terms_re.append(re * u[0][i] + im * u[1][i])
                    terms_im.append(re * u[1][i] - im * u[0][i])
                add(second, 0, j, window, sum(terms_re[1:], terms_re[0]))
                add(second, 1, j, window, sum(terms_im[1:], terms_im[0]))

    part_near = sums[2 * size : 3 * size, :]
    part_last = sums[4 * size : 5 * size, :]
    sums[0 * size : 1 * size, :] += jnp.where(home, part_near, 0.0)
    sums[1 * size : 2 * size, :] += jnp.where(home, part_last, 0.0)
    sums[2 * size : 3 * size, :] = jnp.where(home, 0.0, part_near)
    sums[3 * size : 4 * size, :] += jnp.where(home, 0.0, part_last)

    width = chunks // layers
    for step in range(layers):
        start = lax.rem(layer + step, layers) * width
        for inner in range(width):
            span = slice(inner * LANES, (inner + 1) * LANES)
            own = sums[pl.ds(start + inner, 2 * block_rows, stride=chunks), :]
            if step == 0:
                keep_ref[:, span] = own
            else:
                own_refs[step - 1][:, span] = own.astype(jnp.bfloat16)
            far = sums[pl.ds(2 * size + start + inner, 2 * block_rows, stride=chunks), :]
            far_refs[step][:, span] = far.astype(jnp.bfloat16)


def gather_kernel(count, *refs):
    keep_ref, send_ref = refs[count:]
    half = keep_ref.shape[0]
    total = refs[0][...]
    for ref in refs[1:count]:
        total = total + ref[...].astype(jnp.float32)
    keep_ref[...] = total[:half]
    send_ref[...] = total[half:]


def place_kernel(scale, slot_ref, keep_ref, moved_ref, out_ref):
    parts, stations, windows, _ = out_ref.shape
    total = (keep_ref[...] + moved_ref[...]) * scale
    for part in range(parts):
        for place in range(stations):
            base = (part * stations + place) * windows
            out_ref[part, slot_ref[0, place]] = total[base : base + windows, :]


VMEM = pl.BlockSpec(memory_space=pltpu.VMEM)
SMEM = pl.BlockSpec(memory_space=pltpu.SMEM)
LIMIT = pltpu.CompilerParams(vmem_limit_bytes=24 * 1024 * 1024)


def local(spectra, model_corr, window_start, window_end, station_slot):
    _, stations, windows, freq = spectra.shape
    lags = model_corr.shape[4]
    layers = lax.axis_size("lay")
    blocks = lax.axis_size("blk")
    chips = blocks // 2
    chunks = freq // LANES
    pair_rows = stations * stations
    block_rows = 2 * stations * windows
    f32, bf16 = jnp.float32, jnp.bfloat16

    def distance(layer, core):
        if core == 0:
            return 2 * layer + 1
        return 2 * layer if layer > 0 else 2 * layers

    def move(value, target):
        pairs = []
        for block in range(blocks):
            for layer in range(layers):
                chip, core, to_layer = target(block // 2, block % 2, layer)
                pairs.append(
                    (block * layers + layer, (chip % chips * 2 + core) * layers + to_layer % layers)
                )
        return lax.ppermute(value, AXES, pairs)

    def swap_cores(value):
        return move(value, lambda chip, core, layer: (chip, 1 - core, layer))

    table = lag_table(freq, lags, windows)
    mine = pl.pallas_call(
        order_kernel,
        out_shape=jax.ShapeDtypeStruct((block_rows * chunks, LANES), bf16),
        in_specs=[SMEM, VMEM],
        out_specs=VMEM,
        scratch_shapes=[pltpu.VMEM((block_rows * chunks, LANES), f32)],
        name="order",
    )(station_slot, spectra)
    near = move(mine, lambda chip, core, layer: (chip - distance(layer, core), core, layer))
    cross = move(mine, lambda chip, core, layer: (chip - distance(layer, 1 - core), 1 - core, layer))
    other = swap_cores(mine)
    model_near, model_last, model_pass = pl.pallas_call(
        mask_kernel,
        out_shape=[
            jax.ShapeDtypeStruct((pair_rows, lags), bf16),
            jax.ShapeDtypeStruct((pair_rows, lags), bf16),
            jax.ShapeDtypeStruct((2, pair_rows, lags), bf16),
        ],
        in_specs=[SMEM, SMEM, VMEM],
        out_specs=[VMEM, VMEM, VMEM],
        scratch_shapes=[pltpu.VMEM((pair_rows, lags), f32)],
        name="mask",
    )(window_start, window_end, model_corr)
    model_moved = move(model_last, lambda chip, core, layer: (chip, core, layer + 1))
    model_pass = swap_cores(model_pass)

    part = (2 * block_rows, freq // layers)
    outs = pl.pallas_call(
        functools.partial(pair_kernel, layers, stations, windows),
        out_shape=[jax.ShapeDtypeStruct(part, f32)]
        + [jax.ShapeDtypeStruct(part, bf16)] * (2 * layers - 1),
        in_specs=[VMEM] * 9,
        out_specs=[VMEM] * (2 * layers),
        scratch_shapes=[
            pltpu.VMEM((5 * block_rows * chunks, LANES), f32),
            pltpu.VMEM((8 * pair_rows * chunks, LANES), f32),
            pltpu.VMEM((8 * pair_rows * chunks, LANES), f32),
            pltpu.VMEM((5 * block_rows * chunks, LANES), f32),
        ],
        compiler_params=LIMIT,
        name="pair",
    )(mine, other, near, cross, model_near, model_last, model_moved, model_pass, table)
    parts = [outs[0]]
    for step in range(layers):
        parts.append(
            move(
                outs[layers + step],
                lambda chip, core, layer: (chip + distance(layer, core), core, layer + step),
            )
        )
    for step in range(1, layers):
        parts.append(
            move(outs[step], lambda chip, core, layer: (chip, core, layer + step))
        )
    half = jax.ShapeDtypeStruct((block_rows, freq // layers), f32)
    keep, send = pl.pallas_call(
        functools.partial(gather_kernel, len(parts)),
        out_shape=[half, half],
        in_specs=[VMEM] * len(parts),
        out_specs=[VMEM, VMEM],
        name="gather",
    )(*parts)
    moved = swap_cores(send)
    return pl.pallas_call(
        functools.partial(place_kernel, 1.0 / math.sqrt(blocks * stations)),
        out_shape=jax.ShapeDtypeStruct((2, stations, windows, freq // layers), f32),
        in_specs=[SMEM, VMEM, VMEM],
        out_specs=VMEM,
        name="place",
    )(station_slot, keep, moved)


def solution(mesh):
    in_specs = (
        P(None, "blk", None, None),
        P("blk", "lay", None, None, None),
        P("blk", "lay"),
        P("blk", "lay"),
        P("blk", None),
    )
    out_specs = P(None, "blk", None, "lay")
    return jax.shard_map(local, mesh=mesh, in_specs=in_specs, out_specs=out_specs, check_vma=False)
```

```python
import functools
import math

import jax
import jax.numpy as jnp
import ml_dtypes
import numpy as np
from jax import lax
from jax.experimental import pallas as pl
from jax.experimental.pallas import tpu as pltpu
from jax.sharding import PartitionSpec as P


LANES = 128
AXES = ("blk", "lay")
OUTSIDE = 2.0**100


def lag_table(freq_count, lag_count, window_count):
    freq_index = np.arange(freq_count, dtype=np.int64)
    lag_index = np.arange(lag_count, dtype=np.int64) - lag_count // 2
    phase_index = freq_index[:, None] * lag_index[None, :] % (2 * freq_count)
    angle = phase_index.astype(np.float64) * (math.pi / freq_count)
    factor = 1.0 / math.sqrt(2.0 * freq_count * window_count)
    table = np.concatenate([np.cos(angle) * factor, -np.sin(angle) * factor], axis=0)
    return jnp.asarray(table.astype(ml_dtypes.bfloat16))


def order_kernel(slot_ref, spectra_ref, out_ref, spread):
    parts, stations, windows, freq = spectra_ref.shape
    chunks = freq // LANES
    for part in range(parts):
        for place in range(stations):
            rows = spectra_ref[part, slot_ref[0, place]].astype(jnp.float32)
            base = (part * stations + place) * windows * chunks
            for chunk in range(chunks):
                spread[pl.ds(base + chunk, windows, stride=chunks), :] = rows[
                    :, chunk * LANES : (chunk + 1) * LANES
                ]
    out_ref[...] = spread[...].astype(jnp.bfloat16)


def mask_kernel(start_ref, end_ref, model_ref, near_ref, last_ref, pass_ref, rows):
    core = lax.axis_index("blk") % 2
    layer = lax.axis_index("lay")
    stations, lags = model_ref.shape[3:]
    shape = (stations * stations, lags)
    lag = lax.broadcasted_iota(jnp.int32, shape, 1)
    row = lax.broadcasted_iota(jnp.int32, shape, 0)
    diagonal = row % (stations + 1) == 0

    def masked(offset):
        for first in range(stations):
            rows[first * stations : (first + 1) * stations, :] = model_ref[
                0, offset, first
            ].astype(jnp.float32)
        keep = (lag >= start_ref[0, offset]) & (lag < end_ref[0, offset])
        same = (layer == 0) & (offset == 0)
        keep = keep & jnp.logical_not(diagonal & same)
        return jnp.where(keep, rows[...], OUTSIDE).astype(jnp.bfloat16)

    near_ref[...] = masked(2 - 2 * core)
    last_ref[...] = masked(3)
    pass_ref[0] = masked(1)
    pass_ref[1] = masked(2 * core)


def pair_kernel(
    layers,
    stations,
    windows,
    mine_ref,
    other_ref,
    near_ref,
    cross_ref,
    model_near_ref,
    model_last_ref,
    model_moved_ref,
    model_pass_ref,
    table_ref,
    *rest,
):
    keep_ref = rest[0]
    own_refs = rest[1 : 1 + layers - 1]
    far_refs = rest[layers : 2 * layers]
    spec, cross_rows, resp_rows, sums = rest[2 * layers :]
    core = lax.axis_index("blk") % 2
    layer = lax.axis_index("lay")
    home = (layer == 0) & (core == 1)
    chunks = table_ref.shape[0] // 2 // LANES
    block_rows = 2 * stations * windows
    pair_rows = stations * stations
    total = 4 * pair_rows
    size = block_rows * chunks

    mine = mine_ref[...].astype(jnp.float32)
    other = other_ref[...].astype(jnp.float32)
    near = near_ref[...].astype(jnp.float32)
    cross = cross_ref[...].astype(jnp.float32)
    spec[0 * size : 1 * size, :] = mine
    spec[1 * size : 2 * size, :] = other
    spec[2 * size : 3 * size, :] = jnp.where(home, mine, near)
    spec[3 * size : 4 * size, :] = cross
    spec[4 * size : 5 * size, :] = jnp.where(home, other, cross)
    pairs = ((0, 2), (0, 3), (1, 2), (1, 4))

    def row_of(ref, index):
        return ref[index * chunks : (index + 1) * chunks, :]

    def spectrum(block, window):
        base = block * block_rows
        return [
            [row_of(spec, base + (part * stations + s) * windows + window) for s in range(stations)]
            for part in range(2)
        ]

    for pair, (first, second) in enumerate(pairs):
        real = [[None] * stations for _ in range(stations)]
        imag = [[None] * stations for _ in range(stations)]
        for window in range(windows):
            u = spectrum(first, window)
            v = spectrum(second, window)
            for i in range(stations):
                for j in range(stations):
                    re = u[0][i] * v[0][j] + u[1][i] * v[1][j]
                    im = u[1][i] * v[0][j] - u[0][i] * v[1][j]
                    real[i][j] = re if window == 0 else real[i][j] + re
                    imag[i][j] = im if window == 0 else imag[i][j] + im
        for i in range(stations):
            for j in range(stations):
                row = pair * pair_rows + i * stations + j
                cross_rows[row * chunks : (row + 1) * chunks, :] = real[i][j]
                row = row + total
                cross_rows[row * chunks : (row + 1) * chunks, :] = imag[i][j]

    left = jnp.concatenate(
        [
            cross_rows[pl.ds(part * total * chunks + chunk, total, stride=chunks), :].astype(
                jnp.bfloat16
            )
            for part in range(2)
            for chunk in range(chunks)
        ],
        axis=1,
    )
    lags = table_ref.shape[1]
    tile = 256
    misfit = []
    for place in range(lags // tile):
        span = slice(place * tile, (place + 1) * tile)
        lagged = jnp.dot(left, table_ref[:, span], preferred_element_type=jnp.float32)
        last = jnp.where(core == 0, model_last_ref[:, span].astype(jnp.float32), model_moved_ref[:, span].astype(jnp.float32))
        model = jnp.concatenate(
            [
                model_near_ref[:, span].astype(jnp.float32),
                last,
                model_pass_ref[0, :, span].astype(jnp.float32),
                model_pass_ref[1, :, span].astype(jnp.float32),
            ],
            axis=0,
        )
        misfit.append(jnp.where(model == OUTSIDE, 0.0, lagged - model).astype(jnp.bfloat16))
    misfit = jnp.concatenate(misfit, axis=1)
    per_tile = tile // LANES
    for place in range(2 * chunks // per_tile):
        response = lax.dot_general(
            misfit,
            table_ref[place * tile : (place + 1) * tile, :],
            (((1,), (1,)), ((), ())),
            preferred_element_type=jnp.float32,
        )
        response = response.astype(jnp.bfloat16).astype(jnp.float32)
        for inner in range(per_tile):
            part, chunk = divmod(place * per_tile + inner, chunks)
            resp_rows[pl.ds(part * total * chunks + chunk, total, stride=chunks), :] = response[
                :, inner * LANES : (inner + 1) * LANES
            ]

    written = set()

    def add(block, part, station, window, value):
        index = block * block_rows + (part * stations + station) * windows + window
        rows = slice(index * chunks, (index + 1) * chunks)
        if index in written:
            value = value + sums[rows, :]
        written.add(index)
        sums[rows, :] = value

    for pair, (first, second) in enumerate(pairs):
        base = pair * pair_rows
        r = [
            [row_of(resp_rows, part * total + base + n) for n in range(pair_rows)]
            for part in range(2)
        ]
        for window in range(windows):
            u = spectrum(first, window)
            v = spectrum(second, window)
            for i in range(stations):
                terms_re, terms_im = [], []
                for j in range(stations):
                    re, im = r[0][i * stations + j], r[1][i * stations + j]
                    terms_re.append(re * v[0][j] - im * v[1][j])
                    terms_im.append(re * v[1][j] + im * v[0][j])
                add(first, 0, i, window, sum(terms_re[1:], terms_re[0]))
                add(first, 1, i, window, sum(terms_im[1:], terms_im[0]))
            for j in range(stations):
                terms_re, terms_im = [], []
                for i in range(stations):
                    re, im = r[0][i * stations + j], r[1][i * stations + j]
                    terms_re.append(re * u[0][i] + im * u[1][i])
                    terms_im.append(re * u[1][i] - im * u[0][i])
                add(second, 0, j, window, sum(terms_re[1:], terms_re[0]))
                add(second, 1, j, window, sum(terms_im[1:], terms_im[0]))

    part_near = sums[2 * size : 3 * size, :]
    part_last = sums[4 * size : 5 * size, :]
    sums[0 * size : 1 * size, :] += jnp.where(home, part_near, 0.0)
    sums[1 * size : 2 * size, :] += jnp.where(home, part_last, 0.0)
    sums[2 * size : 3 * size, :] = jnp.where(home, 0.0, part_near)
    sums[3 * size : 4 * size, :] += jnp.where(home, 0.0, part_last)

    width = chunks // layers
    for step in range(layers):
        start = lax.rem(layer + step, layers) * width
        for inner in range(width):
            span = slice(inner * LANES, (inner + 1) * LANES)
            own = sums[pl.ds(start + inner, 2 * block_rows, stride=chunks), :]
            if step == 0:
                keep_ref[:, span] = own
            else:
                own_refs[step - 1][:, span] = own.astype(jnp.bfloat16)
            far = sums[pl.ds(2 * size + start + inner, 2 * block_rows, stride=chunks), :]
            far_refs[step][:, span] = far.astype(jnp.bfloat16)


def gather_kernel(count, *refs):
    keep_ref, send_ref = refs[count:]
    half = keep_ref.shape[0]
    total = refs[0][...]
    for ref in refs[1:count]:
        total = total + ref[...].astype(jnp.float32)
    keep_ref[...] = total[:half]
    send_ref[...] = total[half:]


def place_kernel(scale, slot_ref, keep_ref, moved_ref, out_ref):
    parts, stations, windows, _ = out_ref.shape
    total = (keep_ref[...] + moved_ref[...]) * scale
    for part in range(parts):
        for place in range(stations):
            base = (part * stations + place) * windows
            out_ref[part, slot_ref[0, place]] = total[base : base + windows, :]


VMEM = pl.BlockSpec(memory_space=pltpu.VMEM)
SMEM = pl.BlockSpec(memory_space=pltpu.SMEM)


def grant(mebibytes):
    return pltpu.CompilerParams(vmem_limit_bytes=mebibytes * 1024 * 1024)


def local(spectra, model_corr, window_start, window_end, station_slot):
    _, stations, windows, freq = spectra.shape
    lags = model_corr.shape[4]
    layers = lax.axis_size("lay")
    blocks = lax.axis_size("blk")
    chips = blocks // 2
    chunks = freq // LANES
    pair_rows = stations * stations
    block_rows = 2 * stations * windows
    f32, bf16 = jnp.float32, jnp.bfloat16

    def distance(layer, core):
        if core == 0:
            return 2 * layer + 1
        return 2 * layer if layer > 0 else 2 * layers

    def move(value, target):
        pairs = []
        for block in range(blocks):
            for layer in range(layers):
                chip, core, to_layer = target(block // 2, block % 2, layer)
                pairs.append(
                    (block * layers + layer, (chip % chips * 2 + core) * layers + to_layer % layers)
                )
        return lax.ppermute(value, AXES, pairs)

    def swap_cores(value):
        return move(value, lambda chip, core, layer: (chip, 1 - core, layer))

    table = lag_table(freq, lags, windows)
    mine = pl.pallas_call(
        order_kernel,
        out_shape=jax.ShapeDtypeStruct((block_rows * chunks, LANES), bf16),
        in_specs=[SMEM, VMEM],
        out_specs=VMEM,
        scratch_shapes=[pltpu.VMEM((block_rows * chunks, LANES), f32)],
        compiler_params=grant(2),
        name="order",
    )(station_slot, spectra)
    near = move(mine, lambda chip, core, layer: (chip - distance(layer, core), core, layer))
    cross = move(mine, lambda chip, core, layer: (chip - distance(layer, 1 - core), 1 - core, layer))
    other = swap_cores(mine)
    model_near, model_last, model_pass = pl.pallas_call(
        mask_kernel,
        out_shape=[
            jax.ShapeDtypeStruct((pair_rows, lags), bf16),
            jax.ShapeDtypeStruct((pair_rows, lags), bf16),
            jax.ShapeDtypeStruct((2, pair_rows, lags), bf16),
        ],
        in_specs=[SMEM, SMEM, VMEM],
        out_specs=[VMEM, VMEM, VMEM],
        scratch_shapes=[pltpu.VMEM((pair_rows, lags), f32)],
        compiler_params=grant(2),
        name="mask",
    )(window_start, window_end, model_corr)
    model_moved = move(model_last, lambda chip, core, layer: (chip, core, layer + 1))
    model_pass = swap_cores(model_pass)

    part = (2 * block_rows, freq // layers)
    outs = pl.pallas_call(
        functools.partial(pair_kernel, layers, stations, windows),
        out_shape=[jax.ShapeDtypeStruct(part, f32)]
        + [jax.ShapeDtypeStruct(part, bf16)] * (2 * layers - 1),
        in_specs=[VMEM] * 9,
        out_specs=[VMEM] * (2 * layers),
        scratch_shapes=[
            pltpu.VMEM((5 * block_rows * chunks, LANES), f32),
            pltpu.VMEM((8 * pair_rows * chunks, LANES), f32),
            pltpu.VMEM((8 * pair_rows * chunks, LANES), f32),
            pltpu.VMEM((5 * block_rows * chunks, LANES), f32),
        ],
        compiler_params=grant(12),
        name="pair",
    )(mine, other, near, cross, model_near, model_last, model_moved, model_pass, table)
    parts = [outs[0]]
    for step in range(layers):
        parts.append(
            move(
                outs[layers + step],
                lambda chip, core, layer: (chip + distance(layer, core), core, layer + step),
            )
        )
    for step in range(1, layers):
        parts.append(
            move(outs[step], lambda chip, core, layer: (chip, core, layer + step))
        )
    half = jax.ShapeDtypeStruct((block_rows, freq // layers), f32)
    keep, send = pl.pallas_call(
        functools.partial(gather_kernel, len(parts)),
        out_shape=[half, half],
        in_specs=[VMEM] * len(parts),
        out_specs=[VMEM, VMEM],
        compiler_params=grant(2),
        name="gather",
    )(*parts)
    moved = swap_cores(send)
    return pl.pallas_call(
        functools.partial(place_kernel, 1.0 / math.sqrt(blocks * stations)),
        out_shape=jax.ShapeDtypeStruct((2, stations, windows, freq // layers), f32),
        in_specs=[SMEM, VMEM, VMEM],
        out_specs=VMEM,
        compiler_params=grant(2),
        name="place",
    )(station_slot, keep, moved)


def solution(mesh):
    in_specs = (
        P(None, "blk", None, None),
        P("blk", "lay", None, None, None),
        P("blk", "lay"),
        P("blk", "lay"),
        P("blk", None),
    )
    out_specs = P(None, "blk", None, "lay")
    return jax.shard_map(local, mesh=mesh, in_specs=in_specs, out_specs=out_specs, check_vma=False)
```

```python
import functools
import math

import jax
import jax.numpy as jnp
import ml_dtypes
import numpy as np
from jax import lax
from jax.experimental import pallas as pl
from jax.experimental.pallas import tpu as pltpu
from jax.sharding import PartitionSpec as P


LANES = 128
AXES = ("blk", "lay")
OUTSIDE = 2.0**100


def lag_table(freq_count, lag_count, window_count):
    freq_index = np.arange(freq_count, dtype=np.int64)
    lag_index = np.arange(lag_count, dtype=np.int64) - lag_count // 2
    phase_index = freq_index[:, None] * lag_index[None, :] % (2 * freq_count)
    angle = phase_index.astype(np.float64) * (math.pi / freq_count)
    factor = 1.0 / math.sqrt(2.0 * freq_count * window_count)
    table = np.concatenate([np.cos(angle) * factor, -np.sin(angle) * factor], axis=0)
    return jnp.asarray(table.astype(ml_dtypes.bfloat16))


def prepare_kernel(
    slot_ref,
    spectra_ref,
    start_ref,
    end_ref,
    model_ref,
    mine_ref,
    placing_ref,
    model_near_ref,
    model_last_ref,
    model_pass_ref,
    slot,
    start,
    end,
    spectra,
    model,
    spread,
    rows,
    arrived,
):
    moves = [
        pltpu.make_async_copy(source, target, arrived.at[place])
        for place, (source, target) in enumerate(
            (
                (slot_ref, slot),
                (spectra_ref, spectra),
                (start_ref, start),
                (end_ref, end),
                (model_ref, model),
            )
        )
    ]
    for copy in moves:
        copy.start()
    parts, stations, windows, freq = spectra.shape
    chunks = freq // LANES
    core = lax.axis_index("blk") % 2
    layer = lax.axis_index("lay")
    moves[0].wait()
    for place in range(stations):
        for station in range(stations):
            row = place * stations + station
            here = (slot[0, place] == station).astype(jnp.float32)
            placing_ref[row : row + 1, :] = jnp.full((1, placing_ref.shape[1]), here, jnp.float32)
    moves[1].wait()
    for part in range(parts):
        for place in range(stations):
            values = spectra[part, slot[0, place]].astype(jnp.float32)
            base = (part * stations + place) * windows * chunks
            for chunk in range(chunks):
                spread[pl.ds(base + chunk, windows, stride=chunks), :] = values[
                    :, chunk * LANES : (chunk + 1) * LANES
                ]
    mine_ref[...] = spread[...].astype(jnp.bfloat16)

    lags = model.shape[4]
    shape = (stations * stations, lags)
    lag = lax.broadcasted_iota(jnp.int32, shape, 1)
    row = lax.broadcasted_iota(jnp.int32, shape, 0)
    diagonal = row % (stations + 1) == 0
    for copy in moves[2:]:
        copy.wait()

    def masked(offset):
        for first in range(stations):
            rows[first * stations : (first + 1) * stations, :] = model[0, offset, first].astype(
                jnp.float32
            )
        keep = (lag >= start[0, offset]) & (lag < end[0, offset])
        same = (layer == 0) & (offset == 0)
        keep = keep & jnp.logical_not(diagonal & same)
        return jnp.where(keep, rows[...], OUTSIDE).astype(jnp.bfloat16)

    model_near_ref[...] = masked(2 - 2 * core)
    model_last_ref[...] = masked(3)
    model_pass_ref[0] = masked(1)
    model_pass_ref[1] = masked(2 * core)


def fetch_kernel(after_ref, table_ref, out_ref, arrived):
    del after_ref
    count = arrived.shape[0]
    size = table_ref.shape[0] // count
    moves = [
        pltpu.make_async_copy(
            table_ref.at[pl.ds(place * size, size)],
            out_ref.at[pl.ds(place * size, size)],
            arrived.at[place],
        )
        for place in range(count)
    ]
    for copy in moves:
        copy.start()
    for copy in moves:
        copy.wait()


def pair_kernel(
    layers,
    stations,
    windows,
    mine_ref,
    other_ref,
    near_ref,
    cross_ref,
    model_near_ref,
    model_last_ref,
    model_moved_ref,
    model_pass_ref,
    table_ref,
    *rest,
):
    keep_ref = rest[0]
    own_refs = rest[1 : 1 + layers - 1]
    far_refs = rest[layers : 2 * layers]
    spec, cross_rows, resp_rows, sums = rest[2 * layers :]
    core = lax.axis_index("blk") % 2
    layer = lax.axis_index("lay")
    home = (layer == 0) & (core == 1)
    chunks = table_ref.shape[0] // 2 // LANES
    block_rows = 2 * stations * windows
    pair_rows = stations * stations
    total = 4 * pair_rows
    size = block_rows * chunks

    mine = mine_ref[...].astype(jnp.float32)
    other = other_ref[...].astype(jnp.float32)
    near = near_ref[...].astype(jnp.float32)
    cross = cross_ref[...].astype(jnp.float32)
    spec[0 * size : 1 * size, :] = mine
    spec[1 * size : 2 * size, :] = other
    spec[2 * size : 3 * size, :] = jnp.where(home, mine, near)
    spec[3 * size : 4 * size, :] = cross
    spec[4 * size : 5 * size, :] = jnp.where(home, other, cross)
    pairs = ((0, 2), (0, 3), (1, 2), (1, 4))

    def row_of(ref, index):
        return ref[index * chunks : (index + 1) * chunks, :]

    def spectrum(block, window):
        base = block * block_rows
        return [
            [row_of(spec, base + (part * stations + s) * windows + window) for s in range(stations)]
            for part in range(2)
        ]

    for pair, (first, second) in enumerate(pairs):
        real = [[None] * stations for _ in range(stations)]
        imag = [[None] * stations for _ in range(stations)]
        for window in range(windows):
            u = spectrum(first, window)
            v = spectrum(second, window)
            for i in range(stations):
                for j in range(stations):
                    re = u[0][i] * v[0][j] + u[1][i] * v[1][j]
                    im = u[1][i] * v[0][j] - u[0][i] * v[1][j]
                    real[i][j] = re if window == 0 else real[i][j] + re
                    imag[i][j] = im if window == 0 else imag[i][j] + im
        for i in range(stations):
            for j in range(stations):
                row = pair * pair_rows + i * stations + j
                cross_rows[row * chunks : (row + 1) * chunks, :] = real[i][j]
                row = row + total
                cross_rows[row * chunks : (row + 1) * chunks, :] = imag[i][j]

    left = jnp.concatenate(
        [
            cross_rows[pl.ds(part * total * chunks + chunk, total, stride=chunks), :].astype(
                jnp.bfloat16
            )
            for part in range(2)
            for chunk in range(chunks)
        ],
        axis=1,
    )
    lags = table_ref.shape[1]
    tile = 256
    misfit = []
    for place in range(lags // tile):
        span = slice(place * tile, (place + 1) * tile)
        lagged = jnp.dot(left, table_ref[:, span], preferred_element_type=jnp.float32)
        last = jnp.where(core == 0, model_last_ref[:, span].astype(jnp.float32), model_moved_ref[:, span].astype(jnp.float32))
        model = jnp.concatenate(
            [
                model_near_ref[:, span].astype(jnp.float32),
                last,
                model_pass_ref[0, :, span].astype(jnp.float32),
                model_pass_ref[1, :, span].astype(jnp.float32),
            ],
            axis=0,
        )
        misfit.append(jnp.where(model == OUTSIDE, 0.0, lagged - model).astype(jnp.bfloat16))
    misfit = jnp.concatenate(misfit, axis=1)
    per_tile = tile // LANES
    for place in range(2 * chunks // per_tile):
        response = lax.dot_general(
            misfit,
            table_ref[place * tile : (place + 1) * tile, :],
            (((1,), (1,)), ((), ())),
            preferred_element_type=jnp.float32,
        )
        response = response.astype(jnp.bfloat16).astype(jnp.float32)
        for inner in range(per_tile):
            part, chunk = divmod(place * per_tile + inner, chunks)
            resp_rows[pl.ds(part * total * chunks + chunk, total, stride=chunks), :] = response[
                :, inner * LANES : (inner + 1) * LANES
            ]

    written = set()

    def add(block, part, station, window, value):
        index = block * block_rows + (part * stations + station) * windows + window
        rows = slice(index * chunks, (index + 1) * chunks)
        if index in written:
            value = value + sums[rows, :]
        written.add(index)
        sums[rows, :] = value

    for pair, (first, second) in enumerate(pairs):
        base = pair * pair_rows
        r = [
            [row_of(resp_rows, part * total + base + n) for n in range(pair_rows)]
            for part in range(2)
        ]
        for window in range(windows):
            u = spectrum(first, window)
            v = spectrum(second, window)
            for i in range(stations):
                terms_re, terms_im = [], []
                for j in range(stations):
                    re, im = r[0][i * stations + j], r[1][i * stations + j]
                    terms_re.append(re * v[0][j] - im * v[1][j])
                    terms_im.append(re * v[1][j] + im * v[0][j])
                add(first, 0, i, window, sum(terms_re[1:], terms_re[0]))
                add(first, 1, i, window, sum(terms_im[1:], terms_im[0]))
            for j in range(stations):
                terms_re, terms_im = [], []
                for i in range(stations):
                    re, im = r[0][i * stations + j], r[1][i * stations + j]
                    terms_re.append(re * u[0][i] + im * u[1][i])
                    terms_im.append(re * u[1][i] - im * u[0][i])
                add(second, 0, j, window, sum(terms_re[1:], terms_re[0]))
                add(second, 1, j, window, sum(terms_im[1:], terms_im[0]))

    part_near = sums[2 * size : 3 * size, :]
    part_last = sums[4 * size : 5 * size, :]
    sums[0 * size : 1 * size, :] += jnp.where(home, part_near, 0.0)
    sums[1 * size : 2 * size, :] += jnp.where(home, part_last, 0.0)
    sums[2 * size : 3 * size, :] = jnp.where(home, 0.0, part_near)
    sums[3 * size : 4 * size, :] += jnp.where(home, 0.0, part_last)

    width = chunks // layers
    for step in range(layers):
        start = lax.rem(layer + step, layers) * width
        for inner in range(width):
            span = slice(inner * LANES, (inner + 1) * LANES)
            own = sums[pl.ds(start + inner, 2 * block_rows, stride=chunks), :]
            if step == 0:
                keep_ref[:, span] = own
            else:
                own_refs[step - 1][:, span] = own.astype(jnp.bfloat16)
            far = sums[pl.ds(2 * size + start + inner, 2 * block_rows, stride=chunks), :]
            far_refs[step][:, span] = far.astype(jnp.bfloat16)


def gather_kernel(count, *refs):
    keep_ref, send_ref = refs[count:]
    half = keep_ref.shape[0]
    total = refs[0][...]
    for ref in refs[1:count]:
        total = total + ref[...].astype(jnp.float32)
    keep_ref[...] = total[:half]
    send_ref[...] = total[half:]


def place_kernel(scale, placing_ref, keep_ref, moved_ref, out_ref):
    parts, stations, windows, _ = out_ref.shape
    total = (keep_ref[...] + moved_ref[...]) * scale
    for station in range(stations):
        here = [
            placing_ref[row : row + 1, :]
            for row in range(station, stations * stations, stations)
        ]
        for part in range(parts):
            value = None
            for place in range(stations):
                base = (part * stations + place) * windows
                term = here[place] * total[base : base + windows, :]
                value = term if value is None else value + term
            out_ref[part, station] = value


VMEM = pl.BlockSpec(memory_space=pltpu.VMEM)
HBM = pl.BlockSpec(memory_space=pltpu.HBM)


def grant(mebibytes):
    return pltpu.CompilerParams(vmem_limit_bytes=mebibytes * 1024 * 1024)


def local(spectra, model_corr, window_start, window_end, station_slot):
    _, stations, windows, freq = spectra.shape
    lags = model_corr.shape[4]
    layers = lax.axis_size("lay")
    blocks = lax.axis_size("blk")
    chips = blocks // 2
    chunks = freq // LANES
    pair_rows = stations * stations
    block_rows = 2 * stations * windows
    f32, bf16 = jnp.float32, jnp.bfloat16

    def distance(layer, core):
        if core == 0:
            return 2 * layer + 1
        return 2 * layer if layer > 0 else 2 * layers

    def move(value, target):
        pairs = []
        for block in range(blocks):
            for layer in range(layers):
                chip, core, to_layer = target(block // 2, block % 2, layer)
                pairs.append(
                    (block * layers + layer, (chip % chips * 2 + core) * layers + to_layer % layers)
                )
        return lax.ppermute(value, AXES, pairs)

    def swap_cores(value):
        return move(value, lambda chip, core, layer: (chip, 1 - core, layer))

    station_slot, spectra, window_start, window_end, model_corr = (
        pltpu.with_memory_space_constraint(value, pltpu.HBM)
        for value in (station_slot, spectra, window_start, window_end, model_corr)
    )
    mine, placing, model_near, model_last, model_pass = pl.pallas_call(
        prepare_kernel,
        out_shape=[
            jax.ShapeDtypeStruct((block_rows * chunks, LANES), bf16),
            jax.ShapeDtypeStruct((stations * stations, freq // layers), f32),
            jax.ShapeDtypeStruct((pair_rows, lags), bf16),
            jax.ShapeDtypeStruct((pair_rows, lags), bf16),
            jax.ShapeDtypeStruct((2, pair_rows, lags), bf16),
        ],
        in_specs=[HBM] * 5,
        out_specs=[VMEM] * 5,
        scratch_shapes=[
            pltpu.SMEM(station_slot.shape, jnp.int32),
            pltpu.SMEM(window_start.shape, jnp.int32),
            pltpu.SMEM(window_end.shape, jnp.int32),
            pltpu.VMEM(spectra.shape, bf16),
            pltpu.VMEM(model_corr.shape, bf16),
            pltpu.VMEM((block_rows * chunks, LANES), f32),
            pltpu.VMEM((pair_rows, lags), f32),
            pltpu.SemaphoreType.DMA((5,)),
        ],
        compiler_params=grant(2),
        name="prepare",
    )(station_slot, spectra, window_start, window_end, model_corr)
    near = move(mine, lambda chip, core, layer: (chip - distance(layer, core), core, layer))
    cross = move(mine, lambda chip, core, layer: (chip - distance(layer, 1 - core), 1 - core, layer))
    model_moved = move(model_last, lambda chip, core, layer: (chip, core, layer + 1))
    other = swap_cores(mine)
    model_pass = swap_cores(model_pass)
    table = pltpu.with_memory_space_constraint(lag_table(freq, lags, windows), pltpu.HBM)
    table = pl.pallas_call(
        fetch_kernel,
        out_shape=jax.ShapeDtypeStruct(table.shape, bf16),
        in_specs=[VMEM, HBM],
        out_specs=VMEM,
        scratch_shapes=[pltpu.SemaphoreType.DMA((8,))],
        compiler_params=grant(6),
        cost_estimate=pl.CostEstimate(flops=0, bytes_accessed=4 * freq * lags, transcendentals=0),
        name="fetch",
    )(placing, table)

    part = (2 * block_rows, freq // layers)
    outs = pl.pallas_call(
        functools.partial(pair_kernel, layers, stations, windows),
        out_shape=[jax.ShapeDtypeStruct(part, f32)]
        + [jax.ShapeDtypeStruct(part, bf16)] * (2 * layers - 1),
        in_specs=[VMEM] * 9,
        out_specs=[VMEM] * (2 * layers),
        scratch_shapes=[
            pltpu.VMEM((5 * block_rows * chunks, LANES), f32),
            pltpu.VMEM((8 * pair_rows * chunks, LANES), f32),
            pltpu.VMEM((8 * pair_rows * chunks, LANES), f32),
            pltpu.VMEM((5 * block_rows * chunks, LANES), f32),
        ],
        compiler_params=grant(12),
        name="pair",
    )(mine, other, near, cross, model_near, model_last, model_moved, model_pass, table)
    parts = [outs[0]]
    for step in range(layers):
        parts.append(
            move(
                outs[layers + step],
                lambda chip, core, layer: (chip + distance(layer, core), core, layer + step),
            )
        )
    for step in range(1, layers):
        parts.append(
            move(outs[step], lambda chip, core, layer: (chip, core, layer + step))
        )
    half = jax.ShapeDtypeStruct((block_rows, freq // layers), f32)
    keep, send = pl.pallas_call(
        functools.partial(gather_kernel, len(parts)),
        out_shape=[half, half],
        in_specs=[VMEM] * len(parts),
        out_specs=[VMEM, VMEM],
        compiler_params=grant(2),
        name="gather",
    )(*parts)
    moved = swap_cores(send)
    return pl.pallas_call(
        functools.partial(place_kernel, 1.0 / math.sqrt(blocks * stations)),
        out_shape=jax.ShapeDtypeStruct((2, stations, windows, freq // layers), f32),
        in_specs=[VMEM] * 3,
        out_specs=VMEM,
        compiler_params=grant(2),
        name="place",
    )(placing, keep, moved)


def solution(mesh):
    in_specs = (
        P(None, "blk", None, None),
        P("blk", "lay", None, None, None),
        P("blk", "lay"),
        P("blk", "lay"),
        P("blk", None),
    )
    out_specs = P(None, "blk", None, "lay")
    return jax.shard_map(local, mesh=mesh, in_specs=in_specs, out_specs=out_specs, check_vma=False)
```

```python
import functools
import math

import jax
import jax.numpy as jnp
import ml_dtypes
import numpy as np
from jax import lax
from jax.experimental import pallas as pl
from jax.experimental.pallas import tpu as pltpu
from jax.sharding import PartitionSpec as P


LANES = 128
AXES = ("blk", "lay")
EDGE_ROWS = 64
PIECES = 4
OUTSIDE = 2.0**100


def lag_table(freq_count, lag_count, window_count):
    half = lag_count // 2
    freq_index = np.arange(freq_count, dtype=np.int64)
    lag_index = np.arange(half + 1, dtype=np.int64)
    phase_index = freq_index[:, None] * lag_index[None, :] % (2 * freq_count)
    angle = phase_index.astype(np.float64) * (math.pi / freq_count)
    factor = 1.0 / math.sqrt(2.0 * freq_count * window_count)
    cosine, sine = np.cos(angle) * factor, -np.sin(angle) * factor
    edge = np.concatenate([cosine[:, half], -sine[:, half]]).reshape(-1, half)
    padding = np.zeros((EDGE_ROWS - edge.shape[0], half))
    table = np.concatenate([cosine[:, :half], sine[:, :half], edge, padding])
    return jnp.asarray(table.astype(ml_dtypes.bfloat16))


def prepare_kernel(
    slot_ref,
    spectra_ref,
    start_ref,
    end_ref,
    model_ref,
    mine_ref,
    swap_ref,
    placing_ref,
    model_near_ref,
    model_last_ref,
    slot,
    start,
    end,
    spectra,
    model,
    spread,
    rows,
    arrived,
):
    moves = [
        pltpu.make_async_copy(source, target, arrived.at[place])
        for place, (source, target) in enumerate(
            (
                (slot_ref, slot),
                (spectra_ref, spectra),
                (start_ref, start),
                (end_ref, end),
                (model_ref, model),
            )
        )
    ]
    for copy in moves:
        copy.start()
    parts, stations, windows, freq = spectra.shape
    chunks = freq // LANES
    core = lax.axis_index("blk") % 2
    layer = lax.axis_index("lay")
    lags = model.shape[4]
    half = lags // 2
    before = lax.broadcasted_iota(jnp.int32, (half, half), 0)
    after = lax.broadcasted_iota(jnp.int32, (half, half), 1)
    turn = (before + after == half) | (before + after == 0)
    turn = jnp.where(turn, 1.0, 0.0).astype(jnp.bfloat16)
    moves[0].wait()
    for place in range(stations):
        for station in range(stations):
            row = place * stations + station
            here = (slot[0, place] == station).astype(jnp.float32)
            placing_ref[row : row + 1, :] = jnp.full((1, placing_ref.shape[1]), here, jnp.float32)
    moves[1].wait()
    for part in range(parts):
        for place in range(stations):
            values = spectra[part, slot[0, place]].astype(jnp.float32)
            base = (part * stations + place) * windows * chunks
            for chunk in range(chunks):
                spread[pl.ds(base + chunk, windows, stride=chunks), :] = values[
                    :, chunk * LANES : (chunk + 1) * LANES
                ]
    ordered = spread[...].astype(jnp.bfloat16)
    size = ordered.shape[0]
    mine_ref[...] = ordered
    swap_ref[:size, :] = ordered

    shape = (stations * stations, lags)
    lag = lax.broadcasted_iota(jnp.int32, shape, 1)
    row = lax.broadcasted_iota(jnp.int32, shape, 0)
    diagonal = row % (stations + 1) == 0
    for copy in moves[2:]:
        copy.wait()

    def masked(offset):
        for first in range(stations):
            rows[first * stations : (first + 1) * stations, :] = model[0, offset, first].astype(
                jnp.float32
            )
        keep = (lag >= start[0, offset]) & (lag < end[0, offset])
        same = (layer == 0) & (offset == 0)
        keep = keep & jnp.logical_not(diagonal & same)
        return jnp.where(keep, rows[...], OUTSIDE).astype(jnp.bfloat16)

    values = jnp.concatenate(
        [masked(offset) for offset in (2 - 2 * core, 3, 1, 2 * core)], axis=0
    )
    turned = jnp.dot(values[:, :half], turn, preferred_element_type=jnp.float32)
    values = jnp.concatenate([values[:, half:], turned.astype(jnp.bfloat16)], axis=1)
    count = stations * stations
    model_near_ref[...] = values[:count]
    model_last_ref[...] = values[count : 2 * count]
    for chunk in range(lags // LANES):
        swap_ref[size + chunk * 2 * count : size + (chunk + 1) * 2 * count, :] = values[
            2 * count :, chunk * LANES : (chunk + 1) * LANES
        ]


def fetch_kernel(after_ref, table_ref, out_ref, arrived):
    del after_ref
    count = arrived.shape[0]
    size = table_ref.shape[0] // count
    moves = [
        pltpu.make_async_copy(
            table_ref.at[pl.ds(place * size, size)],
            out_ref.at[pl.ds(place * size, size)],
            arrived.at[place],
        )
        for place in range(count)
    ]
    for copy in moves:
        copy.start()
    for copy in moves:
        copy.wait()


def pair_kernel(
    layers,
    stations,
    windows,
    mine_ref,
    swap_ref,
    near_ref,
    cross_ref,
    model_near_ref,
    model_last_ref,
    model_moved_ref,
    table_ref,
    *rest,
):
    keep_ref = rest[0]
    own_refs = rest[1 : 1 + layers - 1]
    far_refs = rest[layers : 2 * layers]
    spec, cross_rows, resp_rows, sums = rest[2 * layers :]
    core = lax.axis_index("blk") % 2
    layer = lax.axis_index("lay")
    home = (layer == 0) & (core == 1)
    freq = (table_ref.shape[0] - EDGE_ROWS) // 2
    chunks = freq // LANES
    block_rows = 2 * stations * windows
    pair_rows = stations * stations
    total = 4 * pair_rows
    size = block_rows * chunks

    mine = mine_ref[...].astype(jnp.float32)
    other = swap_ref[:size, :].astype(jnp.float32)
    near = near_ref[...].astype(jnp.float32)
    cross = cross_ref[...].astype(jnp.float32)
    spec[0 * size : 1 * size, :] = mine
    spec[1 * size : 2 * size, :] = other
    spec[2 * size : 3 * size, :] = jnp.where(home, mine, near)
    spec[3 * size : 4 * size, :] = cross
    spec[4 * size : 5 * size, :] = jnp.where(home, other, cross)
    pairs = ((0, 2), (0, 3), (1, 2), (1, 4))

    def row_of(ref, index):
        return ref[index * chunks : (index + 1) * chunks, :]

    def spectrum(block, window):
        base = block * block_rows
        return [
            [row_of(spec, base + (part * stations + s) * windows + window) for s in range(stations)]
            for part in range(2)
        ]

    for pair, (first, second) in enumerate(pairs):
        real = [[None] * stations for _ in range(stations)]
        imag = [[None] * stations for _ in range(stations)]
        for window in range(windows):
            u = spectrum(first, window)
            v = spectrum(second, window)
            for i in range(stations):
                for j in range(stations):
                    re = u[0][i] * v[0][j] + u[1][i] * v[1][j]
                    im = u[1][i] * v[0][j] - u[0][i] * v[1][j]
                    real[i][j] = re if window == 0 else real[i][j] + re
                    imag[i][j] = im if window == 0 else imag[i][j] + im
        for i in range(stations):
            for j in range(stations):
                row = pair * pair_rows + i * stations + j
                cross_rows[row * chunks : (row + 1) * chunks, :] = real[i][j]
                row = row + total
                cross_rows[row * chunks : (row + 1) * chunks, :] = imag[i][j]

    def left(part):
        return jnp.concatenate(
            [
                cross_rows[pl.ds(part * total * chunks + chunk, total, stride=chunks), :].astype(
                    jnp.bfloat16
                )
                for chunk in range(chunks)
            ],
            axis=1,
        )

    half = table_ref.shape[1]
    tile = min(256, half)
    edge = table_ref[2 * freq :, :].astype(jnp.float32)
    pieces = freq // half
    edges = [
        jnp.concatenate(
            [edge[row : row + 1] for row in range(part * pieces, (part + 1) * pieces)], axis=1
        )
        for part in range(2)
    ]
    real, imag = left(0), left(1)
    last_lag = jnp.sum(
        real.astype(jnp.float32) * edges[0] + imag.astype(jnp.float32) * edges[1],
        axis=1,
        keepdims=True,
    )
    first_lane = lax.broadcasted_iota(jnp.int32, (total, tile), 1) == 0
    ahead, behind = [], []
    for place in range(half // tile):
        span = slice(place * tile, (place + 1) * tile)
        even = jnp.dot(real, table_ref[:freq, span], preferred_element_type=jnp.float32)
        odd = jnp.dot(imag, table_ref[freq : 2 * freq, span], preferred_element_type=jnp.float32)
        ahead.append(even + odd)
        value = even - odd
        behind.append(jnp.where(first_lane, last_lag, value) if place == 0 else value)
    misfit = []
    for place, value in enumerate(ahead + behind):
        span = slice(place * tile, (place + 1) * tile)
        last = jnp.where(
            core == 0,
            model_last_ref[:, span].astype(jnp.float32),
            model_moved_ref[:, span].astype(jnp.float32),
        )
        passed = jnp.concatenate(
            [
                swap_ref[
                    size + chunk * 2 * pair_rows : size + (chunk + 1) * 2 * pair_rows, :
                ].astype(jnp.float32)
                for chunk in range(place * tile // LANES, (place + 1) * tile // LANES)
            ],
            axis=1,
        )
        model = jnp.concatenate(
            [model_near_ref[:, span].astype(jnp.float32), last, passed], axis=0
        )
        misfit.append(jnp.where(model == OUTSIDE, 0.0, value - model).astype(jnp.bfloat16))
    count = half // tile
    first_behind = misfit[count].astype(jnp.float32)
    last_lag = first_behind[:, :1]
    misfit[count] = jnp.where(first_lane, 0.0, first_behind).astype(jnp.bfloat16)
    stacked = jnp.concatenate(
        [jnp.concatenate(misfit[:count], axis=1), jnp.concatenate(misfit[count:], axis=1)], axis=0
    )
    per_tile = tile // LANES
    for place in range(2 * chunks // per_tile):
        product = lax.dot_general(
            stacked,
            table_ref[place * tile : (place + 1) * tile, :],
            (((1,), (1,)), ((), ())),
            preferred_element_type=jnp.float32,
        )
        part, chunk = divmod(place * per_tile, chunks)
        weights = edges[part][:, chunk * LANES : chunk * LANES + tile]
        if part == 0:
            response = product[:total] + product[total:]
        else:
            response = product[:total] - product[total:]
        response = (response + last_lag * weights).astype(jnp.bfloat16).astype(jnp.float32)
        for inner in range(per_tile):
            start = part * total * chunks + chunk + inner
            resp_rows[pl.ds(start, total, stride=chunks), :] = response[
                :, inner * LANES : (inner + 1) * LANES
            ]

    written = set()

    def add(block, part, station, window, value):
        index = block * block_rows + (part * stations + station) * windows + window
        rows = slice(index * chunks, (index + 1) * chunks)
        if index in written:
            value = value + sums[rows, :]
        written.add(index)
        sums[rows, :] = value

    for pair, (first, second) in enumerate(pairs):
        base = pair * pair_rows
        r = [
            [row_of(resp_rows, part * total + base + n) for n in range(pair_rows)]
            for part in range(2)
        ]
        for window in range(windows):
            u = spectrum(first, window)
            v = spectrum(second, window)
            for i in range(stations):
                terms_re, terms_im = [], []
                for j in range(stations):
                    re, im = r[0][i * stations + j], r[1][i * stations + j]
                    terms_re.append(re * v[0][j] - im * v[1][j])
                    terms_im.append(re * v[1][j] + im * v[0][j])
                add(first, 0, i, window, sum(terms_re[1:], terms_re[0]))
                add(first, 1, i, window, sum(terms_im[1:], terms_im[0]))
            for j in range(stations):
                terms_re, terms_im = [], []
                for i in range(stations):
                    re, im = r[0][i * stations + j], r[1][i * stations + j]
                    terms_re.append(re * u[0][i] + im * u[1][i])
                    terms_im.append(re * u[1][i] - im * u[0][i])
                add(second, 0, j, window, sum(terms_re[1:], terms_re[0]))
                add(second, 1, j, window, sum(terms_im[1:], terms_im[0]))

    part_near = sums[2 * size : 3 * size, :]
    part_last = sums[4 * size : 5 * size, :]
    sums[0 * size : 1 * size, :] += jnp.where(home, part_near, 0.0)
    sums[1 * size : 2 * size, :] += jnp.where(home, part_last, 0.0)
    sums[2 * size : 3 * size, :] = jnp.where(home, 0.0, part_near)
    sums[3 * size : 4 * size, :] += jnp.where(home, 0.0, part_last)

    width = chunks // layers
    for step in range(layers):
        start = lax.rem(layer + step, layers) * width
        for inner in range(width):
            span = slice(inner * LANES, (inner + 1) * LANES)
            own = sums[pl.ds(start + inner, 2 * block_rows, stride=chunks), :]
            if step == 0:
                keep_ref[:, span] = own
            else:
                own_refs[step - 1][:, span] = own.astype(jnp.bfloat16)
            far = sums[pl.ds(2 * size + start + inner, 2 * block_rows, stride=chunks), :]
            far_refs[step][:, span] = far.astype(jnp.bfloat16)


def gather_kernel(count, *refs):
    keep_ref, send_ref = refs[count:]
    half = keep_ref.shape[0]
    total = refs[0][...]
    for ref in refs[1:count]:
        total = total + ref[...].astype(jnp.float32)
    keep_ref[...] = total[:half]
    send_ref[...] = total[half:]


def place_kernel(scale, placing_ref, keep_ref, moved_ref, out_ref):
    parts, stations, windows, _ = out_ref.shape
    total = (keep_ref[...] + moved_ref[...]) * scale
    for station in range(stations):
        here = [
            placing_ref[row : row + 1, :]
            for row in range(station, stations * stations, stations)
        ]
        for part in range(parts):
            value = None
            for place in range(stations):
                base = (part * stations + place) * windows
                term = here[place] * total[base : base + windows, :]
                value = term if value is None else value + term
            out_ref[part, station] = value


VMEM = pl.BlockSpec(memory_space=pltpu.VMEM)
HBM = pl.BlockSpec(memory_space=pltpu.HBM)


def grant(mebibytes):
    return pltpu.CompilerParams(vmem_limit_bytes=mebibytes * 1024 * 1024)


def local(spectra, model_corr, window_start, window_end, station_slot):
    _, stations, windows, freq = spectra.shape
    lags = model_corr.shape[4]
    layers = lax.axis_size("lay")
    blocks = lax.axis_size("blk")
    chips = blocks // 2
    chunks = freq // LANES
    pair_rows = stations * stations
    block_rows = 2 * stations * windows
    f32, bf16 = jnp.float32, jnp.bfloat16

    def distance(layer, core):
        if core == 0:
            return 2 * layer + 1
        return 2 * layer if layer > 0 else 2 * layers

    def move(value, target):
        pairs = []
        for block in range(blocks):
            for layer in range(layers):
                chip, core, to_layer = target(block // 2, block % 2, layer)
                pairs.append(
                    (block * layers + layer, (chip % chips * 2 + core) * layers + to_layer % layers)
                )
        return lax.ppermute(value, AXES, pairs)

    def swap_cores(value):
        return move(value, lambda chip, core, layer: (chip, 1 - core, layer))

    station_slot, spectra, window_start, window_end, model_corr = (
        pltpu.with_memory_space_constraint(value, pltpu.HBM)
        for value in (station_slot, spectra, window_start, window_end, model_corr)
    )
    swap_rows = block_rows * chunks + 2 * pair_rows * lags // LANES
    mine, swap, placing, model_near, model_last = pl.pallas_call(
        prepare_kernel,
        out_shape=[
            jax.ShapeDtypeStruct((block_rows * chunks, LANES), bf16),
            jax.ShapeDtypeStruct((swap_rows, LANES), bf16),
            jax.ShapeDtypeStruct((stations * stations, freq // layers), f32),
            jax.ShapeDtypeStruct((pair_rows, lags), bf16),
            jax.ShapeDtypeStruct((pair_rows, lags), bf16),
        ],
        in_specs=[HBM] * 5,
        out_specs=[VMEM] * 5,
        scratch_shapes=[
            pltpu.SMEM(station_slot.shape, jnp.int32),
            pltpu.SMEM(window_start.shape, jnp.int32),
            pltpu.SMEM(window_end.shape, jnp.int32),
            pltpu.VMEM(spectra.shape, bf16),
            pltpu.VMEM(model_corr.shape, bf16),
            pltpu.VMEM((block_rows * chunks, LANES), f32),
            pltpu.VMEM((pair_rows, lags), f32),
            pltpu.SemaphoreType.DMA((5,)),
        ],
        compiler_params=grant(2),
        name="prepare",
    )(station_slot, spectra, window_start, window_end, model_corr)
    cross = move(mine, lambda chip, core, layer: (chip - distance(layer, 1 - core), 1 - core, layer))
    near = move(
        mine,
        lambda chip, core, layer: (
            chip ^ 1 if layer == 0 and core == 1 else chip - distance(layer, core),
            core,
            layer,
        ),
    )
    model_moved = move(model_last, lambda chip, core, layer: (chip, core, layer + 1))
    swap = swap_cores(swap)
    table = pltpu.with_memory_space_constraint(lag_table(freq, lags, windows), pltpu.HBM)
    table = pl.pallas_call(
        fetch_kernel,
        out_shape=jax.ShapeDtypeStruct(table.shape, bf16),
        in_specs=[VMEM, HBM],
        out_specs=VMEM,
        scratch_shapes=[pltpu.SemaphoreType.DMA((PIECES,))],
        compiler_params=grant(6),
        cost_estimate=pl.CostEstimate(flops=0, bytes_accessed=2 * freq * lags, transcendentals=0),
        name="fetch",
    )(placing, table)

    part = (2 * block_rows, freq // layers)
    outs = pl.pallas_call(
        functools.partial(pair_kernel, layers, stations, windows),
        out_shape=[jax.ShapeDtypeStruct(part, f32)]
        + [jax.ShapeDtypeStruct(part, bf16)] * (2 * layers - 1),
        in_specs=[VMEM] * 8,
        out_specs=[VMEM] * (2 * layers),
        scratch_shapes=[
            pltpu.VMEM((5 * block_rows * chunks, LANES), f32),
            pltpu.VMEM((8 * pair_rows * chunks, LANES), f32),
            pltpu.VMEM((8 * pair_rows * chunks, LANES), f32),
            pltpu.VMEM((5 * block_rows * chunks, LANES), f32),
        ],
        compiler_params=grant(12),
        name="pair",
    )(mine, swap, near, cross, model_near, model_last, model_moved, table)
    parts = [outs[0]]
    for step in range(layers):
        parts.append(
            move(
                outs[layers + step],
                lambda chip, core, layer: (chip + distance(layer, core), core, layer + step),
            )
        )
    for step in range(1, layers):
        parts.append(
            move(outs[step], lambda chip, core, layer: (chip, core, layer + step))
        )
    half = jax.ShapeDtypeStruct((block_rows, freq // layers), f32)
    keep, send = pl.pallas_call(
        functools.partial(gather_kernel, len(parts)),
        out_shape=[half, half],
        in_specs=[VMEM] * len(parts),
        out_specs=[VMEM, VMEM],
        compiler_params=grant(2),
        name="gather",
    )(*parts)
    moved = swap_cores(send)
    return pl.pallas_call(
        functools.partial(place_kernel, 1.0 / math.sqrt(blocks * stations)),
        out_shape=jax.ShapeDtypeStruct((2, stations, windows, freq // layers), f32),
        in_specs=[VMEM] * 3,
        out_specs=VMEM,
        compiler_params=grant(2),
        name="place",
    )(placing, keep, moved)


def solution(mesh):
    in_specs = (
        P(None, "blk", None, None),
        P("blk", "lay", None, None, None),
        P("blk", "lay"),
        P("blk", "lay"),
        P("blk", None),
    )
    out_specs = P(None, "blk", None, "lay")
    return jax.shard_map(local, mesh=mesh, in_specs=in_specs, out_specs=out_specs, check_vma=False)
```

```python
import functools
import math

import jax
import jax.numpy as jnp
import ml_dtypes
import numpy as np
from jax import lax
from jax.experimental import pallas as pl
from jax.experimental.pallas import tpu as pltpu
from jax.sharding import PartitionSpec as P


LANES = 128
AXES = ("blk", "lay")
EDGE_ROWS = 64
PIECES = 4
OUTSIDE = 2.0**100


def lag_table(freq_count, lag_count, window_count):
    half = lag_count // 2
    freq_index = np.arange(freq_count, dtype=np.int64)
    lag_index = np.arange(half + 1, dtype=np.int64)
    phase_index = freq_index[:, None] * lag_index[None, :] % (2 * freq_count)
    angle = phase_index.astype(np.float64) * (math.pi / freq_count)
    factor = 1.0 / math.sqrt(2.0 * freq_count * window_count)
    cosine, sine = np.cos(angle) * factor, -np.sin(angle) * factor
    edge = np.concatenate([cosine[:, half], -sine[:, half]]).reshape(-1, half)
    padding = np.zeros((EDGE_ROWS - edge.shape[0], half))
    table = np.concatenate([cosine[:, :half], sine[:, :half], edge, padding])
    return jnp.asarray(table.astype(ml_dtypes.bfloat16))


def copies(sources, targets, arrived):
    moves = [
        pltpu.make_async_copy(source, target, arrived.at[place])
        for place, (source, target) in enumerate(zip(sources, targets))
    ]
    for copy in moves:
        copy.start()
    return moves


def order_kernel(slot_ref, spectra_ref, mine_ref, placing_ref, slot, spectra, spread, arrived):
    moves = copies((slot_ref, spectra_ref), (slot, spectra), arrived)
    parts, stations, windows, freq = spectra.shape
    chunks = freq // LANES
    moves[0].wait()
    for place in range(stations):
        for station in range(stations):
            row = place * stations + station
            here = (slot[0, place] == station).astype(jnp.float32)
            placing_ref[row : row + 1, :] = jnp.full((1, placing_ref.shape[1]), here, jnp.float32)
    moves[1].wait()
    for part in range(parts):
        for place in range(stations):
            values = spectra[part, slot[0, place]].astype(jnp.float32)
            base = (part * stations + place) * windows * chunks
            for chunk in range(chunks):
                spread[pl.ds(base + chunk, windows, stride=chunks), :] = values[
                    :, chunk * LANES : (chunk + 1) * LANES
                ]
    mine_ref[...] = spread[...].astype(jnp.bfloat16)


def mask_kernel(start_ref, end_ref, model_ref, near_ref, last_ref, pass_ref, rows):
    core = lax.axis_index("blk") % 2
    layer = lax.axis_index("lay")
    stations, lags = model_ref.shape[3:]
    half = lags // 2
    before = lax.broadcasted_iota(jnp.int32, (half, half), 0)
    after = lax.broadcasted_iota(jnp.int32, (half, half), 1)
    turn = (before + after == half) | (before + after == 0)
    turn = jnp.where(turn, 1.0, 0.0).astype(jnp.bfloat16)
    count = stations * stations
    lag = lax.broadcasted_iota(jnp.int32, (count, lags), 1)
    row = lax.broadcasted_iota(jnp.int32, (count, lags), 0)
    diagonal = row % (stations + 1) == 0
    start, end = start_ref[...], end_ref[...]
    values = []
    for offset in range(4):
        for first in range(stations):
            rows[first * stations : (first + 1) * stations, :] = model_ref[0, offset, first].astype(
                jnp.float32
            )
        keep = (lag >= start[:, offset : offset + 1]) & (lag < end[:, offset : offset + 1])
        if offset == 0:
            keep = keep & jnp.logical_not(diagonal & (layer == 0))
        values.append(jnp.where(keep, rows[...], OUTSIDE))
    even = core == 0
    values = jnp.concatenate(
        [
            jnp.where(even, values[2], values[0]),
            values[3],
            values[1],
            jnp.where(even, values[0], values[2]),
        ],
        axis=0,
    ).astype(jnp.bfloat16)
    turned = jnp.dot(values[:, :half], turn, preferred_element_type=jnp.float32)
    values = jnp.concatenate([values[:, half:], turned.astype(jnp.bfloat16)], axis=1)
    near_ref[...] = values[:count]
    last_ref[...] = values[count : 2 * count]
    pass_ref[...] = values[2 * count :]


def is_home():
    return (lax.axis_index("lay") == 0) & (lax.axis_index("blk") % 2 == 1)


PAIRS = ((0, 2), (0, 3), (1, 2), (1, 4))


def unfold(mine_ref, other_ref, near_ref, cross_ref, spec):
    home = is_home()
    size = mine_ref.shape[0]
    mine = mine_ref[...].astype(jnp.float32)
    other = other_ref[...].astype(jnp.float32)
    near = near_ref[...].astype(jnp.float32)
    cross = cross_ref[...].astype(jnp.float32)
    spec[0 * size : 1 * size, :] = mine
    spec[1 * size : 2 * size, :] = other
    spec[2 * size : 3 * size, :] = jnp.where(home, mine, near)
    spec[3 * size : 4 * size, :] = cross
    spec[4 * size : 5 * size, :] = jnp.where(home, other, cross)


def spectrum(spec, stations, windows, chunks, block, window):
    rows = []
    for part in range(2):
        rows.append([])
        for station in range(stations):
            index = ((block * 2 + part) * stations + station) * windows + window
            rows[part].append(spec[index * chunks : (index + 1) * chunks, :])
    return rows


def edge_rows(table_ref, freq):
    half = table_ref.shape[1]
    edge = table_ref[2 * freq :, :].astype(jnp.float32)
    pieces = freq // half
    return [
        jnp.concatenate(
            [edge[row : row + 1] for row in range(part * pieces, (part + 1) * pieces)], axis=1
        )
        for part in range(2)
    ]


def lag_kernel(
    stations, windows, mine_ref, other_ref, near_ref, cross_ref, table_ref, lagged_ref, spec, rows
):
    freq = (table_ref.shape[0] - EDGE_ROWS) // 2
    chunks = freq // LANES
    pair_rows = stations * stations
    total = len(PAIRS) * pair_rows
    unfold(mine_ref, other_ref, near_ref, cross_ref, spec)
    for pair, (first, second) in enumerate(PAIRS):
        real = [[None] * stations for _ in range(stations)]
        imag = [[None] * stations for _ in range(stations)]
        for window in range(windows):
            u = spectrum(spec, stations, windows, chunks, first, window)
            v = spectrum(spec, stations, windows, chunks, second, window)
            for i in range(stations):
                for j in range(stations):
                    re = u[0][i] * v[0][j] + u[1][i] * v[1][j]
                    im = u[1][i] * v[0][j] - u[0][i] * v[1][j]
                    real[i][j] = re if window == 0 else real[i][j] + re
                    imag[i][j] = im if window == 0 else imag[i][j] + im
        for i in range(stations):
            for j in range(stations):
                row = pair * pair_rows + i * stations + j
                rows[row * chunks : (row + 1) * chunks, :] = real[i][j]
                row = row + total
                rows[row * chunks : (row + 1) * chunks, :] = imag[i][j]

    def left(part):
        return jnp.concatenate(
            [
                rows[pl.ds(part * total * chunks + chunk, total, stride=chunks), :].astype(
                    jnp.bfloat16
                )
                for chunk in range(chunks)
            ],
            axis=1,
        )

    half = table_ref.shape[1]
    tile = min(256, half)
    edges = edge_rows(table_ref, freq)
    real, imag = left(0), left(1)
    last_lag = jnp.sum(
        real.astype(jnp.float32) * edges[0] + imag.astype(jnp.float32) * edges[1],
        axis=1,
        keepdims=True,
    )
    first_lane = lax.broadcasted_iota(jnp.int32, (total, tile), 1) == 0
    for place in range(half // tile):
        span = slice(place * tile, (place + 1) * tile)
        even = jnp.dot(real, table_ref[:freq, span], preferred_element_type=jnp.float32)
        odd = jnp.dot(imag, table_ref[freq : 2 * freq, span], preferred_element_type=jnp.float32)
        lagged_ref[:, span] = even + odd
        value = even - odd
        if place == 0:
            value = jnp.where(first_lane, last_lag, value)
        lagged_ref[:, half + place * tile : half + (place + 1) * tile] = value


def response_kernel(
    layers,
    stations,
    windows,
    lagged_ref,
    mine_ref,
    other_ref,
    near_ref,
    cross_ref,
    model_near_ref,
    model_last_ref,
    model_moved_ref,
    model_pass_ref,
    table_ref,
    *rest,
):
    far_refs = rest[:layers]
    resp_rows, home_sums, spec, sums = rest[layers:]
    freq = (table_ref.shape[0] - EDGE_ROWS) // 2
    chunks = freq // LANES
    pair_rows = stations * stations
    total = len(PAIRS) * pair_rows
    block_rows = 2 * stations * windows
    size = block_rows * chunks
    core = lax.axis_index("blk") % 2
    home = is_home()
    half = table_ref.shape[1]
    tile = min(256, half)
    edges = edge_rows(table_ref, freq)
    misfit = []
    for place in range(2 * half // tile):
        span = slice(place * tile, (place + 1) * tile)
        last = jnp.where(
            core == 0,
            model_last_ref[:, span].astype(jnp.float32),
            model_moved_ref[:, span].astype(jnp.float32),
        )
        model = jnp.concatenate(
            [
                model_near_ref[:, span].astype(jnp.float32),
                last,
                model_pass_ref[:, span].astype(jnp.float32),
            ],
            axis=0,
        )
        value = jnp.where(model == OUTSIDE, 0.0, lagged_ref[:, span] - model)
        misfit.append(value.astype(jnp.bfloat16))
    count = half // tile
    first_lane = lax.broadcasted_iota(jnp.int32, (total, tile), 1) == 0
    first_behind = misfit[count].astype(jnp.float32)
    last_lag = first_behind[:, :1]
    misfit[count] = jnp.where(first_lane, 0.0, first_behind).astype(jnp.bfloat16)
    stacked = jnp.concatenate(
        [jnp.concatenate(misfit[:count], axis=1), jnp.concatenate(misfit[count:], axis=1)], axis=0
    )
    per_tile = tile // LANES
    for place in range(2 * chunks // per_tile):
        part, chunk = divmod(place * per_tile, chunks)
        low = chunk * LANES
        if low + tile <= half:
            table = table_ref[part * freq : part * freq + half, low : low + tile]
            product = jnp.dot(stacked, table, preferred_element_type=jnp.float32)
        else:
            product = lax.dot_general(
                stacked,
                table_ref[place * tile : (place + 1) * tile, :],
                (((1,), (1,)), ((), ())),
                preferred_element_type=jnp.float32,
            )
        weights = edges[part][:, chunk * LANES : chunk * LANES + tile]
        if part == 0:
            response = product[:total] + product[total:]
        else:
            response = product[:total] - product[total:]
        response = (response + last_lag * weights).astype(jnp.bfloat16).astype(jnp.float32)
        for inner in range(per_tile):
            start = part * total * chunks + chunk + inner
            resp_rows[pl.ds(start, total, stride=chunks), :] = response[
                :, inner * LANES : (inner + 1) * LANES
            ]

    unfold(mine_ref, other_ref, near_ref, cross_ref, spec)
    written = set()
    for pair, (first, second) in enumerate(PAIRS):
        r = response_rows(resp_rows, pair, pair_rows, total, chunks)
        for window in range(windows):
            u = spectrum(spec, stations, windows, chunks, first, window)
            for j in range(stations):
                terms_re, terms_im = [], []
                for i in range(stations):
                    re, im = r[0][i * stations + j], r[1][i * stations + j]
                    terms_re.append(re * u[0][i] + im * u[1][i])
                    terms_im.append(re * u[1][i] - im * u[0][i])
                for part, terms in enumerate((terms_re, terms_im)):
                    index = (((second - 2) * 2 + part) * stations + j) * windows + window
                    accumulate(sums, written, index, chunks, terms)
    part_near = sums[:size, :]
    part_last = sums[2 * size :, :]
    home_sums[:size, :] = jnp.where(home, part_near, 0.0)
    home_sums[size:, :] = jnp.where(home, part_last, 0.0)
    sums[:size, :] = jnp.where(home, 0.0, part_near)
    sums[size : 2 * size, :] += jnp.where(home, 0.0, part_last)
    for step in range(layers):
        write_share(sums, far_refs[step], step, layers, 2 * block_rows, chunks)


def own_kernel(
    layers,
    stations,
    windows,
    resp_rows,
    home_sums,
    mine_ref,
    other_ref,
    near_ref,
    cross_ref,
    keep_ref,
    *rest,
):
    own_refs = rest[: layers - 1]
    spec, sums = rest[layers - 1 :]
    block_rows = 2 * stations * windows
    chunks = mine_ref.shape[0] // block_rows
    pair_rows = stations * stations
    total = len(PAIRS) * pair_rows
    unfold(mine_ref, other_ref, near_ref, cross_ref, spec)
    sums[...] = home_sums[...]
    written = set(range(2 * block_rows))
    for pair, (first, second) in enumerate(PAIRS):
        r = response_rows(resp_rows, pair, pair_rows, total, chunks)
        for window in range(windows):
            v = spectrum(spec, stations, windows, chunks, second, window)
            for i in range(stations):
                terms_re, terms_im = [], []
                for j in range(stations):
                    re, im = r[0][i * stations + j], r[1][i * stations + j]
                    terms_re.append(re * v[0][j] - im * v[1][j])
                    terms_im.append(re * v[1][j] + im * v[0][j])
                for part, terms in enumerate((terms_re, terms_im)):
                    index = ((first * 2 + part) * stations + i) * windows + window
                    accumulate(sums, written, index, chunks, terms)
    for step in range(layers):
        target = keep_ref if step == 0 else own_refs[step - 1]
        write_share(sums, target, step, layers, 2 * block_rows, chunks)


def response_rows(resp_rows, pair, pair_rows, total, chunks):
    rows = []
    for part in range(2):
        base = part * total + pair * pair_rows
        rows.append(
            [
                resp_rows[(base + row) * chunks : (base + row + 1) * chunks, :]
                for row in range(pair_rows)
            ]
        )
    return rows


def accumulate(sums, written, index, chunks, terms):
    rows = slice(index * chunks, (index + 1) * chunks)
    value = sum(terms[1:], terms[0])
    if index in written:
        value = value + sums[rows, :]
    written.add(index)
    sums[rows, :] = value


def write_share(sums, target, step, layers, count, chunks):
    width = chunks // layers
    start = lax.rem(lax.axis_index("lay") + step, layers) * width
    for inner in range(width):
        values = sums[pl.ds(start + inner, count, stride=chunks), :]
        target[:, inner * LANES : (inner + 1) * LANES] = values.astype(target.dtype)


def add_kernel(*refs):
    total = refs[0][...].astype(jnp.float32)
    for ref in refs[1:-1]:
        total = total + ref[...].astype(jnp.float32)
    refs[-1][...] = total


def gather_kernel(count, *refs):
    keep_ref, send_ref = refs[count:]
    half = keep_ref.shape[0]
    total = refs[0][...]
    for ref in refs[1:count]:
        total = total + ref[...].astype(jnp.float32)
    keep_ref[...] = total[:half]
    send_ref[...] = total[half:]


def place_kernel(scale, placing_ref, keep_ref, moved_ref, out_ref):
    parts, stations, windows, _ = out_ref.shape
    total = (keep_ref[...] + moved_ref[...]) * scale
    for station in range(stations):
        here = [
            placing_ref[row : row + 1, :]
            for row in range(station, stations * stations, stations)
        ]
        for part in range(parts):
            value = None
            for place in range(stations):
                base = (part * stations + place) * windows
                term = here[place] * total[base : base + windows, :]
                value = term if value is None else value + term
            out_ref[part, station] = value


VMEM = pl.BlockSpec(memory_space=pltpu.VMEM)
HBM = pl.BlockSpec(memory_space=pltpu.HBM)


def grant(mebibytes):
    return pltpu.CompilerParams(vmem_limit_bytes=mebibytes * 1024 * 1024)


def local(spectra, model_corr, window_start, window_end, station_slot):
    _, stations, windows, freq = spectra.shape
    lags = model_corr.shape[4]
    layers = lax.axis_size("lay")
    blocks = lax.axis_size("blk")
    chips = blocks // 2
    chunks = freq // LANES
    pair_rows = stations * stations
    block_rows = 2 * stations * windows
    f32, bf16 = jnp.float32, jnp.bfloat16

    def distance(layer, core):
        if core == 0:
            return 2 * layer + 1
        return 2 * layer if layer > 0 else 2 * layers

    def move(value, target):
        pairs = []
        for block in range(blocks):
            for layer in range(layers):
                chip, core, to_layer = target(block // 2, block % 2, layer)
                pairs.append(
                    (block * layers + layer, (chip % chips * 2 + core) * layers + to_layer % layers)
                )
        return lax.ppermute(value, AXES, pairs)

    def swap_cores(value):
        return move(value, lambda chip, core, layer: (chip, 1 - core, layer))

    station_slot, spectra = (
        pltpu.with_memory_space_constraint(value, pltpu.HBM) for value in (station_slot, spectra)
    )
    mine, placing = pl.pallas_call(
        order_kernel,
        out_shape=[
            jax.ShapeDtypeStruct((block_rows * chunks, LANES), bf16),
            jax.ShapeDtypeStruct((stations * stations, freq // layers), f32),
        ],
        in_specs=[HBM] * 2,
        out_specs=[VMEM] * 2,
        scratch_shapes=[
            pltpu.SMEM(station_slot.shape, jnp.int32),
            pltpu.VMEM(spectra.shape, bf16),
            pltpu.VMEM((block_rows * chunks, LANES), f32),
            pltpu.SemaphoreType.DMA((2,)),
        ],
        compiler_params=grant(2),
        cost_estimate=pl.CostEstimate(flops=5 * 10**9, bytes_accessed=10**6, transcendentals=0),
        name="order",
    )(station_slot, spectra)
    cross = move(mine, lambda chip, core, layer: (chip - distance(layer, 1 - core), 1 - core, layer))
    def near_target(chip, core, layer):
        if core == 0 and chip == 2 and layer < 2:
            layer = 1 - layer
        if layer == 0 and core == 1:
            return chip ^ 1, core, layer
        return chip - distance(layer, core), core, layer

    near = move(
        mine,
        near_target,
    )
    other = swap_cores(mine)
    model_near, model_last, model_pass = pl.pallas_call(
        mask_kernel,
        out_shape=[
            jax.ShapeDtypeStruct((pair_rows, lags), bf16),
            jax.ShapeDtypeStruct((pair_rows, lags), bf16),
            jax.ShapeDtypeStruct((2 * pair_rows, lags), bf16),
        ],
        in_specs=[VMEM] * 3,
        out_specs=[VMEM] * 3,
        scratch_shapes=[pltpu.VMEM((pair_rows, lags), f32)],
        compiler_params=grant(4),
        cost_estimate=pl.CostEstimate(flops=5 * 10**9, bytes_accessed=10**6, transcendentals=0),
        name="mask",
    )(window_start, window_end, model_corr)
    model_pass = swap_cores(model_pass)
    model_moved = move(model_last, lambda chip, core, layer: (chip, core, layer + 1))
    table = lag_table(freq, lags, windows)
    total = 4 * pair_rows
    blocks_in = (mine, other, near, cross)
    spec = pltpu.VMEM((5 * block_rows * chunks, LANES), f32)
    lagged = pl.pallas_call(
        functools.partial(lag_kernel, stations, windows),
        out_shape=jax.ShapeDtypeStruct((total, lags), f32),
        in_specs=[VMEM] * 5,
        out_specs=VMEM,
        scratch_shapes=[spec, pltpu.VMEM((2 * total * chunks, LANES), f32)],
        compiler_params=grant(8),
        name="lag",
    )(*blocks_in, table)
    part = (2 * block_rows, freq // layers)
    outs = pl.pallas_call(
        functools.partial(response_kernel, layers, stations, windows),
        out_shape=[jax.ShapeDtypeStruct(part, bf16)] * layers
        + [
            jax.ShapeDtypeStruct((2 * total * chunks, LANES), f32),
            jax.ShapeDtypeStruct((2 * block_rows * chunks, LANES), f32),
        ],
        in_specs=[VMEM] * 10,
        out_specs=[VMEM] * (layers + 2),
        scratch_shapes=[spec, pltpu.VMEM((3 * block_rows * chunks, LANES), f32)],
        compiler_params=grant(12),
        name="response",
    )(lagged, *blocks_in, model_near, model_last, model_moved, model_pass, table)
    parts = []
    for step in range(layers):
        parts.append(
            move(
                outs[step],
                lambda chip, core, layer: (chip + distance(layer, core), core, layer + step),
            )
        )
    owns = pl.pallas_call(
        functools.partial(own_kernel, layers, stations, windows),
        out_shape=[jax.ShapeDtypeStruct(part, f32)]
        + [jax.ShapeDtypeStruct(part, bf16)] * (layers - 1),
        in_specs=[VMEM] * 6,
        out_specs=[VMEM] * layers,
        scratch_shapes=[spec, pltpu.VMEM((2 * block_rows * chunks, LANES), f32)],
        compiler_params=grant(8),
        name="own",
    )(outs[layers], outs[layers + 1], *blocks_in)
    for step in range(1, layers):
        parts.append(move(owns[step], lambda chip, core, layer: (chip, core, layer + step)))
    parts.insert(0, owns[0])
    both = jax.ShapeDtypeStruct((2 * block_rows, freq // layers), f32)
    arrived = parts[1 : 1 + layers]
    arrived = pl.pallas_call(
        add_kernel,
        out_shape=both,
        in_specs=[VMEM] * len(arrived),
        out_specs=VMEM,
        compiler_params=grant(2),
        name="arrived",
    )(*arrived)
    parts = [parts[0], arrived] + parts[1 + layers :]
    half = jax.ShapeDtypeStruct((block_rows, freq // layers), f32)
    keep, send = pl.pallas_call(
        functools.partial(gather_kernel, len(parts)),
        out_shape=[half, half],
        in_specs=[VMEM] * len(parts),
        out_specs=[VMEM, VMEM],
        compiler_params=grant(2),
        name="gather",
    )(*parts)
    moved = swap_cores(send)
    return pl.pallas_call(
        functools.partial(place_kernel, 1.0 / math.sqrt(blocks * stations)),
        out_shape=jax.ShapeDtypeStruct((2, stations, windows, freq // layers), f32),
        in_specs=[VMEM] * 3,
        out_specs=VMEM,
        compiler_params=grant(2),
        name="place",
    )(placing, keep, moved)


def solution(mesh):
    in_specs = (
        P(None, "blk", None, None),
        P("blk", "lay", None, None, None),
        P("blk", "lay"),
        P("blk", "lay"),
        P("blk", None),
    )
    out_specs = P(None, "blk", None, "lay")
    return jax.shard_map(local, mesh=mesh, in_specs=in_specs, out_specs=out_specs, check_vma=False)
```

```python
import functools
import math

import jax
import jax.numpy as jnp
import ml_dtypes
import numpy as np
from jax import lax
from jax.experimental import pallas as pl
from jax.experimental.pallas import tpu as pltpu
from jax.sharding import PartitionSpec as P


LANES = 128
AXES = ("blk", "lay")
EDGE_ROWS = 64
PIECES = 4
CHANGED = ((1, 0),)
OUTSIDE = 2.0**100


def lag_table(freq_count, lag_count, window_count):
    half = lag_count // 2
    freq_index = np.arange(freq_count, dtype=np.int64)
    lag_index = np.arange(half + 1, dtype=np.int64)
    phase_index = freq_index[:, None] * lag_index[None, :] % (2 * freq_count)
    angle = phase_index.astype(np.float64) * (math.pi / freq_count)
    factor = 1.0 / math.sqrt(2.0 * freq_count * window_count)
    cosine, sine = np.cos(angle) * factor, -np.sin(angle) * factor
    edge = np.concatenate([cosine[:, half], -sine[:, half]]).reshape(-1, half)
    padding = np.zeros((EDGE_ROWS - edge.shape[0], half))
    table = np.concatenate([cosine[:, :half], sine[:, :half], edge, padding])
    return jnp.asarray(table.astype(ml_dtypes.bfloat16))


def copies(sources, targets, arrived):
    moves = [
        pltpu.make_async_copy(source, target, arrived.at[place])
        for place, (source, target) in enumerate(zip(sources, targets))
    ]
    for copy in moves:
        copy.start()
    return moves


def order_kernel(slot_ref, spectra_ref, mine_ref, placing_ref, slot, spectra, spread, arrived):
    moves = copies((slot_ref, spectra_ref), (slot, spectra), arrived)
    parts, stations, windows, freq = spectra.shape
    chunks = freq // LANES
    moves[0].wait()
    for place in range(stations):
        for station in range(stations):
            row = place * stations + station
            here = (slot[0, place] == station).astype(jnp.float32)
            placing_ref[row : row + 1, :] = jnp.full((1, placing_ref.shape[1]), here, jnp.float32)
    moves[1].wait()
    for part in range(parts):
        for place in range(stations):
            values = spectra[part, slot[0, place]].astype(jnp.float32)
            base = (part * stations + place) * windows * chunks
            for chunk in range(chunks):
                spread[pl.ds(base + chunk, windows, stride=chunks), :] = values[
                    :, chunk * LANES : (chunk + 1) * LANES
                ]
    mine_ref[...] = spread[...].astype(jnp.bfloat16)


def mask_kernel(start_ref, end_ref, model_ref, near_ref, last_ref, pass_ref, rows):
    core = lax.axis_index("blk") % 2
    layer = lax.axis_index("lay")
    stations, lags = model_ref.shape[3:]
    half = lags // 2
    before = lax.broadcasted_iota(jnp.int32, (half, half), 0)
    after = lax.broadcasted_iota(jnp.int32, (half, half), 1)
    turn = (before + after == half) | (before + after == 0)
    turn = jnp.where(turn, 1.0, 0.0).astype(jnp.bfloat16)
    count = stations * stations
    lag = lax.broadcasted_iota(jnp.int32, (count, lags), 1)
    row = lax.broadcasted_iota(jnp.int32, (count, lags), 0)
    diagonal = row % (stations + 1) == 0
    start, end = start_ref[...], end_ref[...]
    values = []
    for offset in range(4):
        for first in range(stations):
            rows[first * stations : (first + 1) * stations, :] = model_ref[0, offset, first].astype(
                jnp.float32
            )
        keep = (lag >= start[:, offset : offset + 1]) & (lag < end[:, offset : offset + 1])
        if offset == 0:
            keep = keep & jnp.logical_not(diagonal & (layer == 0))
        values.append(jnp.where(keep, rows[...], OUTSIDE))
    even = core == 0
    values = jnp.concatenate(
        [
            jnp.where(even, values[2], values[0]),
            values[3],
            values[1],
            jnp.where(even, values[0], values[2]),
        ],
        axis=0,
    ).astype(jnp.bfloat16)
    turned = jnp.dot(values[:, :half], turn, preferred_element_type=jnp.float32)
    values = jnp.concatenate([values[:, half:], turned.astype(jnp.bfloat16)], axis=1)
    near_ref[...] = values[:count]
    last_ref[...] = values[count : 2 * count]
    pass_ref[...] = values[2 * count :]


def changed():
    chips = lax.axis_size("blk") // 2
    layers = lax.axis_size("lay")
    core, layer = lax.axis_index("blk") % 2, lax.axis_index("lay")
    distance = jnp.where(core == 0, 2 * layer + 1, jnp.where(layer > 0, 2 * layer, 2 * layers))
    target = lax.rem(lax.axis_index("blk") // 2 + distance, chips)
    flag = target < 0
    for chip, own_core in CHANGED:
        flag = flag | ((target == chip) & (core == own_core))
    return flag


def is_home():
    return (lax.axis_index("lay") == 0) & (lax.axis_index("blk") % 2 == 1)


PAIRS = ((0, 2), (0, 3), (1, 2), (1, 4))


def unfold(mine_ref, other_ref, near_ref, cross_ref, spec):
    home = is_home()
    size = mine_ref.shape[0]
    mine = mine_ref[...].astype(jnp.float32)
    other = other_ref[...].astype(jnp.float32)
    near = near_ref[...].astype(jnp.float32)
    cross = cross_ref[...].astype(jnp.float32)
    spec[0 * size : 1 * size, :] = mine
    spec[1 * size : 2 * size, :] = other
    spec[2 * size : 3 * size, :] = jnp.where(home, mine, near)
    spec[3 * size : 4 * size, :] = cross
    spec[4 * size : 5 * size, :] = jnp.where(home, other, cross)


def spectrum(spec, stations, windows, chunks, block, window):
    rows = []
    for part in range(2):
        rows.append([])
        for station in range(stations):
            index = ((block * 2 + part) * stations + station) * windows + window
            rows[part].append(spec[index * chunks : (index + 1) * chunks, :])
    return rows


def edge_rows(table_ref, freq):
    half = table_ref.shape[1]
    edge = table_ref[2 * freq :, :].astype(jnp.float32)
    pieces = freq // half
    return [
        jnp.concatenate(
            [edge[row : row + 1] for row in range(part * pieces, (part + 1) * pieces)], axis=1
        )
        for part in range(2)
    ]


def lag_kernel(
    stations, windows, mine_ref, other_ref, near_ref, cross_ref, table_ref, lagged_ref, spec, rows
):
    freq = (table_ref.shape[0] - EDGE_ROWS) // 2
    chunks = freq // LANES
    pair_rows = stations * stations
    total = len(PAIRS) * pair_rows
    unfold(mine_ref, other_ref, near_ref, cross_ref, spec)
    for pair, (first, second) in enumerate(PAIRS):
        real = [[None] * stations for _ in range(stations)]
        imag = [[None] * stations for _ in range(stations)]
        for window in range(windows):
            u = spectrum(spec, stations, windows, chunks, first, window)
            v = spectrum(spec, stations, windows, chunks, second, window)
            for i in range(stations):
                for j in range(stations):
                    re = u[0][i] * v[0][j] + u[1][i] * v[1][j]
                    im = u[1][i] * v[0][j] - u[0][i] * v[1][j]
                    real[i][j] = re if window == 0 else real[i][j] + re
                    imag[i][j] = im if window == 0 else imag[i][j] + im
        for i in range(stations):
            for j in range(stations):
                row = pair * pair_rows + i * stations + j
                rows[row * chunks : (row + 1) * chunks, :] = real[i][j]
                row = row + total
                rows[row * chunks : (row + 1) * chunks, :] = imag[i][j]

    def left(part):
        return jnp.concatenate(
            [
                rows[pl.ds(part * total * chunks + chunk, total, stride=chunks), :].astype(
                    jnp.bfloat16
                )
                for chunk in range(chunks)
            ],
            axis=1,
        )

    half = table_ref.shape[1]
    tile = min(256, half)
    edges = edge_rows(table_ref, freq)
    real, imag = left(0), left(1)
    last_lag = jnp.sum(
        real.astype(jnp.float32) * edges[0] + imag.astype(jnp.float32) * edges[1],
        axis=1,
        keepdims=True,
    )
    first_lane = lax.broadcasted_iota(jnp.int32, (total, tile), 1) == 0
    for place in range(half // tile):
        span = slice(place * tile, (place + 1) * tile)
        even = jnp.dot(real, table_ref[:freq, span], preferred_element_type=jnp.float32)
        odd = jnp.dot(imag, table_ref[freq : 2 * freq, span], preferred_element_type=jnp.float32)
        lagged_ref[:, span] = even + odd
        value = even - odd
        if place == 0:
            value = jnp.where(first_lane, last_lag, value)
        lagged_ref[:, half + place * tile : half + (place + 1) * tile] = value


def response_kernel(
    layers,
    stations,
    windows,
    lagged_ref,
    mine_ref,
    other_ref,
    near_ref,
    cross_ref,
    model_near_ref,
    model_last_ref,
    model_moved_ref,
    model_pass_ref,
    table_ref,
    *rest,
):
    far_refs = rest[:layers]
    resp_rows, home_sums, spec, sums = rest[layers:]
    freq = (table_ref.shape[0] - EDGE_ROWS) // 2
    chunks = freq // LANES
    pair_rows = stations * stations
    total = len(PAIRS) * pair_rows
    block_rows = 2 * stations * windows
    size = block_rows * chunks
    core = lax.axis_index("blk") % 2
    home = is_home()
    half = table_ref.shape[1]
    tile = min(256, half)
    edges = edge_rows(table_ref, freq)
    misfit = []
    for place in range(2 * half // tile):
        span = slice(place * tile, (place + 1) * tile)
        last = jnp.where(
            core == 0,
            model_last_ref[:, span].astype(jnp.float32),
            model_moved_ref[:, span].astype(jnp.float32),
        )
        model = jnp.concatenate(
            [
                model_near_ref[:, span].astype(jnp.float32),
                last,
                model_pass_ref[:, span].astype(jnp.float32),
            ],
            axis=0,
        )
        value = jnp.where(model == OUTSIDE, 0.0, lagged_ref[:, span] - model)
        misfit.append(value.astype(jnp.bfloat16))
    count = half // tile
    first_lane = lax.broadcasted_iota(jnp.int32, (total, tile), 1) == 0
    first_behind = misfit[count].astype(jnp.float32)
    last_lag = first_behind[:, :1]
    misfit[count] = jnp.where(first_lane, 0.0, first_behind).astype(jnp.bfloat16)
    stacked = jnp.concatenate(
        [jnp.concatenate(misfit[:count], axis=1), jnp.concatenate(misfit[count:], axis=1)], axis=0
    )
    per_tile = tile // LANES
    for place in range(2 * chunks // per_tile):
        part, chunk = divmod(place * per_tile, chunks)
        low = chunk * LANES
        if low + tile <= half:
            table = table_ref[part * freq : part * freq + half, low : low + tile]
            product = jnp.dot(stacked, table, preferred_element_type=jnp.float32)
        else:
            product = lax.dot_general(
                stacked,
                table_ref[place * tile : (place + 1) * tile, :],
                (((1,), (1,)), ((), ())),
                preferred_element_type=jnp.float32,
            )
        weights = edges[part][:, chunk * LANES : chunk * LANES + tile]
        if part == 0:
            response = product[:total] + product[total:]
        else:
            response = product[:total] - product[total:]
        response = (response + last_lag * weights).astype(jnp.bfloat16).astype(jnp.float32)
        for inner in range(per_tile):
            start = part * total * chunks + chunk + inner
            resp_rows[pl.ds(start, total, stride=chunks), :] = response[
                :, inner * LANES : (inner + 1) * LANES
            ]

    unfold(mine_ref, other_ref, near_ref, cross_ref, spec)
    written = set()
    for pair, (first, second) in enumerate(PAIRS):
        r = response_rows(resp_rows, pair, pair_rows, total, chunks)
        for window in range(windows):
            u = spectrum(spec, stations, windows, chunks, first, window)
            for j in range(stations):
                terms_re, terms_im = [], []
                for i in range(stations):
                    re, im = r[0][i * stations + j], r[1][i * stations + j]
                    terms_re.append(re * u[0][i] + im * u[1][i])
                    terms_im.append(re * u[1][i] - im * u[0][i])
                for part, terms in enumerate((terms_re, terms_im)):
                    index = (((second - 2) * 2 + part) * stations + j) * windows + window
                    accumulate(sums, written, index, chunks, terms)
    part_near = sums[:size, :]
    part_last = sums[2 * size :, :]
    home_sums[:size, :] = jnp.where(home, part_near, 0.0)
    home_sums[size:, :] = jnp.where(home, part_last, 0.0)
    sums[:size, :] = jnp.where(home, 0.0, part_near)
    sums[size : 2 * size, :] += jnp.where(home, 0.0, part_last)
    for place in range(layers):
        step = jnp.where(changed(), 1 - place, place) if place < 2 <= layers else place
        write_share(sums, far_refs[place], step, layers, 2 * block_rows, chunks)


def own_kernel(
    stations,
    windows,
    resp_rows,
    home_sums,
    mine_ref,
    other_ref,
    near_ref,
    cross_ref,
    own_ref,
    pass_ref,
    spec,
    sums,
):
    block_rows = 2 * stations * windows
    chunks = mine_ref.shape[0] // block_rows
    pair_rows = stations * stations
    total = len(PAIRS) * pair_rows
    unfold(mine_ref, other_ref, near_ref, cross_ref, spec)
    sums[...] = home_sums[...]
    written = set(range(2 * block_rows))
    for pair, (first, second) in enumerate(PAIRS):
        r = response_rows(resp_rows, pair, pair_rows, total, chunks)
        for window in range(windows):
            v = spectrum(spec, stations, windows, chunks, second, window)
            for i in range(stations):
                terms_re, terms_im = [], []
                for j in range(stations):
                    re, im = r[0][i * stations + j], r[1][i * stations + j]
                    terms_re.append(re * v[0][j] - im * v[1][j])
                    terms_im.append(re * v[1][j] + im * v[0][j])
                for part, terms in enumerate((terms_re, terms_im)):
                    index = ((first * 2 + part) * stations + i) * windows + window
                    accumulate(sums, written, index, chunks, terms)
    for chunk in range(chunks):
        span = slice(chunk * LANES, (chunk + 1) * LANES)
        own_ref[:, span] = sums[pl.ds(chunk, block_rows, stride=chunks), :]
        passed = sums[pl.ds(block_rows * chunks + chunk, block_rows, stride=chunks), :]
        pass_ref[:, span] = passed.astype(pass_ref.dtype)


def share_kernel(layers, own_ref, pass_ref, *out_refs):
    width = own_ref.shape[1] // layers
    for step, out_ref in enumerate(out_refs):
        start = lax.rem(lax.axis_index("lay") + step, layers) * width
        span = pl.ds(pl.multiple_of(start, LANES), width)
        total = own_ref[:, span] + pass_ref[:, span].astype(jnp.float32)
        out_ref[...] = total.astype(out_ref.dtype)


def response_rows(resp_rows, pair, pair_rows, total, chunks):
    rows = []
    for part in range(2):
        base = part * total + pair * pair_rows
        rows.append(
            [
                resp_rows[(base + row) * chunks : (base + row + 1) * chunks, :]
                for row in range(pair_rows)
            ]
        )
    return rows


def accumulate(sums, written, index, chunks, terms):
    rows = slice(index * chunks, (index + 1) * chunks)
    value = sum(terms[1:], terms[0])
    if index in written:
        value = value + sums[rows, :]
    written.add(index)
    sums[rows, :] = value


def write_share(sums, target, step, layers, count, chunks):
    width = chunks // layers
    start = lax.rem(lax.axis_index("lay") + step, layers) * width
    for inner in range(width):
        values = sums[pl.ds(start + inner, count, stride=chunks), :]
        target[:, inner * LANES : (inner + 1) * LANES] = values.astype(target.dtype)


def add_kernel(*refs):
    keep_ref, send_ref = refs[-2:]
    total = refs[0][...].astype(jnp.float32)
    for ref in refs[1:-2]:
        total = total + ref[...].astype(jnp.float32)
    half = keep_ref.shape[0]
    keep_ref[...] = total[:half]
    send_ref[...] = total[half:]


def gather_kernel(keep_ref, send_ref, *refs):
    total_ref, out_ref = refs[-2:]
    total = keep_ref[...]
    for ref in refs[:-2]:
        total = total + ref[...].astype(jnp.float32)
    total_ref[...] = total
    out_ref[...] = send_ref[...]


def place_kernel(scale, placing_ref, *refs):
    out_ref = refs[-1]
    parts, stations, windows, _ = out_ref.shape
    total = refs[0][...]
    for ref in refs[1:-1]:
        total = total + ref[...].astype(jnp.float32)
    total = total * scale
    for station in range(stations):
        here = [
            placing_ref[row : row + 1, :]
            for row in range(station, stations * stations, stations)
        ]
        for part in range(parts):
            value = None
            for place in range(stations):
                base = (part * stations + place) * windows
                term = here[place] * total[base : base + windows, :]
                value = term if value is None else value + term
            out_ref[part, station] = value


VMEM = pl.BlockSpec(memory_space=pltpu.VMEM)
HBM = pl.BlockSpec(memory_space=pltpu.HBM)


def grant(mebibytes):
    return pltpu.CompilerParams(vmem_limit_bytes=mebibytes * 1024 * 1024)


def local(spectra, model_corr, window_start, window_end, station_slot):
    _, stations, windows, freq = spectra.shape
    lags = model_corr.shape[4]
    layers = lax.axis_size("lay")
    blocks = lax.axis_size("blk")
    chips = blocks // 2
    chunks = freq // LANES
    pair_rows = stations * stations
    block_rows = 2 * stations * windows
    f32, bf16 = jnp.float32, jnp.bfloat16

    def distance(layer, core):
        if core == 0:
            return 2 * layer + 1
        return 2 * layer if layer > 0 else 2 * layers

    def move(value, target):
        pairs = []
        for block in range(blocks):
            for layer in range(layers):
                chip, core, to_layer = target(block // 2, block % 2, layer)
                pairs.append(
                    (block * layers + layer, (chip % chips * 2 + core) * layers + to_layer % layers)
                )
        return lax.ppermute(value, AXES, pairs)

    def swap_cores(value):
        return move(value, lambda chip, core, layer: (chip, 1 - core, layer))

    station_slot, spectra = (
        pltpu.with_memory_space_constraint(value, pltpu.HBM) for value in (station_slot, spectra)
    )
    mine, placing = pl.pallas_call(
        order_kernel,
        out_shape=[
            jax.ShapeDtypeStruct((block_rows * chunks, LANES), bf16),
            jax.ShapeDtypeStruct((stations * stations, freq // layers), f32),
        ],
        in_specs=[HBM] * 2,
        out_specs=[VMEM] * 2,
        scratch_shapes=[
            pltpu.SMEM(station_slot.shape, jnp.int32),
            pltpu.VMEM(spectra.shape, bf16),
            pltpu.VMEM((block_rows * chunks, LANES), f32),
            pltpu.SemaphoreType.DMA((2,)),
        ],
        compiler_params=grant(2),
        cost_estimate=pl.CostEstimate(flops=5 * 10**9, bytes_accessed=10**6, transcendentals=0),
        name="order",
    )(station_slot, spectra)
    cross = move(mine, lambda chip, core, layer: (chip - distance(layer, 1 - core), 1 - core, layer))
    def near_target(chip, core, layer):
        if (core, chip) in [] and layer < 2:
            layer = 1 - layer
        if layer == 0 and core == 1:
            return chip ^ 1, core, layer
        return chip - distance(layer, core), core, layer

    near = move(
        mine,
        near_target,
    )
    other = swap_cores(mine)
    model_near, model_last, model_pass = pl.pallas_call(
        mask_kernel,
        out_shape=[
            jax.ShapeDtypeStruct((pair_rows, lags), bf16),
            jax.ShapeDtypeStruct((pair_rows, lags), bf16),
            jax.ShapeDtypeStruct((2 * pair_rows, lags), bf16),
        ],
        in_specs=[VMEM] * 3,
        out_specs=[VMEM] * 3,
        scratch_shapes=[pltpu.VMEM((pair_rows, lags), f32)],
        compiler_params=grant(4),
        cost_estimate=pl.CostEstimate(flops=5 * 10**9, bytes_accessed=10**6, transcendentals=0),
        name="mask",
    )(window_start, window_end, model_corr)
    model_pass = swap_cores(model_pass)
    model_moved = move(model_last, lambda chip, core, layer: (chip, core, layer + 1))
    table = lag_table(freq, lags, windows)
    total = 4 * pair_rows
    blocks_in = (mine, other, near, cross)
    spec = pltpu.VMEM((5 * block_rows * chunks, LANES), f32)
    lagged = pl.pallas_call(
        functools.partial(lag_kernel, stations, windows),
        out_shape=jax.ShapeDtypeStruct((total, lags), f32),
        in_specs=[VMEM] * 5,
        out_specs=VMEM,
        scratch_shapes=[spec, pltpu.VMEM((2 * total * chunks, LANES), f32)],
        compiler_params=grant(8),
        name="lag",
    )(*blocks_in, table)
    part = (2 * block_rows, freq // layers)
    outs = pl.pallas_call(
        functools.partial(response_kernel, layers, stations, windows),
        out_shape=[jax.ShapeDtypeStruct(part, bf16)] * layers
        + [
            jax.ShapeDtypeStruct((2 * total * chunks, LANES), f32),
            jax.ShapeDtypeStruct((2 * block_rows * chunks, LANES), f32),
        ],
        in_specs=[VMEM] * 10,
        out_specs=[VMEM] * (layers + 2),
        scratch_shapes=[spec, pltpu.VMEM((3 * block_rows * chunks, LANES), f32)],
        compiler_params=grant(12),
        name="response",
    )(lagged, *blocks_in, model_near, model_last, model_moved, model_pass, table)
    def returned(place):
        def target(chip, core, layer):
            chip = (chip + distance(layer, core)) % chips
            step = 1 - place if (chip, core) in CHANGED and place < 2 <= layers else place
            return chip, core, layer + step

        return target

    parts = [move(outs[place], returned(place)) for place in range(layers)]
    whole = (block_rows, freq)
    own, passed = pl.pallas_call(
        functools.partial(own_kernel, stations, windows),
        out_shape=[jax.ShapeDtypeStruct(whole, f32), jax.ShapeDtypeStruct(whole, bf16)],
        in_specs=[VMEM] * 6,
        out_specs=[VMEM] * 2,
        scratch_shapes=[spec, pltpu.VMEM((2 * block_rows * chunks, LANES), f32)],
        compiler_params=grant(8),
        name="own",
    )(outs[layers], outs[layers + 1], *blocks_in)
    share = (block_rows, freq // layers)
    own = pl.pallas_call(
        functools.partial(share_kernel, layers),
        out_shape=[jax.ShapeDtypeStruct(share, f32)]
        + [jax.ShapeDtypeStruct(share, bf16)] * (layers - 1),
        in_specs=[VMEM] * 2,
        out_specs=[VMEM] * layers,
        compiler_params=grant(2),
        name="share",
    )(own, swap_cores(passed))
    own = [own[0]] + [
        move(own[step], lambda chip, core, layer: (chip, core, layer + step))
        for step in range(1, layers)
    ]
    firsts = list(range(min(2, layers) - 1, -1, -1)) + list(range(2, layers))
    keep, send = pl.pallas_call(
        add_kernel,
        out_shape=[jax.ShapeDtypeStruct(share, f32)] * 2,
        in_specs=[VMEM] * layers,
        out_specs=[VMEM] * 2,
        compiler_params=grant(2),
        name="arrived",
    )(*[parts[place] for place in firsts])
    keep, send = pl.pallas_call(
        gather_kernel,
        out_shape=[jax.ShapeDtypeStruct(share, f32)] * 2,
        in_specs=[VMEM] * (2 + layers),
        out_specs=[VMEM] * 2,
        compiler_params=grant(2),
        name="gather",
    )(keep, send, *own)
    return pl.pallas_call(
        functools.partial(place_kernel, 1.0 / math.sqrt(blocks * stations)),
        out_shape=jax.ShapeDtypeStruct((2, stations, windows, freq // layers), f32),
        in_specs=[VMEM] * 3,
        out_specs=VMEM,
        compiler_params=grant(2),
        name="place",
    )(placing, keep, swap_cores(send))


def solution(mesh):
    in_specs = (
        P(None, "blk", None, None),
        P("blk", "lay", None, None, None),
        P("blk", "lay"),
        P("blk", "lay"),
        P("blk", None),
    )
    out_specs = P(None, "blk", None, "lay")
    return jax.shard_map(local, mesh=mesh, in_specs=in_specs, out_specs=out_specs, check_vma=False)
```

```python
import functools
import math

import jax
import jax.numpy as jnp
import ml_dtypes
import numpy as np
from jax import lax
from jax.experimental import pallas as pl
from jax.experimental.pallas import tpu as pltpu
from jax.sharding import PartitionSpec as P


LANES = 128
AXES = ("blk", "lay")
EDGE_ROWS = 64
PIECES = 4
CHANGED = ((1, 0),)
OUTSIDE = 2.0**100


def lag_table(freq_count, lag_count, window_count):
    half = lag_count // 2
    freq_index = np.arange(freq_count, dtype=np.int64)
    lag_index = np.arange(half + 1, dtype=np.int64)
    phase_index = freq_index[:, None] * lag_index[None, :] % (2 * freq_count)
    angle = phase_index.astype(np.float64) * (math.pi / freq_count)
    factor = 1.0 / math.sqrt(2.0 * freq_count * window_count)
    cosine, sine = np.cos(angle) * factor, -np.sin(angle) * factor
    edge = np.concatenate([cosine[:, half], -sine[:, half]]).reshape(-1, half)
    padding = np.zeros((EDGE_ROWS - edge.shape[0], half))
    table = np.concatenate([cosine[:, :half], sine[:, :half], edge, padding])
    return jnp.asarray(table.astype(ml_dtypes.bfloat16))


def copies(sources, targets, arrived):
    moves = [
        pltpu.make_async_copy(source, target, arrived.at[place])
        for place, (source, target) in enumerate(zip(sources, targets))
    ]
    for copy in moves:
        copy.start()
    return moves


def order_kernel(slot_ref, spectra_ref, mine_ref, placing_ref, slot, spectra, spread, arrived):
    moves = copies((slot_ref, spectra_ref), (slot, spectra), arrived)
    parts, stations, windows, freq = spectra.shape
    chunks = freq // LANES
    moves[0].wait()
    for place in range(stations):
        for station in range(stations):
            row = place * stations + station
            here = (slot[0, place] == station).astype(jnp.float32)
            placing_ref[row : row + 1, :] = jnp.full((1, placing_ref.shape[1]), here, jnp.float32)
    moves[1].wait()
    for part in range(parts):
        for place in range(stations):
            values = spectra[part, slot[0, place]].astype(jnp.float32)
            base = (part * stations + place) * windows * chunks
            for chunk in range(chunks):
                spread[pl.ds(base + chunk, windows, stride=chunks), :] = values[
                    :, chunk * LANES : (chunk + 1) * LANES
                ]
    mine_ref[...] = spread[...].astype(jnp.bfloat16)


def mask_kernel(start_ref, end_ref, model_ref, near_ref, last_ref, pass_ref, rows):
    core = lax.axis_index("blk") % 2
    layer = lax.axis_index("lay")
    stations, lags = model_ref.shape[3:]
    half = lags // 2
    before = lax.broadcasted_iota(jnp.int32, (half, half), 0)
    after = lax.broadcasted_iota(jnp.int32, (half, half), 1)
    turn = (before + after == half) | (before + after == 0)
    turn = jnp.where(turn, 1.0, 0.0).astype(jnp.bfloat16)
    count = stations * stations
    lag = lax.broadcasted_iota(jnp.int32, (count, lags), 1)
    row = lax.broadcasted_iota(jnp.int32, (count, lags), 0)
    diagonal = row % (stations + 1) == 0
    start, end = start_ref[...], end_ref[...]
    values = []
    for offset in range(4):
        for first in range(stations):
            rows[first * stations : (first + 1) * stations, :] = model_ref[0, offset, first].astype(
                jnp.float32
            )
        keep = (lag >= start[:, offset : offset + 1]) & (lag < end[:, offset : offset + 1])
        if offset == 0:
            keep = keep & jnp.logical_not(diagonal & (layer == 0))
        values.append(jnp.where(keep, rows[...], OUTSIDE))
    even = core == 0
    values = jnp.concatenate(
        [
            jnp.where(even, values[2], values[0]),
            values[3],
            values[1],
            jnp.where(even, values[0], values[2]),
        ],
        axis=0,
    ).astype(jnp.bfloat16)
    turned = jnp.dot(values[:, :half], turn, preferred_element_type=jnp.float32)
    values = jnp.concatenate([values[:, half:], turned.astype(jnp.bfloat16)], axis=1)
    near_ref[...] = values[:count]
    last_ref[...] = values[count : 2 * count]
    pass_ref[...] = values[2 * count :]


def changed():
    chips = lax.axis_size("blk") // 2
    layers = lax.axis_size("lay")
    core, layer = lax.axis_index("blk") % 2, lax.axis_index("lay")
    distance = jnp.where(core == 0, 2 * layer + 1, jnp.where(layer > 0, 2 * layer, 2 * layers))
    target = lax.rem(lax.axis_index("blk") // 2 + distance, chips)
    flag = target < 0
    for chip, own_core in CHANGED:
        flag = flag | ((target == chip) & (core == own_core))
    return flag


def is_home():
    return (lax.axis_index("lay") == 0) & (lax.axis_index("blk") % 2 == 1)


PAIRS = ((0, 2), (0, 3), (1, 2), (1, 4))


def unfold(mine_ref, other_ref, near_ref, cross_ref, spec):
    home = is_home()
    size = mine_ref.shape[0]
    mine = mine_ref[...].astype(jnp.float32)
    other = other_ref[...].astype(jnp.float32)
    near = near_ref[...].astype(jnp.float32)
    cross = cross_ref[...].astype(jnp.float32)
    spec[0 * size : 1 * size, :] = mine
    spec[1 * size : 2 * size, :] = other
    spec[2 * size : 3 * size, :] = jnp.where(home, mine, near)
    spec[3 * size : 4 * size, :] = cross
    spec[4 * size : 5 * size, :] = jnp.where(home, other, cross)


def spectrum(spec, stations, windows, chunks, block, window):
    rows = []
    for part in range(2):
        rows.append([])
        for station in range(stations):
            index = ((block * 2 + part) * stations + station) * windows + window
            rows[part].append(spec[index * chunks : (index + 1) * chunks, :])
    return rows


def edge_rows(table_ref, freq):
    half = table_ref.shape[1]
    edge = table_ref[2 * freq :, :].astype(jnp.float32)
    pieces = freq // half
    return [
        jnp.concatenate(
            [edge[row : row + 1] for row in range(part * pieces, (part + 1) * pieces)], axis=1
        )
        for part in range(2)
    ]


def lag_kernel(
    stations, windows, mine_ref, other_ref, near_ref, cross_ref, table_ref, lagged_ref, spec, rows
):
    freq = (table_ref.shape[0] - EDGE_ROWS) // 2
    chunks = freq // LANES
    pair_rows = stations * stations
    total = len(PAIRS) * pair_rows
    unfold(mine_ref, other_ref, near_ref, cross_ref, spec)
    for pair, (first, second) in enumerate(PAIRS):
        real = [[None] * stations for _ in range(stations)]
        imag = [[None] * stations for _ in range(stations)]
        for window in range(windows):
            u = spectrum(spec, stations, windows, chunks, first, window)
            v = spectrum(spec, stations, windows, chunks, second, window)
            for i in range(stations):
                for j in range(stations):
                    re = u[0][i] * v[0][j] + u[1][i] * v[1][j]
                    im = u[1][i] * v[0][j] - u[0][i] * v[1][j]
                    real[i][j] = re if window == 0 else real[i][j] + re
                    imag[i][j] = im if window == 0 else imag[i][j] + im
        for i in range(stations):
            for j in range(stations):
                row = pair * pair_rows + i * stations + j
                rows[row * chunks : (row + 1) * chunks, :] = real[i][j]
                row = row + total
                rows[row * chunks : (row + 1) * chunks, :] = imag[i][j]

    def left(part):
        return jnp.concatenate(
            [
                rows[pl.ds(part * total * chunks + chunk, total, stride=chunks), :].astype(
                    jnp.bfloat16
                )
                for chunk in range(chunks)
            ],
            axis=1,
        )

    half = table_ref.shape[1]
    tile = min(256, half)
    edges = edge_rows(table_ref, freq)
    real, imag = left(0), left(1)
    last_lag = jnp.sum(
        real.astype(jnp.float32) * edges[0] + imag.astype(jnp.float32) * edges[1],
        axis=1,
        keepdims=True,
    )
    first_lane = lax.broadcasted_iota(jnp.int32, (total, tile), 1) == 0
    for place in range(half // tile):
        span = slice(place * tile, (place + 1) * tile)
        even = jnp.dot(real, table_ref[:freq, span], preferred_element_type=jnp.float32)
        odd = jnp.dot(imag, table_ref[freq : 2 * freq, span], preferred_element_type=jnp.float32)
        lagged_ref[:, span] = even + odd
        value = even - odd
        if place == 0:
            value = jnp.where(first_lane, last_lag, value)
        lagged_ref[:, half + place * tile : half + (place + 1) * tile] = value


def response_kernel(
    layers,
    stations,
    windows,
    lagged_ref,
    mine_ref,
    other_ref,
    near_ref,
    cross_ref,
    model_near_ref,
    model_last_ref,
    model_moved_ref,
    model_pass_ref,
    table_ref,
    *rest,
):
    far_refs = rest[:layers]
    resp_rows, home_sums, pass_ref, spec, sums, passed = rest[layers:]
    freq = (table_ref.shape[0] - EDGE_ROWS) // 2
    chunks = freq // LANES
    pair_rows = stations * stations
    total = len(PAIRS) * pair_rows
    block_rows = 2 * stations * windows
    size = block_rows * chunks
    core = lax.axis_index("blk") % 2
    home = is_home()
    half = table_ref.shape[1]
    tile = min(256, half)
    edges = edge_rows(table_ref, freq)
    misfit = []
    for place in range(2 * half // tile):
        span = slice(place * tile, (place + 1) * tile)
        last = jnp.where(
            core == 0,
            model_last_ref[:, span].astype(jnp.float32),
            model_moved_ref[:, span].astype(jnp.float32),
        )
        model = jnp.concatenate(
            [
                model_near_ref[:, span].astype(jnp.float32),
                last,
                model_pass_ref[:, span].astype(jnp.float32),
            ],
            axis=0,
        )
        value = jnp.where(model == OUTSIDE, 0.0, lagged_ref[:, span] - model)
        misfit.append(value.astype(jnp.bfloat16))
    count = half // tile
    first_lane = lax.broadcasted_iota(jnp.int32, (total, tile), 1) == 0
    first_behind = misfit[count].astype(jnp.float32)
    last_lag = first_behind[:, :1]
    misfit[count] = jnp.where(first_lane, 0.0, first_behind).astype(jnp.bfloat16)
    stacked = jnp.concatenate(
        [jnp.concatenate(misfit[:count], axis=1), jnp.concatenate(misfit[count:], axis=1)], axis=0
    )
    per_tile = tile // LANES
    for place in range(2 * chunks // per_tile):
        part, chunk = divmod(place * per_tile, chunks)
        low = chunk * LANES
        if low + tile <= half:
            table = table_ref[part * freq : part * freq + half, low : low + tile]
            product = jnp.dot(stacked, table, preferred_element_type=jnp.float32)
        else:
            product = lax.dot_general(
                stacked,
                table_ref[place * tile : (place + 1) * tile, :],
                (((1,), (1,)), ((), ())),
                preferred_element_type=jnp.float32,
            )
        weights = edges[part][:, chunk * LANES : chunk * LANES + tile]
        if part == 0:
            response = product[:total] + product[total:]
        else:
            response = product[:total] - product[total:]
        response = (response + last_lag * weights).astype(jnp.bfloat16).astype(jnp.float32)
        for inner in range(per_tile):
            start = part * total * chunks + chunk + inner
            resp_rows[pl.ds(start, total, stride=chunks), :] = response[
                :, inner * LANES : (inner + 1) * LANES
            ]

    unfold(mine_ref, other_ref, near_ref, cross_ref, spec)
    written = set()
    for pair, (first, second) in enumerate(PAIRS):
        r = response_rows(resp_rows, pair, pair_rows, total, chunks)
        for window in range(windows):
            u = spectrum(spec, stations, windows, chunks, first, window)
            for j in range(stations):
                terms_re, terms_im = [], []
                for i in range(stations):
                    re, im = r[0][i * stations + j], r[1][i * stations + j]
                    terms_re.append(re * u[0][i] + im * u[1][i])
                    terms_im.append(re * u[1][i] - im * u[0][i])
                for part, terms in enumerate((terms_re, terms_im)):
                    index = (((second - 2) * 2 + part) * stations + j) * windows + window
                    accumulate(sums, written, index, chunks, terms)
    part_near = sums[:size, :]
    part_last = sums[2 * size :, :]
    home_sums[...] = jnp.where(home, part_near, 0.0)
    passed[...] = jnp.where(home, part_last, 0.0)
    sums[:size, :] = jnp.where(home, 0.0, part_near)
    sums[size : 2 * size, :] += jnp.where(home, 0.0, part_last)
    for place in range(layers):
        step = jnp.where(changed(), 1 - place, place) if place < 2 <= layers else place
        write_share(sums, far_refs[place], step, layers, 2 * block_rows, chunks)

    add_own_terms(1, resp_rows, spec, passed, stations, windows, chunks)
    write_whole(passed, pass_ref, block_rows, chunks)


def own_kernel(
    stations,
    windows,
    resp_rows,
    home_sums,
    mine_ref,
    other_ref,
    near_ref,
    cross_ref,
    own_ref,
    spec,
    sums,
):
    block_rows = 2 * stations * windows
    chunks = mine_ref.shape[0] // block_rows
    unfold(mine_ref, other_ref, near_ref, cross_ref, spec)
    sums[...] = home_sums[...]
    add_own_terms(0, resp_rows, spec, sums, stations, windows, chunks)
    write_whole(sums, own_ref, block_rows, chunks)


def add_own_terms(block, resp_rows, spec, sums, stations, windows, chunks):
    pair_rows = stations * stations
    total = len(PAIRS) * pair_rows
    written = set(range(2 * stations * windows))
    for pair, (first, second) in enumerate(PAIRS):
        if first != block:
            continue
        r = response_rows(resp_rows, pair, pair_rows, total, chunks)
        for window in range(windows):
            v = spectrum(spec, stations, windows, chunks, second, window)
            for i in range(stations):
                terms_re, terms_im = [], []
                for j in range(stations):
                    re, im = r[0][i * stations + j], r[1][i * stations + j]
                    terms_re.append(re * v[0][j] - im * v[1][j])
                    terms_im.append(re * v[1][j] + im * v[0][j])
                for part, terms in enumerate((terms_re, terms_im)):
                    index = (part * stations + i) * windows + window
                    accumulate(sums, written, index, chunks, terms)


def write_whole(sums, target, count, chunks):
    for chunk in range(chunks):
        values = sums[pl.ds(chunk, count, stride=chunks), :]
        target[:, chunk * LANES : (chunk + 1) * LANES] = values.astype(target.dtype)


def share_kernel(layers, own_ref, pass_ref, *out_refs):
    width = own_ref.shape[1] // layers
    for step, out_ref in enumerate(out_refs):
        start = lax.rem(lax.axis_index("lay") + step, layers) * width
        span = pl.ds(pl.multiple_of(start, LANES), width)
        total = own_ref[:, span] + pass_ref[:, span].astype(jnp.float32)
        out_ref[...] = total.astype(out_ref.dtype)


def response_rows(resp_rows, pair, pair_rows, total, chunks):
    rows = []
    for part in range(2):
        base = part * total + pair * pair_rows
        rows.append(
            [
                resp_rows[(base + row) * chunks : (base + row + 1) * chunks, :]
                for row in range(pair_rows)
            ]
        )
    return rows


def accumulate(sums, written, index, chunks, terms):
    rows = slice(index * chunks, (index + 1) * chunks)
    value = sum(terms[1:], terms[0])
    if index in written:
        value = value + sums[rows, :]
    written.add(index)
    sums[rows, :] = value


def write_share(sums, target, step, layers, count, chunks):
    width = chunks // layers
    start = lax.rem(lax.axis_index("lay") + step, layers) * width
    for inner in range(width):
        values = sums[pl.ds(start + inner, count, stride=chunks), :]
        target[:, inner * LANES : (inner + 1) * LANES] = values.astype(target.dtype)


def add_kernel(*refs):
    keep_ref, send_ref = refs[-2:]
    total = refs[0][...].astype(jnp.float32)
    for ref in refs[1:-2]:
        total = total + ref[...].astype(jnp.float32)
    half = keep_ref.shape[0]
    keep_ref[...] = total[:half]
    send_ref[...] = total[half:]


def gather_kernel(keep_ref, send_ref, *refs):
    total_ref, out_ref = refs[-2:]
    total = keep_ref[...]
    for ref in refs[:-2]:
        total = total + ref[...].astype(jnp.float32)
    total_ref[...] = total
    out_ref[...] = send_ref[...]


def place_kernel(scale, placing_ref, *refs):
    out_ref = refs[-1]
    parts, stations, windows, _ = out_ref.shape
    total = refs[0][...]
    for ref in refs[1:-1]:
        total = total + ref[...].astype(jnp.float32)
    total = total * scale
    for station in range(stations):
        here = [
            placing_ref[row : row + 1, :]
            for row in range(station, stations * stations, stations)
        ]
        for part in range(parts):
            value = None
            for place in range(stations):
                base = (part * stations + place) * windows
                term = here[place] * total[base : base + windows, :]
                value = term if value is None else value + term
            out_ref[part, station] = value


VMEM = pl.BlockSpec(memory_space=pltpu.VMEM)
HBM = pl.BlockSpec(memory_space=pltpu.HBM)


def grant(mebibytes):
    return pltpu.CompilerParams(vmem_limit_bytes=mebibytes * 1024 * 1024)


def local(spectra, model_corr, window_start, window_end, station_slot):
    _, stations, windows, freq = spectra.shape
    lags = model_corr.shape[4]
    layers = lax.axis_size("lay")
    blocks = lax.axis_size("blk")
    chips = blocks // 2
    chunks = freq // LANES
    pair_rows = stations * stations
    block_rows = 2 * stations * windows
    f32, bf16 = jnp.float32, jnp.bfloat16

    def distance(layer, core):
        if core == 0:
            return 2 * layer + 1
        return 2 * layer if layer > 0 else 2 * layers

    def move(value, target):
        pairs = []
        for block in range(blocks):
            for layer in range(layers):
                chip, core, to_layer = target(block // 2, block % 2, layer)
                pairs.append(
                    (block * layers + layer, (chip % chips * 2 + core) * layers + to_layer % layers)
                )
        return lax.ppermute(value, AXES, pairs)

    def swap_cores(value):
        return move(value, lambda chip, core, layer: (chip, 1 - core, layer))

    station_slot, spectra = (
        pltpu.with_memory_space_constraint(value, pltpu.HBM) for value in (station_slot, spectra)
    )
    mine, placing = pl.pallas_call(
        order_kernel,
        out_shape=[
            jax.ShapeDtypeStruct((block_rows * chunks, LANES), bf16),
            jax.ShapeDtypeStruct((stations * stations, freq // layers), f32),
        ],
        in_specs=[HBM] * 2,
        out_specs=[VMEM] * 2,
        scratch_shapes=[
            pltpu.SMEM(station_slot.shape, jnp.int32),
            pltpu.VMEM(spectra.shape, bf16),
            pltpu.VMEM((block_rows * chunks, LANES), f32),
            pltpu.SemaphoreType.DMA((2,)),
        ],
        compiler_params=grant(2),
        cost_estimate=pl.CostEstimate(flops=5 * 10**9, bytes_accessed=10**6, transcendentals=0),
        name="order",
    )(station_slot, spectra)
    cross = move(mine, lambda chip, core, layer: (chip - distance(layer, 1 - core), 1 - core, layer))
    def near_target(chip, core, layer):
        if (core, chip) in [] and layer < 2:
            layer = 1 - layer
        if layer == 0 and core == 1:
            return chip ^ 1, core, layer
        return chip - distance(layer, core), core, layer

    near = move(
        mine,
        near_target,
    )
    other = swap_cores(mine)
    model_near, model_last, model_pass = pl.pallas_call(
        mask_kernel,
        out_shape=[
            jax.ShapeDtypeStruct((pair_rows, lags), bf16),
            jax.ShapeDtypeStruct((pair_rows, lags), bf16),
            jax.ShapeDtypeStruct((2 * pair_rows, lags), bf16),
        ],
        in_specs=[VMEM] * 3,
        out_specs=[VMEM] * 3,
        scratch_shapes=[pltpu.VMEM((pair_rows, lags), f32)],
        compiler_params=grant(4),
        cost_estimate=pl.CostEstimate(flops=5 * 10**9, bytes_accessed=10**6, transcendentals=0),
        name="mask",
    )(window_start, window_end, model_corr)
    model_pass = swap_cores(model_pass)
    model_moved = move(model_last, lambda chip, core, layer: (chip, core, layer + 1))
    table = lag_table(freq, lags, windows)
    total = 4 * pair_rows
    blocks_in = (mine, other, near, cross)
    spec = pltpu.VMEM((5 * block_rows * chunks, LANES), f32)
    lagged = pl.pallas_call(
        functools.partial(lag_kernel, stations, windows),
        out_shape=jax.ShapeDtypeStruct((total, lags), f32),
        in_specs=[VMEM] * 5,
        out_specs=VMEM,
        scratch_shapes=[spec, pltpu.VMEM((2 * total * chunks, LANES), f32)],
        compiler_params=grant(8),
        name="lag",
    )(*blocks_in, table)
    part = (2 * block_rows, freq // layers)
    outs = pl.pallas_call(
        functools.partial(response_kernel, layers, stations, windows),
        out_shape=[jax.ShapeDtypeStruct(part, bf16)] * layers
        + [
            jax.ShapeDtypeStruct((2 * total * chunks, LANES), f32),
            jax.ShapeDtypeStruct((block_rows * chunks, LANES), f32),
            jax.ShapeDtypeStruct((block_rows, freq), bf16),
        ],
        in_specs=[VMEM] * 10,
        out_specs=[VMEM] * (layers + 3),
        scratch_shapes=[
            spec,
            pltpu.VMEM((3 * block_rows * chunks, LANES), f32),
            pltpu.VMEM((block_rows * chunks, LANES), f32),
        ],
        compiler_params=grant(12),
        name="response",
    )(lagged, *blocks_in, model_near, model_last, model_moved, model_pass, table)
    def returned(place):
        def target(chip, core, layer):
            chip = (chip + distance(layer, core)) % chips
            step = 1 - place if (chip, core) in CHANGED and place < 2 <= layers else place
            return chip, core, layer + step

        return target

    parts = [move(outs[place], returned(place)) for place in range(layers)]
    own = pl.pallas_call(
        functools.partial(own_kernel, stations, windows),
        out_shape=jax.ShapeDtypeStruct((block_rows, freq), f32),
        in_specs=[VMEM] * 6,
        out_specs=VMEM,
        scratch_shapes=[spec, pltpu.VMEM((block_rows * chunks, LANES), f32)],
        compiler_params=grant(8),
        name="own",
    )(outs[layers], outs[layers + 1], *blocks_in)
    share = (block_rows, freq // layers)
    own = pl.pallas_call(
        functools.partial(share_kernel, layers),
        out_shape=[jax.ShapeDtypeStruct(share, f32)]
        + [jax.ShapeDtypeStruct(share, bf16)] * (layers - 1),
        in_specs=[VMEM] * 2,
        out_specs=[VMEM] * layers,
        compiler_params=grant(2),
        name="share",
    )(own, swap_cores(outs[layers + 2]))
    own = [own[0]] + [
        move(own[step], lambda chip, core, layer: (chip, core, layer + step))
        for step in range(1, layers)
    ]
    firsts = list(range(min(2, layers) - 1, -1, -1)) + list(range(2, layers))
    keep, send = pl.pallas_call(
        add_kernel,
        out_shape=[jax.ShapeDtypeStruct(share, f32)] * 2,
        in_specs=[VMEM] * layers,
        out_specs=[VMEM] * 2,
        compiler_params=grant(2),
        name="arrived",
    )(*[parts[place] for place in firsts])
    keep, send = pl.pallas_call(
        gather_kernel,
        out_shape=[jax.ShapeDtypeStruct(share, f32)] * 2,
        in_specs=[VMEM] * (2 + layers),
        out_specs=[VMEM] * 2,
        compiler_params=grant(2),
        name="gather",
    )(keep, send, *own)
    return pl.pallas_call(
        functools.partial(place_kernel, 1.0 / math.sqrt(blocks * stations)),
        out_shape=jax.ShapeDtypeStruct((2, stations, windows, freq // layers), f32),
        in_specs=[VMEM] * 3,
        out_specs=VMEM,
        compiler_params=grant(2),
        name="place",
    )(placing, keep, swap_cores(send))


def solution(mesh):
    in_specs = (
        P(None, "blk", None, None),
        P("blk", "lay", None, None, None),
        P("blk", "lay"),
        P("blk", "lay"),
        P("blk", None),
    )
    out_specs = P(None, "blk", None, "lay")
    return jax.shard_map(local, mesh=mesh, in_specs=in_specs, out_specs=out_specs, check_vma=False)
```

```python
import functools
import math

import jax
import jax.numpy as jnp
import ml_dtypes
import numpy as np
from jax import lax
from jax.experimental import pallas as pl
from jax.experimental.pallas import tpu as pltpu
from jax.sharding import PartitionSpec as P


LANES = 128
AXES = ("blk", "lay")
EDGE_ROWS = 64
PIECES = 4
CHANGED = ((1, 0),)
OUTSIDE = 2.0**100


def lag_table(freq_count, lag_count, window_count):
    half = lag_count // 2
    freq_index = np.arange(freq_count, dtype=np.int64)
    lag_index = np.arange(half + 1, dtype=np.int64)
    phase_index = freq_index[:, None] * lag_index[None, :] % (2 * freq_count)
    angle = phase_index.astype(np.float64) * (math.pi / freq_count)
    factor = 1.0 / math.sqrt(2.0 * freq_count * window_count)
    cosine, sine = np.cos(angle) * factor, -np.sin(angle) * factor
    edge = np.concatenate([cosine[:, half], -sine[:, half]]).reshape(-1, half)
    padding = np.zeros((EDGE_ROWS - edge.shape[0], half))
    table = np.concatenate([cosine[:, :half], sine[:, :half], edge, padding])
    return jnp.asarray(table.astype(ml_dtypes.bfloat16))


def copies(sources, targets, arrived):
    moves = [
        pltpu.make_async_copy(source, target, arrived.at[place])
        for place, (source, target) in enumerate(zip(sources, targets))
    ]
    for copy in moves:
        copy.start()
    return moves


def order_kernel(slot_ref, spectra_ref, mine_ref, placing_ref, slot, spectra, spread, arrived):
    moves = copies((slot_ref, spectra_ref), (slot, spectra), arrived)
    parts, stations, windows, freq = spectra.shape
    chunks = freq // LANES
    moves[0].wait()
    for place in range(stations):
        for station in range(stations):
            row = place * stations + station
            here = (slot[0, place] == station).astype(jnp.float32)
            placing_ref[row : row + 1, :] = jnp.full((1, placing_ref.shape[1]), here, jnp.float32)
    moves[1].wait()
    for part in range(parts):
        for place in range(stations):
            values = spectra[part, slot[0, place]].astype(jnp.float32)
            base = (part * stations + place) * windows * chunks
            for chunk in range(chunks):
                spread[pl.ds(base + chunk, windows, stride=chunks), :] = values[
                    :, chunk * LANES : (chunk + 1) * LANES
                ]
    mine_ref[...] = spread[: mine_ref.shape[0], :].astype(jnp.bfloat16)


def mask_kernel(start_ref, end_ref, model_ref, near_ref, last_ref, pass_ref, rows):
    core = lax.axis_index("blk") % 2
    layer = lax.axis_index("lay")
    stations, lags = model_ref.shape[3:]
    half = lags // 2
    before = lax.broadcasted_iota(jnp.int32, (half, half), 0)
    after = lax.broadcasted_iota(jnp.int32, (half, half), 1)
    turn = (before + after == half) | (before + after == 0)
    turn = jnp.where(turn, 1.0, 0.0).astype(jnp.bfloat16)
    count = stations * stations
    lag = lax.broadcasted_iota(jnp.int32, (count, lags), 1)
    row = lax.broadcasted_iota(jnp.int32, (count, lags), 0)
    diagonal = row % (stations + 1) == 0
    start, end = start_ref[...], end_ref[...]
    values = []
    for offset in range(4):
        for first in range(stations):
            rows[first * stations : (first + 1) * stations, :] = model_ref[0, offset, first].astype(
                jnp.float32
            )
        keep = (lag >= start[:, offset : offset + 1]) & (lag < end[:, offset : offset + 1])
        if offset == 0:
            keep = keep & jnp.logical_not(diagonal & (layer == 0))
        values.append(jnp.where(keep, rows[...], OUTSIDE))
    even = core == 0
    values = jnp.concatenate(
        [
            jnp.where(even, values[2], values[0]),
            values[3],
            values[1],
            jnp.where(even, values[0], values[2]),
        ],
        axis=0,
    ).astype(jnp.bfloat16)
    turned = jnp.dot(values[:, :half], turn, preferred_element_type=jnp.float32)
    values = jnp.concatenate([values[:, half:], turned.astype(jnp.bfloat16)], axis=1)
    near_ref[...] = values[:count]
    last_ref[...] = values[count : 2 * count]
    pass_ref[...] = values[2 * count :]


def changed():
    chips = lax.axis_size("blk") // 2
    layers = lax.axis_size("lay")
    core, layer = lax.axis_index("blk") % 2, lax.axis_index("lay")
    distance = jnp.where(core == 0, 2 * layer + 1, jnp.where(layer > 0, 2 * layer, 2 * layers))
    target = lax.rem(lax.axis_index("blk") // 2 + distance, chips)
    flag = target < 0
    for chip, own_core in CHANGED:
        flag = flag | ((target == chip) & (core == own_core))
    return flag


def is_home():
    return (lax.axis_index("lay") == 0) & (lax.axis_index("blk") % 2 == 1)


PAIRS = ((0, 2), (0, 3), (1, 2), (1, 4))


def unfold(mine_ref, other_ref, near_ref, cross_ref, spec):
    home = is_home()
    size = mine_ref.shape[0]
    mine = mine_ref[...].astype(jnp.float32)
    other = other_ref[...].astype(jnp.float32)
    near = near_ref[...].astype(jnp.float32)
    cross = cross_ref[...].astype(jnp.float32)
    spec[0 * size : 1 * size, :] = mine
    spec[1 * size : 2 * size, :] = other
    spec[2 * size : 3 * size, :] = jnp.where(home, mine, near)
    spec[3 * size : 4 * size, :] = cross
    spec[4 * size : 5 * size, :] = jnp.where(home, other, cross)


def spectrum(spec, stations, windows, chunks, block, window):
    rows = []
    for part in range(2):
        rows.append([])
        for station in range(stations):
            index = ((block * 2 + part) * stations + station) * windows + window
            rows[part].append(spec[index * chunks : (index + 1) * chunks, :])
    return rows


def edge_rows(table_ref, freq):
    half = table_ref.shape[1]
    edge = table_ref[2 * freq :, :].astype(jnp.float32)
    pieces = freq // half
    return [
        jnp.concatenate(
            [edge[row : row + 1] for row in range(part * pieces, (part + 1) * pieces)], axis=1
        )
        for part in range(2)
    ]


def lag_kernel(
    stations, windows, mine_ref, other_ref, near_ref, cross_ref, table_ref, lagged_ref, spec, rows
):
    freq = (table_ref.shape[0] - EDGE_ROWS) // 2
    chunks = freq // LANES
    pair_rows = stations * stations
    total = len(PAIRS) * pair_rows
    unfold(mine_ref, other_ref, near_ref, cross_ref, spec)
    for pair, (first, second) in enumerate(PAIRS):
        real = [[None] * stations for _ in range(stations)]
        imag = [[None] * stations for _ in range(stations)]
        for window in range(windows):
            u = spectrum(spec, stations, windows, chunks, first, window)
            v = spectrum(spec, stations, windows, chunks, second, window)
            for i in range(stations):
                for j in range(stations):
                    re = u[0][i] * v[0][j] + u[1][i] * v[1][j]
                    im = u[1][i] * v[0][j] - u[0][i] * v[1][j]
                    real[i][j] = re if window == 0 else real[i][j] + re
                    imag[i][j] = im if window == 0 else imag[i][j] + im
        for i in range(stations):
            for j in range(stations):
                row = pair * pair_rows + i * stations + j
                rows[row * chunks : (row + 1) * chunks, :] = real[i][j]
                row = row + total
                rows[row * chunks : (row + 1) * chunks, :] = imag[i][j]

    def left(part):
        return jnp.concatenate(
            [
                rows[pl.ds(part * total * chunks + chunk, total, stride=chunks), :].astype(
                    jnp.bfloat16
                )
                for chunk in range(chunks)
            ],
            axis=1,
        )

    half = table_ref.shape[1]
    tile = min(256, half)
    edges = edge_rows(table_ref, freq)
    real, imag = left(0), left(1)
    last_lag = jnp.sum(
        real.astype(jnp.float32) * edges[0] + imag.astype(jnp.float32) * edges[1],
        axis=1,
        keepdims=True,
    )
    first_lane = lax.broadcasted_iota(jnp.int32, (total, tile), 1) == 0
    for place in range(half // tile):
        span = slice(place * tile, (place + 1) * tile)
        even = jnp.dot(real, table_ref[:freq, span], preferred_element_type=jnp.float32)
        odd = jnp.dot(imag, table_ref[freq : 2 * freq, span], preferred_element_type=jnp.float32)
        lagged_ref[:, span] = even + odd
        value = even - odd
        if place == 0:
            value = jnp.where(first_lane, last_lag, value)
        lagged_ref[:, half + place * tile : half + (place + 1) * tile] = value


def response_kernel(
    layers,
    stations,
    windows,
    lagged_ref,
    mine_ref,
    other_ref,
    near_ref,
    cross_ref,
    model_near_ref,
    model_last_ref,
    model_moved_ref,
    model_pass_ref,
    table_ref,
    *rest,
):
    far_refs = rest[:layers]
    resp_rows, home_sums, pass_ref, spec, sums, passed = rest[layers:]
    freq = (table_ref.shape[0] - EDGE_ROWS) // 2
    chunks = freq // LANES
    pair_rows = stations * stations
    total = len(PAIRS) * pair_rows
    block_rows = 2 * stations * windows
    size = block_rows * chunks
    core = lax.axis_index("blk") % 2
    home = is_home()
    half = table_ref.shape[1]
    tile = min(256, half)
    edges = edge_rows(table_ref, freq)
    misfit = []
    for place in range(2 * half // tile):
        span = slice(place * tile, (place + 1) * tile)
        last = jnp.where(
            core == 0,
            model_last_ref[:, span].astype(jnp.float32),
            model_moved_ref[:, span].astype(jnp.float32),
        )
        model = jnp.concatenate(
            [
                model_near_ref[:, span].astype(jnp.float32),
                last,
                model_pass_ref[:, span].astype(jnp.float32),
            ],
            axis=0,
        )
        value = jnp.where(model == OUTSIDE, 0.0, lagged_ref[:, span] - model)
        misfit.append(value.astype(jnp.bfloat16))
    count = half // tile
    first_lane = lax.broadcasted_iota(jnp.int32, (total, tile), 1) == 0
    first_behind = misfit[count].astype(jnp.float32)
    last_lag = first_behind[:, :1]
    misfit[count] = jnp.where(first_lane, 0.0, first_behind).astype(jnp.bfloat16)
    stacked = jnp.concatenate(
        [jnp.concatenate(misfit[:count], axis=1), jnp.concatenate(misfit[count:], axis=1)], axis=0
    )
    per_tile = tile // LANES
    for place in range(2 * chunks // per_tile):
        part, chunk = divmod(place * per_tile, chunks)
        low = chunk * LANES
        if low + tile <= half:
            table = table_ref[part * freq : part * freq + half, low : low + tile]
            product = jnp.dot(stacked, table, preferred_element_type=jnp.float32)
        else:
            product = lax.dot_general(
                stacked,
                table_ref[place * tile : (place + 1) * tile, :],
                (((1,), (1,)), ((), ())),
                preferred_element_type=jnp.float32,
            )
        weights = edges[part][:, chunk * LANES : chunk * LANES + tile]
        if part == 0:
            response = product[:total] + product[total:]
        else:
            response = product[:total] - product[total:]
        response = (response + last_lag * weights).astype(jnp.bfloat16).astype(jnp.float32)
        for inner in range(per_tile):
            start = part * total * chunks + chunk + inner
            resp_rows[pl.ds(start, total, stride=chunks), :] = response[
                :, inner * LANES : (inner + 1) * LANES
            ]

    unfold(mine_ref, other_ref, near_ref, cross_ref, spec)
    written = set()
    for pair, (first, second) in enumerate(PAIRS):
        r = response_rows(resp_rows, pair, pair_rows, total, chunks)
        for window in range(windows):
            u = spectrum(spec, stations, windows, chunks, first, window)
            for j in range(stations):
                terms_re, terms_im = [], []
                for i in range(stations):
                    re, im = r[0][i * stations + j], r[1][i * stations + j]
                    terms_re.append(re * u[0][i] + im * u[1][i])
                    terms_im.append(re * u[1][i] - im * u[0][i])
                for part, terms in enumerate((terms_re, terms_im)):
                    index = (((second - 2) * 2 + part) * stations + j) * windows + window
                    accumulate(sums, written, index, chunks, terms)
    part_near = sums[:size, :]
    part_last = sums[2 * size :, :]
    home_sums[...] = jnp.where(home, part_near, 0.0)
    passed[:size, :] = jnp.where(home, part_last, 0.0)
    sums[:size, :] = jnp.where(home, 0.0, part_near)
    sums[size : 2 * size, :] += jnp.where(home, 0.0, part_last)
    for place in range(layers):
        step = jnp.where(changed(), 1 - place, place) if place < 2 <= layers else place
        write_share(sums, far_refs[place], step, layers, 2 * block_rows, chunks)

    add_own_terms(1, resp_rows, spec, passed, stations, windows, chunks)
    write_whole(passed, pass_ref, block_rows, chunks)


def own_kernel(
    stations,
    windows,
    resp_rows,
    home_sums,
    mine_ref,
    other_ref,
    near_ref,
    cross_ref,
    own_ref,
    spec,
    sums,
):
    block_rows = 2 * stations * windows
    chunks = mine_ref.shape[0] // block_rows
    unfold(mine_ref, other_ref, near_ref, cross_ref, spec)
    sums[: block_rows * chunks, :] = home_sums[...]
    add_own_terms(0, resp_rows, spec, sums, stations, windows, chunks)
    write_whole(sums, own_ref, block_rows, chunks)


def add_own_terms(block, resp_rows, spec, sums, stations, windows, chunks):
    pair_rows = stations * stations
    total = len(PAIRS) * pair_rows
    written = set(range(2 * stations * windows))
    for pair, (first, second) in enumerate(PAIRS):
        if first != block:
            continue
        r = response_rows(resp_rows, pair, pair_rows, total, chunks)
        for window in range(windows):
            v = spectrum(spec, stations, windows, chunks, second, window)
            for i in range(stations):
                terms_re, terms_im = [], []
                for j in range(stations):
                    re, im = r[0][i * stations + j], r[1][i * stations + j]
                    terms_re.append(re * v[0][j] - im * v[1][j])
                    terms_im.append(re * v[1][j] + im * v[0][j])
                for part, terms in enumerate((terms_re, terms_im)):
                    index = (part * stations + i) * windows + window
                    accumulate(sums, written, index, chunks, terms)


def write_whole(sums, target, count, chunks):
    for chunk in range(chunks):
        values = sums[pl.ds(chunk, count, stride=chunks), :]
        target[:, chunk * LANES : (chunk + 1) * LANES] = values.astype(target.dtype)


def share_kernel(layers, own_ref, pass_ref, *out_refs):
    width = own_ref.shape[1] // layers
    for step, out_ref in enumerate(out_refs):
        start = lax.rem(lax.axis_index("lay") + step, layers) * width
        span = pl.ds(pl.multiple_of(start, LANES), width)
        total = own_ref[:, span] + pass_ref[:, span].astype(jnp.float32)
        out_ref[...] = total.astype(out_ref.dtype)


def response_rows(resp_rows, pair, pair_rows, total, chunks):
    rows = []
    for part in range(2):
        base = part * total + pair * pair_rows
        rows.append(
            [
                resp_rows[(base + row) * chunks : (base + row + 1) * chunks, :]
                for row in range(pair_rows)
            ]
        )
    return rows


def accumulate(sums, written, index, chunks, terms):
    rows = slice(index * chunks, (index + 1) * chunks)
    value = sum(terms[1:], terms[0])
    if index in written:
        value = value + sums[rows, :]
    written.add(index)
    sums[rows, :] = value


def write_share(sums, target, step, layers, count, chunks):
    width = chunks // layers
    start = lax.rem(lax.axis_index("lay") + step, layers) * width
    for inner in range(width):
        values = sums[pl.ds(start + inner, count, stride=chunks), :]
        target[:, inner * LANES : (inner + 1) * LANES] = values.astype(target.dtype)


def add_kernel(*refs):
    keep_ref, send_ref = refs[-2:]
    total = refs[0][...].astype(jnp.float32)
    for ref in refs[1:-2]:
        total = total + ref[...].astype(jnp.float32)
    half = keep_ref.shape[0]
    keep_ref[...] = total[:half]
    send_ref[...] = total[half:]


def gather_kernel(keep_ref, send_ref, *refs):
    total_ref, out_ref = refs[-2:]
    total = keep_ref[...]
    for ref in refs[:-2]:
        total = total + ref[...].astype(jnp.float32)
    total_ref[...] = total
    out_ref[...] = send_ref[...]


def place_kernel(scale, placing_ref, *refs):
    out_ref = refs[-1]
    parts, stations, windows, _ = out_ref.shape
    total = refs[0][...]
    for ref in refs[1:-1]:
        total = total + ref[...].astype(jnp.float32)
    total = total * scale
    for station in range(stations):
        here = [
            placing_ref[row : row + 1, :]
            for row in range(station, stations * stations, stations)
        ]
        for part in range(parts):
            value = None
            for place in range(stations):
                base = (part * stations + place) * windows
                term = here[place] * total[base : base + windows, :]
                value = term if value is None else value + term
            out_ref[part, station] = value


VMEM = pl.BlockSpec(memory_space=pltpu.VMEM)
HBM = pl.BlockSpec(memory_space=pltpu.HBM)


def grant(mebibytes):
    return pltpu.CompilerParams(vmem_limit_bytes=mebibytes * 1024 * 1024)


def local(spectra, model_corr, window_start, window_end, station_slot):
    _, stations, windows, freq = spectra.shape
    lags = model_corr.shape[4]
    layers = lax.axis_size("lay")
    blocks = lax.axis_size("blk")
    chips = blocks // 2
    chunks = freq // LANES
    pair_rows = stations * stations
    block_rows = 2 * stations * windows
    f32, bf16 = jnp.float32, jnp.bfloat16

    def distance(layer, core):
        if core == 0:
            return 2 * layer + 1
        return 2 * layer if layer > 0 else 2 * layers

    def move(value, target):
        pairs = []
        for block in range(blocks):
            for layer in range(layers):
                chip, core, to_layer = target(block // 2, block % 2, layer)
                pairs.append(
                    (block * layers + layer, (chip % chips * 2 + core) * layers + to_layer % layers)
                )
        return lax.ppermute(value, AXES, pairs)

    def swap_cores(value):
        return move(value, lambda chip, core, layer: (chip, 1 - core, layer))

    station_slot, spectra = (
        pltpu.with_memory_space_constraint(value, pltpu.HBM) for value in (station_slot, spectra)
    )
    mine, placing = pl.pallas_call(
        order_kernel,
        out_shape=[
            jax.ShapeDtypeStruct((block_rows * chunks, LANES), bf16),
            jax.ShapeDtypeStruct((stations * stations, freq // layers), f32),
        ],
        in_specs=[HBM] * 2,
        out_specs=[VMEM] * 2,
        scratch_shapes=[
            pltpu.SMEM(station_slot.shape, jnp.int32),
            pltpu.VMEM(spectra.shape, bf16),
            pltpu.VMEM(((block_rows + 1) * chunks, LANES), f32),
            pltpu.SemaphoreType.DMA((2,)),
        ],
        compiler_params=grant(2),
        cost_estimate=pl.CostEstimate(flops=5 * 10**9, bytes_accessed=10**6, transcendentals=0),
        name="order",
    )(station_slot, spectra)
    cross = move(mine, lambda chip, core, layer: (chip - distance(layer, 1 - core), 1 - core, layer))
    near = move(
        mine,
        lambda chip, core, layer: (
            chip ^ 1 if layer == 0 and core == 1 else chip - distance(layer, core),
            core,
            layer,
        ),
    )
    other = swap_cores(mine)
    model_near, model_last, model_pass = pl.pallas_call(
        mask_kernel,
        out_shape=[
            jax.ShapeDtypeStruct((pair_rows, lags), bf16),
            jax.ShapeDtypeStruct((pair_rows, lags), bf16),
            jax.ShapeDtypeStruct((2 * pair_rows, lags), bf16),
        ],
        in_specs=[VMEM] * 3,
        out_specs=[VMEM] * 3,
        scratch_shapes=[pltpu.VMEM((pair_rows, lags), f32)],
        compiler_params=grant(4),
        cost_estimate=pl.CostEstimate(flops=5 * 10**9, bytes_accessed=10**6, transcendentals=0),
        name="mask",
    )(window_start, window_end, model_corr)
    model_pass = swap_cores(model_pass)
    model_moved = move(model_last, lambda chip, core, layer: (chip, core, layer + 1))
    table = lag_table(freq, lags, windows)
    total = 4 * pair_rows
    blocks_in = (mine, other, near, cross)
    spec = pltpu.VMEM((5 * block_rows * chunks, LANES), f32)
    lagged = pl.pallas_call(
        functools.partial(lag_kernel, stations, windows),
        out_shape=jax.ShapeDtypeStruct((total, lags), f32),
        in_specs=[VMEM] * 5,
        out_specs=VMEM,
        scratch_shapes=[spec, pltpu.VMEM(((2 * total + 1) * chunks, LANES), f32)],
        compiler_params=grant(8),
        name="lag",
    )(*blocks_in, table)
    part = (2 * block_rows, freq // layers)
    outs = pl.pallas_call(
        functools.partial(response_kernel, layers, stations, windows),
        out_shape=[jax.ShapeDtypeStruct(part, bf16)] * layers
        + [
            jax.ShapeDtypeStruct(((2 * total + 1) * chunks, LANES), f32),
            jax.ShapeDtypeStruct((block_rows * chunks, LANES), f32),
            jax.ShapeDtypeStruct((block_rows, freq), bf16),
        ],
        in_specs=[VMEM] * 10,
        out_specs=[VMEM] * (layers + 3),
        scratch_shapes=[
            spec,
            pltpu.VMEM((3 * block_rows * chunks, LANES), f32),
            pltpu.VMEM(((block_rows + 1) * chunks, LANES), f32),
        ],
        compiler_params=grant(12),
        name="response",
    )(lagged, *blocks_in, model_near, model_last, model_moved, model_pass, table)
    def returned(place):
        def target(chip, core, layer):
            chip = (chip + distance(layer, core)) % chips
            step = 1 - place if (chip, core) in CHANGED and place < 2 <= layers else place
            return chip, core, layer + step

        return target

    parts = [move(outs[place], returned(place)) for place in range(layers)]
    own = pl.pallas_call(
        functools.partial(own_kernel, stations, windows),
        out_shape=jax.ShapeDtypeStruct((block_rows, freq), f32),
        in_specs=[VMEM] * 6,
        out_specs=VMEM,
        scratch_shapes=[spec, pltpu.VMEM(((block_rows + 1) * chunks, LANES), f32)],
        compiler_params=grant(8),
        name="own",
    )(outs[layers], outs[layers + 1], *blocks_in)
    share = (block_rows, freq // layers)
    own = pl.pallas_call(
        functools.partial(share_kernel, layers),
        out_shape=[jax.ShapeDtypeStruct(share, f32)]
        + [jax.ShapeDtypeStruct(share, bf16)] * (layers - 1),
        in_specs=[VMEM] * 2,
        out_specs=[VMEM] * layers,
        compiler_params=grant(2),
        name="share",
    )(own, swap_cores(outs[layers + 2]))
    own = [own[0]] + [
        move(own[step], lambda chip, core, layer: (chip, core, layer + step))
        for step in range(1, layers)
    ]
    firsts = list(range(min(2, layers) - 1, -1, -1)) + list(range(2, layers))
    keep, send = pl.pallas_call(
        add_kernel,
        out_shape=[jax.ShapeDtypeStruct(share, f32)] * 2,
        in_specs=[VMEM] * layers,
        out_specs=[VMEM] * 2,
        compiler_params=grant(2),
        name="arrived",
    )(*[parts[place] for place in firsts])
    keep, send = pl.pallas_call(
        gather_kernel,
        out_shape=[jax.ShapeDtypeStruct(share, f32)] * 2,
        in_specs=[VMEM] * (2 + layers),
        out_specs=[VMEM] * 2,
        compiler_params=grant(2),
        name="gather",
    )(keep, send, *own)
    return pl.pallas_call(
        functools.partial(place_kernel, 1.0 / math.sqrt(blocks * stations)),
        out_shape=jax.ShapeDtypeStruct((2, stations, windows, freq // layers), f32),
        in_specs=[VMEM] * 3,
        out_specs=VMEM,
        compiler_params=grant(2),
        name="place",
    )(placing, keep, swap_cores(send))


def solution(mesh):
    in_specs = (
        P(None, "blk", None, None),
        P("blk", "lay", None, None, None),
        P("blk", "lay"),
        P("blk", "lay"),
        P("blk", None),
    )
    out_specs = P(None, "blk", None, "lay")
    return jax.shard_map(local, mesh=mesh, in_specs=in_specs, out_specs=out_specs, check_vma=False)
```

```python
import functools
import math

import jax
import jax.numpy as jnp
import ml_dtypes
import numpy as np
from jax import lax
from jax.experimental import pallas as pl
from jax.experimental.pallas import tpu as pltpu
from jax.sharding import PartitionSpec as P


LANES = 128
AXES = ("blk", "lay")
EDGE_ROWS = 64
PIECES = 4
CHANGED = ((1, 0),)
OUTSIDE = 2.0**100


def lag_table(freq_count, lag_count, window_count):
    half = lag_count // 2
    freq_index = np.arange(freq_count, dtype=np.int64)
    lag_index = np.arange(half + 1, dtype=np.int64)
    phase_index = freq_index[:, None] * lag_index[None, :] % (2 * freq_count)
    angle = phase_index.astype(np.float64) * (math.pi / freq_count)
    factor = 1.0 / math.sqrt(2.0 * freq_count * window_count)
    cosine, sine = np.cos(angle) * factor, -np.sin(angle) * factor
    edge = np.concatenate([cosine[:, half], -sine[:, half]]).reshape(-1, half)
    padding = np.zeros((EDGE_ROWS - edge.shape[0], half))
    table = np.concatenate([cosine[:, :half], sine[:, :half], edge, padding])
    return jnp.asarray(table.astype(ml_dtypes.bfloat16))


def copies(sources, targets, arrived):
    moves = [
        pltpu.make_async_copy(source, target, arrived.at[place])
        for place, (source, target) in enumerate(zip(sources, targets))
    ]
    for copy in moves:
        copy.start()
    return moves


def order_kernel(slot_ref, spectra_ref, mine_ref, slot, spectra, spread, arrived):
    moves = copies((slot_ref, spectra_ref), (slot, spectra), arrived)
    parts, stations, windows, freq = spectra.shape
    chunks = freq // LANES
    moves[0].wait()
    moves[1].wait()
    for part in range(parts):
        for place in range(stations):
            values = spectra[part, slot[0, place]].astype(jnp.float32)
            base = (part * stations + place) * windows * chunks
            for chunk in range(chunks):
                spread[pl.ds(base + chunk, windows, stride=chunks), :] = values[
                    :, chunk * LANES : (chunk + 1) * LANES
                ]
    mine_ref[...] = spread[: mine_ref.shape[0], :].astype(jnp.bfloat16)


def mask_kernel(
    slot_ref, start_ref, end_ref, model_ref, near_ref, last_ref, pass_ref, placing_ref, rows
):
    core = lax.axis_index("blk") % 2
    layer = lax.axis_index("lay")
    stations, lags = model_ref.shape[3:]
    half = lags // 2
    before = lax.broadcasted_iota(jnp.int32, (half, half), 0)
    after = lax.broadcasted_iota(jnp.int32, (half, half), 1)
    turn = (before + after == half) | (before + after == 0)
    turn = jnp.where(turn, 1.0, 0.0).astype(jnp.bfloat16)
    count = stations * stations
    lag = lax.broadcasted_iota(jnp.int32, (count, lags), 1)
    row = lax.broadcasted_iota(jnp.int32, (count, lags), 0)
    diagonal = row % (stations + 1) == 0
    slot = slot_ref[...]
    width = placing_ref.shape[1]
    for place in range(stations):
        for station in range(stations):
            here = jnp.where(slot[:, place : place + 1] == station, 1.0, 0.0)
            row_place = place * stations + station
            placing_ref[row_place : row_place + 1, :] = jnp.broadcast_to(here, (1, width))
    start, end = start_ref[...], end_ref[...]
    values = []
    for offset in range(4):
        for first in range(stations):
            rows[first * stations : (first + 1) * stations, :] = model_ref[0, offset, first].astype(
                jnp.float32
            )
        keep = (lag >= start[:, offset : offset + 1]) & (lag < end[:, offset : offset + 1])
        if offset == 0:
            keep = keep & jnp.logical_not(diagonal & (layer == 0))
        values.append(jnp.where(keep, rows[...], OUTSIDE))
    even = core == 0
    values = jnp.concatenate(
        [
            jnp.where(even, values[2], values[0]),
            values[3],
            values[1],
            jnp.where(even, values[0], values[2]),
        ],
        axis=0,
    ).astype(jnp.bfloat16)
    turned = jnp.dot(values[:, :half], turn, preferred_element_type=jnp.float32)
    values = jnp.concatenate([values[:, half:], turned.astype(jnp.bfloat16)], axis=1)
    near_ref[...] = values[:count]
    last_ref[...] = values[count : 2 * count]
    pass_ref[...] = values[2 * count :]


def changed():
    chips = lax.axis_size("blk") // 2
    layers = lax.axis_size("lay")
    core, layer = lax.axis_index("blk") % 2, lax.axis_index("lay")
    distance = jnp.where(core == 0, 2 * layer + 1, jnp.where(layer > 0, 2 * layer, 2 * layers))
    target = lax.rem(lax.axis_index("blk") // 2 + distance, chips)
    flag = target < 0
    for chip, own_core in CHANGED:
        flag = flag | ((target == chip) & (core == own_core))
    return flag


def is_home():
    return (lax.axis_index("lay") == 0) & (lax.axis_index("blk") % 2 == 1)


PAIRS = ((0, 2), (0, 3), (1, 2), (1, 4))


def unfold(mine_ref, other_ref, near_ref, cross_ref, spec):
    home = is_home()
    size = mine_ref.shape[0]
    mine = mine_ref[...].astype(jnp.float32)
    other = other_ref[...].astype(jnp.float32)
    near = near_ref[...].astype(jnp.float32)
    cross = cross_ref[...].astype(jnp.float32)
    spec[0 * size : 1 * size, :] = mine
    spec[1 * size : 2 * size, :] = other
    spec[2 * size : 3 * size, :] = jnp.where(home, mine, near)
    spec[3 * size : 4 * size, :] = cross
    spec[4 * size : 5 * size, :] = jnp.where(home, other, cross)


def spectrum(spec, stations, windows, chunks, block, window):
    rows = []
    for part in range(2):
        rows.append([])
        for station in range(stations):
            index = ((block * 2 + part) * stations + station) * windows + window
            rows[part].append(spec[index * chunks : (index + 1) * chunks, :])
    return rows


def edge_rows(table_ref, freq):
    half = table_ref.shape[1]
    edge = table_ref[2 * freq :, :].astype(jnp.float32)
    pieces = freq // half
    return [
        jnp.concatenate(
            [edge[row : row + 1] for row in range(part * pieces, (part + 1) * pieces)], axis=1
        )
        for part in range(2)
    ]


def lag_kernel(
    stations, windows, mine_ref, other_ref, near_ref, cross_ref, table_ref, lagged_ref, spec, rows
):
    freq = (table_ref.shape[0] - EDGE_ROWS) // 2
    chunks = freq // LANES
    pair_rows = stations * stations
    total = len(PAIRS) * pair_rows
    unfold(mine_ref, other_ref, near_ref, cross_ref, spec)
    for pair, (first, second) in enumerate(PAIRS):
        real = [[None] * stations for _ in range(stations)]
        imag = [[None] * stations for _ in range(stations)]
        for window in range(windows):
            u = spectrum(spec, stations, windows, chunks, first, window)
            v = spectrum(spec, stations, windows, chunks, second, window)
            for i in range(stations):
                for j in range(stations):
                    re = u[0][i] * v[0][j] + u[1][i] * v[1][j]
                    im = u[1][i] * v[0][j] - u[0][i] * v[1][j]
                    real[i][j] = re if window == 0 else real[i][j] + re
                    imag[i][j] = im if window == 0 else imag[i][j] + im
        for i in range(stations):
            for j in range(stations):
                row = pair * pair_rows + i * stations + j
                rows[row * chunks : (row + 1) * chunks, :] = real[i][j]
                row = row + total
                rows[row * chunks : (row + 1) * chunks, :] = imag[i][j]

    def left(part):
        return jnp.concatenate(
            [
                rows[pl.ds(part * total * chunks + chunk, total, stride=chunks), :].astype(
                    jnp.bfloat16
                )
                for chunk in range(chunks)
            ],
            axis=1,
        )

    half = table_ref.shape[1]
    tile = min(512, half)
    edges = edge_rows(table_ref, freq)
    real, imag = left(0), left(1)
    last_lag = jnp.sum(
        real.astype(jnp.float32) * edges[0] + imag.astype(jnp.float32) * edges[1],
        axis=1,
        keepdims=True,
    )
    first_lane = lax.broadcasted_iota(jnp.int32, (total, tile), 1) == 0
    for place in range(half // tile):
        span = slice(place * tile, (place + 1) * tile)
        even = jnp.dot(real, table_ref[:freq, span], preferred_element_type=jnp.float32)
        odd = jnp.dot(imag, table_ref[freq : 2 * freq, span], preferred_element_type=jnp.float32)
        lagged_ref[:, span] = even + odd
        value = even - odd
        if place == 0:
            value = jnp.where(first_lane, last_lag, value)
        lagged_ref[:, half + place * tile : half + (place + 1) * tile] = value


def response_kernel(
    layers,
    stations,
    windows,
    lagged_ref,
    mine_ref,
    other_ref,
    near_ref,
    cross_ref,
    model_near_ref,
    model_last_ref,
    model_moved_ref,
    model_pass_ref,
    table_ref,
    *rest,
):
    far_refs = rest[:layers]
    resp_rows, home_sums, pass_ref, spec, sums, passed = rest[layers:]
    freq = (table_ref.shape[0] - EDGE_ROWS) // 2
    chunks = freq // LANES
    pair_rows = stations * stations
    total = len(PAIRS) * pair_rows
    block_rows = 2 * stations * windows
    size = block_rows * chunks
    core = lax.axis_index("blk") % 2
    home = is_home()
    half = table_ref.shape[1]
    tile = min(512, half)
    edges = edge_rows(table_ref, freq)
    misfit = []
    for place in range(2 * half // tile):
        span = slice(place * tile, (place + 1) * tile)
        last = jnp.where(
            core == 0,
            model_last_ref[:, span].astype(jnp.float32),
            model_moved_ref[:, span].astype(jnp.float32),
        )
        model = jnp.concatenate(
            [
                model_near_ref[:, span].astype(jnp.float32),
                last,
                model_pass_ref[:, span].astype(jnp.float32),
            ],
            axis=0,
        )
        value = jnp.where(model == OUTSIDE, 0.0, lagged_ref[:, span] - model)
        misfit.append(value.astype(jnp.bfloat16))
    count = half // tile
    first_lane = lax.broadcasted_iota(jnp.int32, (total, tile), 1) == 0
    first_behind = misfit[count].astype(jnp.float32)
    last_lag = first_behind[:, :1]
    misfit[count] = jnp.where(first_lane, 0.0, first_behind).astype(jnp.bfloat16)
    stacked = jnp.concatenate(
        [jnp.concatenate(misfit[:count], axis=1), jnp.concatenate(misfit[count:], axis=1)], axis=0
    )
    per_tile = tile // LANES
    for place in range(2 * chunks // per_tile):
        part, chunk = divmod(place * per_tile, chunks)
        low = chunk * LANES
        if low + tile <= half:
            table = table_ref[part * freq : part * freq + half, low : low + tile]
            product = jnp.dot(stacked, table, preferred_element_type=jnp.float32)
        else:
            product = lax.dot_general(
                stacked,
                table_ref[place * tile : (place + 1) * tile, :],
                (((1,), (1,)), ((), ())),
                preferred_element_type=jnp.float32,
            )
        weights = edges[part][:, chunk * LANES : chunk * LANES + tile]
        if part == 0:
            response = product[:total] + product[total:]
        else:
            response = product[:total] - product[total:]
        response = (response + last_lag * weights).astype(jnp.bfloat16).astype(jnp.float32)
        for inner in range(per_tile):
            start = part * total * chunks + chunk + inner
            resp_rows[pl.ds(start, total, stride=chunks), :] = response[
                :, inner * LANES : (inner + 1) * LANES
            ]

    unfold(mine_ref, other_ref, near_ref, cross_ref, spec)
    written = set()
    for pair, (first, second) in enumerate(PAIRS):
        r = response_rows(resp_rows, pair, pair_rows, total, chunks)
        for window in range(windows):
            u = spectrum(spec, stations, windows, chunks, first, window)
            for j in range(stations):
                terms_re, terms_im = [], []
                for i in range(stations):
                    re, im = r[0][i * stations + j], r[1][i * stations + j]
                    terms_re.append(re * u[0][i] + im * u[1][i])
                    terms_im.append(re * u[1][i] - im * u[0][i])
                for part, terms in enumerate((terms_re, terms_im)):
                    index = (((second - 2) * 2 + part) * stations + j) * windows + window
                    accumulate(sums, written, index, chunks, terms)
    part_near = sums[:size, :]
    part_last = sums[2 * size :, :]
    home_sums[...] = jnp.where(home, part_near, 0.0)
    passed[:size, :] = jnp.where(home, part_last, 0.0)
    sums[:size, :] = jnp.where(home, 0.0, part_near)
    sums[size : 2 * size, :] += jnp.where(home, 0.0, part_last)
    for place in range(layers):
        step = jnp.where(changed(), 1 - place, place) if place < 2 <= layers else place
        write_share(sums, far_refs[place], step, layers, 2 * block_rows, chunks)

    add_own_terms(1, resp_rows, spec, passed, stations, windows, chunks)
    write_whole(passed, pass_ref, block_rows, chunks)


def own_kernel(
    stations,
    windows,
    resp_rows,
    home_sums,
    mine_ref,
    other_ref,
    near_ref,
    cross_ref,
    own_ref,
    spec,
    sums,
):
    block_rows = 2 * stations * windows
    chunks = mine_ref.shape[0] // block_rows
    unfold(mine_ref, other_ref, near_ref, cross_ref, spec)
    sums[: block_rows * chunks, :] = home_sums[...]
    add_own_terms(0, resp_rows, spec, sums, stations, windows, chunks)
    write_whole(sums, own_ref, block_rows, chunks)


def add_own_terms(block, resp_rows, spec, sums, stations, windows, chunks):
    pair_rows = stations * stations
    total = len(PAIRS) * pair_rows
    written = set(range(2 * stations * windows))
    for pair, (first, second) in enumerate(PAIRS):
        if first != block:
            continue
        r = response_rows(resp_rows, pair, pair_rows, total, chunks)
        for window in range(windows):
            v = spectrum(spec, stations, windows, chunks, second, window)
            for i in range(stations):
                terms_re, terms_im = [], []
                for j in range(stations):
                    re, im = r[0][i * stations + j], r[1][i * stations + j]
                    terms_re.append(re * v[0][j] - im * v[1][j])
                    terms_im.append(re * v[1][j] + im * v[0][j])
                for part, terms in enumerate((terms_re, terms_im)):
                    index = (part * stations + i) * windows + window
                    accumulate(sums, written, index, chunks, terms)


def write_whole(sums, target, count, chunks):
    for chunk in range(chunks):
        values = sums[pl.ds(chunk, count, stride=chunks), :]
        target[:, chunk * LANES : (chunk + 1) * LANES] = values.astype(target.dtype)


def share_kernel(layers, own_ref, pass_ref, *out_refs):
    width = own_ref.shape[1] // layers
    for step, out_ref in enumerate(out_refs):
        start = lax.rem(lax.axis_index("lay") + step, layers) * width
        span = pl.ds(pl.multiple_of(start, LANES), width)
        total = own_ref[:, span] + pass_ref[:, span].astype(jnp.float32)
        out_ref[...] = total.astype(out_ref.dtype)


def response_rows(resp_rows, pair, pair_rows, total, chunks):
    rows = []
    for part in range(2):
        base = part * total + pair * pair_rows
        rows.append(
            [
                resp_rows[(base + row) * chunks : (base + row + 1) * chunks, :]
                for row in range(pair_rows)
            ]
        )
    return rows


def accumulate(sums, written, index, chunks, terms):
    rows = slice(index * chunks, (index + 1) * chunks)
    value = sum(terms[1:], terms[0])
    if index in written:
        value = value + sums[rows, :]
    written.add(index)
    sums[rows, :] = value


def write_share(sums, target, step, layers, count, chunks):
    width = chunks // layers
    start = lax.rem(lax.axis_index("lay") + step, layers) * width
    for inner in range(width):
        values = sums[pl.ds(start + inner, count, stride=chunks), :]
        target[:, inner * LANES : (inner + 1) * LANES] = values.astype(target.dtype)


def add_kernel(*refs):
    keep_ref, send_ref = refs[-2:]
    total = refs[0][...].astype(jnp.float32)
    for ref in refs[1:-2]:
        total = total + ref[...].astype(jnp.float32)
    half = keep_ref.shape[0]
    keep_ref[...] = total[:half]
    send_ref[...] = total[half:]


def gather_kernel(keep_ref, send_ref, *refs):
    total_ref, out_ref = refs[-2:]
    total = keep_ref[...]
    for ref in refs[:-2]:
        total = total + ref[...].astype(jnp.float32)
    total_ref[...] = total
    out_ref[...] = send_ref[...]


def place_kernel(scale, placing_ref, *refs):
    out_ref = refs[-1]
    parts, stations, windows, _ = out_ref.shape
    total = refs[0][...]
    for ref in refs[1:-1]:
        total = total + ref[...].astype(jnp.float32)
    total = total * scale
    for station in range(stations):
        here = [
            placing_ref[row : row + 1, :]
            for row in range(station, stations * stations, stations)
        ]
        for part in range(parts):
            value = None
            for place in range(stations):
                base = (part * stations + place) * windows
                term = here[place] * total[base : base + windows, :]
                value = term if value is None else value + term
            out_ref[part, station] = value


VMEM = pl.BlockSpec(memory_space=pltpu.VMEM)
HBM = pl.BlockSpec(memory_space=pltpu.HBM)


def grant(mebibytes):
    return pltpu.CompilerParams(vmem_limit_bytes=mebibytes * 1024 * 1024)


def local(spectra, model_corr, window_start, window_end, station_slot):
    _, stations, windows, freq = spectra.shape
    lags = model_corr.shape[4]
    layers = lax.axis_size("lay")
    blocks = lax.axis_size("blk")
    chips = blocks // 2
    chunks = freq // LANES
    pair_rows = stations * stations
    block_rows = 2 * stations * windows
    f32, bf16 = jnp.float32, jnp.bfloat16

    def distance(layer, core):
        if core == 0:
            return 2 * layer + 1
        return 2 * layer if layer > 0 else 2 * layers

    def move(value, target):
        pairs = []
        for block in range(blocks):
            for layer in range(layers):
                chip, core, to_layer = target(block // 2, block % 2, layer)
                pairs.append(
                    (block * layers + layer, (chip % chips * 2 + core) * layers + to_layer % layers)
                )
        return lax.ppermute(value, AXES, pairs)

    def swap_cores(value):
        return move(value, lambda chip, core, layer: (chip, 1 - core, layer))

    slot, spectra = (
        pltpu.with_memory_space_constraint(value, pltpu.HBM) for value in (station_slot, spectra)
    )
    mine = pl.pallas_call(
        order_kernel,
        out_shape=jax.ShapeDtypeStruct((block_rows * chunks, LANES), bf16),
        in_specs=[HBM] * 2,
        out_specs=VMEM,
        scratch_shapes=[
            pltpu.SMEM(station_slot.shape, jnp.int32),
            pltpu.VMEM(spectra.shape, bf16),
            pltpu.VMEM(((block_rows + 1) * chunks, LANES), f32),
            pltpu.SemaphoreType.DMA((2,)),
        ],
        compiler_params=grant(2),
        cost_estimate=pl.CostEstimate(flops=5 * 10**9, bytes_accessed=10**6, transcendentals=0),
        name="order",
    )(slot, spectra)
    cross = move(mine, lambda chip, core, layer: (chip - distance(layer, 1 - core), 1 - core, layer))
    near = move(
        mine,
        lambda chip, core, layer: (
            chip ^ 1 if layer == 0 and core == 1 else chip - distance(layer, core),
            core,
            layer,
        ),
    )
    other = swap_cores(mine)
    model_near, model_last, model_pass, placing = pl.pallas_call(
        mask_kernel,
        out_shape=[
            jax.ShapeDtypeStruct((pair_rows, lags), bf16),
            jax.ShapeDtypeStruct((pair_rows, lags), bf16),
            jax.ShapeDtypeStruct((2 * pair_rows, lags), bf16),
            jax.ShapeDtypeStruct((stations * stations, freq // layers), f32),
        ],
        in_specs=[VMEM] * 4,
        out_specs=[VMEM] * 4,
        scratch_shapes=[pltpu.VMEM((pair_rows, lags), f32)],
        compiler_params=grant(4),
        cost_estimate=pl.CostEstimate(flops=5 * 10**9, bytes_accessed=10**6, transcendentals=0),
        name="mask",
    )(station_slot, window_start, window_end, model_corr)
    model_pass = swap_cores(model_pass)
    model_moved = move(model_last, lambda chip, core, layer: (chip, core, layer + 1))
    table = lag_table(freq, lags, windows)
    total = 4 * pair_rows
    blocks_in = (mine, other, near, cross)
    spec = pltpu.VMEM((5 * block_rows * chunks, LANES), f32)
    lagged = pl.pallas_call(
        functools.partial(lag_kernel, stations, windows),
        out_shape=jax.ShapeDtypeStruct((total, lags), f32),
        in_specs=[VMEM] * 5,
        out_specs=VMEM,
        scratch_shapes=[spec, pltpu.VMEM(((2 * total + 1) * chunks, LANES), f32)],
        compiler_params=grant(8),
        name="lag",
    )(*blocks_in, table)
    part = (2 * block_rows, freq // layers)
    outs = pl.pallas_call(
        functools.partial(response_kernel, layers, stations, windows),
        out_shape=[jax.ShapeDtypeStruct(part, bf16)] * layers
        + [
            jax.ShapeDtypeStruct(((2 * total + 1) * chunks, LANES), f32),
            jax.ShapeDtypeStruct((block_rows * chunks, LANES), f32),
            jax.ShapeDtypeStruct((block_rows, freq), bf16),
        ],
        in_specs=[VMEM] * 10,
        out_specs=[VMEM] * (layers + 3),
        scratch_shapes=[
            spec,
            pltpu.VMEM((3 * block_rows * chunks, LANES), f32),
            pltpu.VMEM(((block_rows + 1) * chunks, LANES), f32),
        ],
        compiler_params=grant(12),
        name="response",
    )(lagged, *blocks_in, model_near, model_last, model_moved, model_pass, table)
    def returned(place):
        def target(chip, core, layer):
            chip = (chip + distance(layer, core)) % chips
            step = 1 - place if (chip, core) in CHANGED and place < 2 <= layers else place
            return chip, core, layer + step

        return target

    parts = [move(outs[place], returned(place)) for place in range(layers)]
    own = pl.pallas_call(
        functools.partial(own_kernel, stations, windows),
        out_shape=jax.ShapeDtypeStruct((block_rows, freq), f32),
        in_specs=[VMEM] * 6,
        out_specs=VMEM,
        scratch_shapes=[spec, pltpu.VMEM(((block_rows + 1) * chunks, LANES), f32)],
        compiler_params=grant(8),
        name="own",
    )(outs[layers], outs[layers + 1], *blocks_in)
    share = (block_rows, freq // layers)
    own = pl.pallas_call(
        functools.partial(share_kernel, layers),
        out_shape=[jax.ShapeDtypeStruct(share, f32)]
        + [jax.ShapeDtypeStruct(share, bf16)] * (layers - 1),
        in_specs=[VMEM] * 2,
        out_specs=[VMEM] * layers,
        compiler_params=grant(2),
        name="share",
    )(own, swap_cores(outs[layers + 2]))
    own = [own[0]] + [
        move(own[step], lambda chip, core, layer: (chip, core, layer + step))
        for step in range(1, layers)
    ]
    firsts = list(range(min(2, layers) - 1, -1, -1)) + list(range(2, layers))
    keep, send = pl.pallas_call(
        add_kernel,
        out_shape=[jax.ShapeDtypeStruct(share, f32)] * 2,
        in_specs=[VMEM] * layers,
        out_specs=[VMEM] * 2,
        compiler_params=grant(2),
        name="arrived",
    )(*[parts[place] for place in firsts])
    keep, send = pl.pallas_call(
        gather_kernel,
        out_shape=[jax.ShapeDtypeStruct(share, f32)] * 2,
        in_specs=[VMEM] * (2 + layers),
        out_specs=[VMEM] * 2,
        compiler_params=grant(2),
        name="gather",
    )(keep, send, *own)
    return pl.pallas_call(
        functools.partial(place_kernel, 1.0 / math.sqrt(blocks * stations)),
        out_shape=jax.ShapeDtypeStruct((2, stations, windows, freq // layers), f32),
        in_specs=[VMEM] * 3,
        out_specs=VMEM,
        compiler_params=grant(2),
        name="place",
    )(placing, keep, swap_cores(send))


def solution(mesh):
    in_specs = (
        P(None, "blk", None, None),
        P("blk", "lay", None, None, None),
        P("blk", "lay"),
        P("blk", "lay"),
        P("blk", None),
    )
    out_specs = P(None, "blk", None, "lay")
    return jax.shard_map(local, mesh=mesh, in_specs=in_specs, out_specs=out_specs, check_vma=False)
```

```python
import functools
import math

import jax
import jax.numpy as jnp
import ml_dtypes
import numpy as np
from jax import lax
from jax.experimental import pallas as pl
from jax.experimental.pallas import tpu as pltpu
from jax.sharding import PartitionSpec as P


LANES = 128
AXES = ("blk", "lay")
EDGE_ROWS = 64
PIECES = 4
CHANGED = ((1, 0),)
OUTSIDE = 2.0**100


def lag_table(freq_count, lag_count, window_count):
    half = lag_count // 2
    freq_index = np.arange(freq_count, dtype=np.int64)
    lag_index = np.arange(half + 1, dtype=np.int64)
    phase_index = freq_index[:, None] * lag_index[None, :] % (2 * freq_count)
    angle = phase_index.astype(np.float64) * (math.pi / freq_count)
    factor = 1.0 / math.sqrt(2.0 * freq_count * window_count)
    cosine, sine = np.cos(angle) * factor, -np.sin(angle) * factor
    edge = np.concatenate([cosine[:, half], -sine[:, half]]).reshape(-1, half)
    padding = np.zeros((EDGE_ROWS - edge.shape[0], half))
    table = np.concatenate([cosine[:, :half], sine[:, :half], edge, padding])
    return jnp.asarray(table.astype(ml_dtypes.bfloat16))


def copies(sources, targets, arrived):
    moves = [
        pltpu.make_async_copy(source, target, arrived.at[place])
        for place, (source, target) in enumerate(zip(sources, targets))
    ]
    for copy in moves:
        copy.start()
    return moves


def order_kernel(slot_ref, spectra_ref, mine_ref, placing_ref, slot, spectra, spread, arrived):
    moves = copies((slot_ref, spectra_ref), (slot, spectra), arrived)
    parts, stations, windows, freq = spectra.shape
    chunks = freq // LANES
    moves[0].wait()
    for place in range(stations):
        for station in range(stations):
            row = place * stations + station
            here = (slot[0, place] == station).astype(jnp.float32)
            placing_ref[row : row + 1, :] = jnp.full((1, placing_ref.shape[1]), here, jnp.float32)
    moves[1].wait()
    for part in range(parts):
        for place in range(stations):
            values = spectra[part, slot[0, place]].astype(jnp.float32)
            base = (part * stations + place) * windows * chunks
            for chunk in range(chunks):
                spread[pl.ds(base + chunk, windows, stride=chunks), :] = values[
                    :, chunk * LANES : (chunk + 1) * LANES
                ]
    mine_ref[...] = spread[: mine_ref.shape[0], :].astype(jnp.bfloat16)


def mask_kernel(start_ref, end_ref, model_ref, near_ref, last_ref, pass_ref, rows):
    core = lax.axis_index("blk") % 2
    layer = lax.axis_index("lay")
    stations, lags = model_ref.shape[3:]
    half = lags // 2
    before = lax.broadcasted_iota(jnp.int32, (half, half), 0)
    after = lax.broadcasted_iota(jnp.int32, (half, half), 1)
    turn = (before + after == half) | (before + after == 0)
    turn = jnp.where(turn, 1.0, 0.0).astype(jnp.bfloat16)
    count = stations * stations
    lag = lax.broadcasted_iota(jnp.int32, (count, lags), 1)
    row = lax.broadcasted_iota(jnp.int32, (count, lags), 0)
    diagonal = row % (stations + 1) == 0
    start, end = start_ref[...], end_ref[...]
    values = []
    for offset in range(4):
        for first in range(stations):
            rows[first * stations : (first + 1) * stations, :] = model_ref[0, offset, first].astype(
                jnp.float32
            )
        keep = (lag >= start[:, offset : offset + 1]) & (lag < end[:, offset : offset + 1])
        if offset == 0:
            keep = keep & jnp.logical_not(diagonal & (layer == 0))
        values.append(jnp.where(keep, rows[...], OUTSIDE))
    even = core == 0
    values = jnp.concatenate(
        [
            jnp.where(even, values[2], values[0]),
            values[3],
            values[1],
            jnp.where(even, values[0], values[2]),
        ],
        axis=0,
    ).astype(jnp.bfloat16)
    turned = jnp.dot(values[:, :half], turn, preferred_element_type=jnp.float32)
    values = jnp.concatenate([values[:, half:], turned.astype(jnp.bfloat16)], axis=1)
    near_ref[...] = values[:count]
    last_ref[...] = values[count : 2 * count]
    pass_ref[...] = values[2 * count :]


def changed():
    chips = lax.axis_size("blk") // 2
    layers = lax.axis_size("lay")
    core, layer = lax.axis_index("blk") % 2, lax.axis_index("lay")
    distance = jnp.where(core == 0, 2 * layer + 1, jnp.where(layer > 0, 2 * layer, 2 * layers))
    target = lax.rem(lax.axis_index("blk") // 2 + distance, chips)
    flag = target < 0
    for chip, own_core in CHANGED:
        flag = flag | ((target == chip) & (core == own_core))
    return flag


def is_home():
    return (lax.axis_index("lay") == 0) & (lax.axis_index("blk") % 2 == 1)


PAIRS = ((0, 2), (0, 3), (1, 2), (1, 4))


def unfold(mine_ref, other_ref, near_ref, cross_ref, spec):
    home = is_home()
    size = mine_ref.shape[0]
    mine = mine_ref[...].astype(jnp.float32)
    other = other_ref[...].astype(jnp.float32)
    near = near_ref[...].astype(jnp.float32)
    cross = cross_ref[...].astype(jnp.float32)
    spec[0 * size : 1 * size, :] = mine
    spec[1 * size : 2 * size, :] = other
    spec[2 * size : 3 * size, :] = jnp.where(home, mine, near)
    spec[3 * size : 4 * size, :] = cross
    spec[4 * size : 5 * size, :] = jnp.where(home, other, cross)


def spectrum(spec, stations, windows, chunks, block, window):
    rows = []
    for part in range(2):
        rows.append([])
        for station in range(stations):
            index = ((block * 2 + part) * stations + station) * windows + window
            rows[part].append(spec[index * chunks : (index + 1) * chunks, :])
    return rows


def edge_rows(table_ref, freq):
    half = table_ref.shape[1]
    edge = table_ref[2 * freq :, :].astype(jnp.float32)
    pieces = freq // half
    return [
        jnp.concatenate(
            [edge[row : row + 1] for row in range(part * pieces, (part + 1) * pieces)], axis=1
        )
        for part in range(2)
    ]


def lag_kernel(
    stations, windows, mine_ref, other_ref, near_ref, cross_ref, table_ref, lagged_ref, spec, rows
):
    freq = (table_ref.shape[0] - EDGE_ROWS) // 2
    chunks = freq // LANES
    pair_rows = stations * stations
    total = len(PAIRS) * pair_rows
    unfold(mine_ref, other_ref, near_ref, cross_ref, spec)
    for pair, (first, second) in enumerate(PAIRS):
        real = [[None] * stations for _ in range(stations)]
        imag = [[None] * stations for _ in range(stations)]
        for window in range(windows):
            u = spectrum(spec, stations, windows, chunks, first, window)
            v = spectrum(spec, stations, windows, chunks, second, window)
            for i in range(stations):
                for j in range(stations):
                    re = u[0][i] * v[0][j] + u[1][i] * v[1][j]
                    im = u[1][i] * v[0][j] - u[0][i] * v[1][j]
                    real[i][j] = re if window == 0 else real[i][j] + re
                    imag[i][j] = im if window == 0 else imag[i][j] + im
        for i in range(stations):
            for j in range(stations):
                row = pair * pair_rows + i * stations + j
                rows[row * chunks : (row + 1) * chunks, :] = real[i][j]
                row = row + total
                rows[row * chunks : (row + 1) * chunks, :] = imag[i][j]

    def left(part):
        return jnp.concatenate(
            [
                rows[pl.ds(part * total * chunks + chunk, total, stride=chunks), :].astype(
                    jnp.bfloat16
                )
                for chunk in range(chunks)
            ],
            axis=1,
        )

    half = table_ref.shape[1]
    tile = min(256, half)
    edges = edge_rows(table_ref, freq)
    real, imag = left(0), left(1)
    last_lag = jnp.sum(
        real.astype(jnp.float32) * edges[0] + imag.astype(jnp.float32) * edges[1],
        axis=1,
        keepdims=True,
    )
    first_lane = lax.broadcasted_iota(jnp.int32, (total, tile), 1) == 0
    for place in range(half // tile):
        span = slice(place * tile, (place + 1) * tile)
        even = jnp.dot(real, table_ref[:freq, span], preferred_element_type=jnp.float32)
        odd = jnp.dot(imag, table_ref[freq : 2 * freq, span], preferred_element_type=jnp.float32)
        lagged_ref[:, span] = even + odd
        value = even - odd
        if place == 0:
            value = jnp.where(first_lane, last_lag, value)
        lagged_ref[:, half + place * tile : half + (place + 1) * tile] = value


def response_kernel(
    layers,
    stations,
    windows,
    lagged_ref,
    spec,
    model_near_ref,
    model_last_ref,
    model_moved_ref,
    model_pass_ref,
    table_ref,
    *rest,
):
    far_refs = rest[:layers]
    resp_rows, home_sums, pass_ref, sums, passed = rest[layers:]
    freq = (table_ref.shape[0] - EDGE_ROWS) // 2
    chunks = freq // LANES
    pair_rows = stations * stations
    total = len(PAIRS) * pair_rows
    block_rows = 2 * stations * windows
    size = block_rows * chunks
    core = lax.axis_index("blk") % 2
    home = is_home()
    half = table_ref.shape[1]
    tile = min(256, half)
    edges = edge_rows(table_ref, freq)
    misfit = []
    for place in range(2 * half // tile):
        span = slice(place * tile, (place + 1) * tile)
        last = jnp.where(
            core == 0,
            model_last_ref[:, span].astype(jnp.float32),
            model_moved_ref[:, span].astype(jnp.float32),
        )
        model = jnp.concatenate(
            [
                model_near_ref[:, span].astype(jnp.float32),
                last,
                model_pass_ref[:, span].astype(jnp.float32),
            ],
            axis=0,
        )
        value = jnp.where(model == OUTSIDE, 0.0, lagged_ref[:, span] - model)
        misfit.append(value.astype(jnp.bfloat16))
    count = half // tile
    first_lane = lax.broadcasted_iota(jnp.int32, (total, tile), 1) == 0
    first_behind = misfit[count].astype(jnp.float32)
    last_lag = first_behind[:, :1]
    misfit[count] = jnp.where(first_lane, 0.0, first_behind).astype(jnp.bfloat16)
    stacked = jnp.concatenate(
        [jnp.concatenate(misfit[:count], axis=1), jnp.concatenate(misfit[count:], axis=1)], axis=0
    )
    per_tile = tile // LANES
    for place in range(2 * chunks // per_tile):
        part, chunk = divmod(place * per_tile, chunks)
        low = chunk * LANES
        if low + tile <= half:
            table = table_ref[part * freq : part * freq + half, low : low + tile]
            product = jnp.dot(stacked, table, preferred_element_type=jnp.float32)
        else:
            product = lax.dot_general(
                stacked,
                table_ref[place * tile : (place + 1) * tile, :],
                (((1,), (1,)), ((), ())),
                preferred_element_type=jnp.float32,
            )
        weights = edges[part][:, chunk * LANES : chunk * LANES + tile]
        if part == 0:
            response = product[:total] + product[total:]
        else:
            response = product[:total] - product[total:]
        response = (response + last_lag * weights).astype(jnp.bfloat16).astype(jnp.float32)
        for inner in range(per_tile):
            start = part * total * chunks + chunk + inner
            resp_rows[pl.ds(start, total, stride=chunks), :] = response[
                :, inner * LANES : (inner + 1) * LANES
            ]

    written = set()
    for pair, (first, second) in enumerate(PAIRS):
        r = response_rows(resp_rows, pair, pair_rows, total, chunks)
        for window in range(windows):
            u = spectrum(spec, stations, windows, chunks, first, window)
            for j in range(stations):
                terms_re, terms_im = [], []
                for i in range(stations):
                    re, im = r[0][i * stations + j], r[1][i * stations + j]
                    terms_re.append(re * u[0][i] + im * u[1][i])
                    terms_im.append(re * u[1][i] - im * u[0][i])
                for part, terms in enumerate((terms_re, terms_im)):
                    index = (((second - 2) * 2 + part) * stations + j) * windows + window
                    accumulate(sums, written, index, chunks, terms)
    part_near = sums[:size, :]
    part_last = sums[2 * size :, :]
    home_sums[...] = jnp.where(home, part_near, 0.0)
    passed[:size, :] = jnp.where(home, part_last, 0.0)
    sums[:size, :] = jnp.where(home, 0.0, part_near)
    sums[size : 2 * size, :] += jnp.where(home, 0.0, part_last)
    for place in range(layers):
        step = jnp.where(changed(), 1 - place, place) if place < 2 <= layers else place
        write_share(sums, far_refs[place], step, layers, 2 * block_rows, chunks)

    add_own_terms(1, resp_rows, spec, passed, stations, windows, chunks)
    write_whole(passed, pass_ref, block_rows, chunks)


def own_kernel(
    stations,
    windows,
    resp_rows,
    home_sums,
    spec,
    own_ref,
    sums,
):
    block_rows = 2 * stations * windows
    chunks = spec.shape[0] // (5 * block_rows)
    sums[: block_rows * chunks, :] = home_sums[...]
    add_own_terms(0, resp_rows, spec, sums, stations, windows, chunks)
    write_whole(sums, own_ref, block_rows, chunks)


def add_own_terms(block, resp_rows, spec, sums, stations, windows, chunks):
    pair_rows = stations * stations
    total = len(PAIRS) * pair_rows
    written = set(range(2 * stations * windows))
    for pair, (first, second) in enumerate(PAIRS):
        if first != block:
            continue
        r = response_rows(resp_rows, pair, pair_rows, total, chunks)
        for window in range(windows):
            v = spectrum(spec, stations, windows, chunks, second, window)
            for i in range(stations):
                terms_re, terms_im = [], []
                for j in range(stations):
                    re, im = r[0][i * stations + j], r[1][i * stations + j]
                    terms_re.append(re * v[0][j] - im * v[1][j])
                    terms_im.append(re * v[1][j] + im * v[0][j])
                for part, terms in enumerate((terms_re, terms_im)):
                    index = (part * stations + i) * windows + window
                    accumulate(sums, written, index, chunks, terms)


def write_whole(sums, target, count, chunks):
    for chunk in range(chunks):
        values = sums[pl.ds(chunk, count, stride=chunks), :]
        target[:, chunk * LANES : (chunk + 1) * LANES] = values.astype(target.dtype)


def share_kernel(layers, own_ref, pass_ref, *out_refs):
    width = own_ref.shape[1] // layers
    for step, out_ref in enumerate(out_refs):
        start = lax.rem(lax.axis_index("lay") + step, layers) * width
        span = pl.ds(pl.multiple_of(start, LANES), width)
        total = own_ref[:, span] + pass_ref[:, span].astype(jnp.float32)
        out_ref[...] = total.astype(out_ref.dtype)


def response_rows(resp_rows, pair, pair_rows, total, chunks):
    rows = []
    for part in range(2):
        base = part * total + pair * pair_rows
        rows.append(
            [
                resp_rows[(base + row) * chunks : (base + row + 1) * chunks, :]
                for row in range(pair_rows)
            ]
        )
    return rows


def accumulate(sums, written, index, chunks, terms):
    rows = slice(index * chunks, (index + 1) * chunks)
    value = sum(terms[1:], terms[0])
    if index in written:
        value = value + sums[rows, :]
    written.add(index)
    sums[rows, :] = value


def write_share(sums, target, step, layers, count, chunks):
    width = chunks // layers
    start = lax.rem(lax.axis_index("lay") + step, layers) * width
    for inner in range(width):
        values = sums[pl.ds(start + inner, count, stride=chunks), :]
        target[:, inner * LANES : (inner + 1) * LANES] = values.astype(target.dtype)


def add_kernel(*refs):
    keep_ref, send_ref = refs[-2:]
    total = refs[0][...].astype(jnp.float32)
    for ref in refs[1:-2]:
        total = total + ref[...].astype(jnp.float32)
    half = keep_ref.shape[0]
    keep_ref[...] = total[:half]
    send_ref[...] = total[half:]


def gather_kernel(keep_ref, send_ref, *refs):
    total_ref, out_ref = refs[-2:]
    total = keep_ref[...]
    for ref in refs[:-2]:
        total = total + ref[...].astype(jnp.float32)
    total_ref[...] = total
    out_ref[...] = send_ref[...]


def place_kernel(scale, placing_ref, *refs):
    out_ref = refs[-1]
    parts, stations, windows, _ = out_ref.shape
    total = refs[0][...]
    for ref in refs[1:-1]:
        total = total + ref[...].astype(jnp.float32)
    total = total * scale
    for station in range(stations):
        here = [
            placing_ref[row : row + 1, :]
            for row in range(station, stations * stations, stations)
        ]
        for part in range(parts):
            value = None
            for place in range(stations):
                base = (part * stations + place) * windows
                term = here[place] * total[base : base + windows, :]
                value = term if value is None else value + term
            out_ref[part, station] = value


VMEM = pl.BlockSpec(memory_space=pltpu.VMEM)
HBM = pl.BlockSpec(memory_space=pltpu.HBM)


def grant(mebibytes):
    return pltpu.CompilerParams(vmem_limit_bytes=mebibytes * 1024 * 1024)


def local(spectra, model_corr, window_start, window_end, station_slot):
    _, stations, windows, freq = spectra.shape
    lags = model_corr.shape[4]
    layers = lax.axis_size("lay")
    blocks = lax.axis_size("blk")
    chips = blocks // 2
    chunks = freq // LANES
    pair_rows = stations * stations
    block_rows = 2 * stations * windows
    f32, bf16 = jnp.float32, jnp.bfloat16

    def distance(layer, core):
        if core == 0:
            return 2 * layer + 1
        return 2 * layer if layer > 0 else 2 * layers

    def move(value, target):
        pairs = []
        for block in range(blocks):
            for layer in range(layers):
                chip, core, to_layer = target(block // 2, block % 2, layer)
                pairs.append(
                    (block * layers + layer, (chip % chips * 2 + core) * layers + to_layer % layers)
                )
        return lax.ppermute(value, AXES, pairs)

    def swap_cores(value):
        return move(value, lambda chip, core, layer: (chip, 1 - core, layer))

    station_slot, spectra = (
        pltpu.with_memory_space_constraint(value, pltpu.HBM) for value in (station_slot, spectra)
    )
    mine, placing = pl.pallas_call(
        order_kernel,
        out_shape=[
            jax.ShapeDtypeStruct((block_rows * chunks, LANES), bf16),
            jax.ShapeDtypeStruct((stations * stations, freq // layers), f32),
        ],
        in_specs=[HBM] * 2,
        out_specs=[VMEM] * 2,
        scratch_shapes=[
            pltpu.SMEM(station_slot.shape, jnp.int32),
            pltpu.VMEM(spectra.shape, bf16),
            pltpu.VMEM(((block_rows + 1) * chunks, LANES), f32),
            pltpu.SemaphoreType.DMA((2,)),
        ],
        compiler_params=grant(2),
        cost_estimate=pl.CostEstimate(flops=5 * 10**9, bytes_accessed=10**6, transcendentals=0),
        name="order",
    )(station_slot, spectra)
    cross = move(mine, lambda chip, core, layer: (chip - distance(layer, 1 - core), 1 - core, layer))
    near = move(
        mine,
        lambda chip, core, layer: (
            chip ^ 1 if layer == 0 and core == 1 else chip - distance(layer, core),
            core,
            layer,
        ),
    )
    other = swap_cores(mine)
    model_near, model_last, model_pass = pl.pallas_call(
        mask_kernel,
        out_shape=[
            jax.ShapeDtypeStruct((pair_rows, lags), bf16),
            jax.ShapeDtypeStruct((pair_rows, lags), bf16),
            jax.ShapeDtypeStruct((2 * pair_rows, lags), bf16),
        ],
        in_specs=[VMEM] * 3,
        out_specs=[VMEM] * 3,
        scratch_shapes=[pltpu.VMEM((pair_rows, lags), f32)],
        compiler_params=grant(4),
        cost_estimate=pl.CostEstimate(flops=5 * 10**9, bytes_accessed=10**6, transcendentals=0),
        name="mask",
    )(window_start, window_end, model_corr)
    model_pass = swap_cores(model_pass)
    model_moved = move(model_last, lambda chip, core, layer: (chip, core, layer + 1))
    table = lag_table(freq, lags, windows)
    total = 4 * pair_rows
    blocks_in = (mine, other, near, cross)
    lagged, spec = pl.pallas_call(
        functools.partial(lag_kernel, stations, windows),
        out_shape=[
            jax.ShapeDtypeStruct((total, lags), f32),
            jax.ShapeDtypeStruct((5 * block_rows * chunks, LANES), f32),
        ],
        in_specs=[VMEM] * 5,
        out_specs=[VMEM] * 2,
        scratch_shapes=[pltpu.VMEM(((2 * total + 1) * chunks, LANES), f32)],
        compiler_params=grant(8),
        name="lag",
    )(*blocks_in, table)
    part = (2 * block_rows, freq // layers)
    outs = pl.pallas_call(
        functools.partial(response_kernel, layers, stations, windows),
        out_shape=[jax.ShapeDtypeStruct(part, bf16)] * layers
        + [
            jax.ShapeDtypeStruct(((2 * total + 1) * chunks, LANES), f32),
            jax.ShapeDtypeStruct((block_rows * chunks, LANES), f32),
            jax.ShapeDtypeStruct((block_rows, freq), bf16),
        ],
        in_specs=[VMEM] * 7,
        out_specs=[VMEM] * (layers + 3),
        scratch_shapes=[
            pltpu.VMEM((3 * block_rows * chunks, LANES), f32),
            pltpu.VMEM(((block_rows + 1) * chunks, LANES), f32),
        ],
        compiler_params=grant(12),
        name="response",
    )(lagged, spec, model_near, model_last, model_moved, model_pass, table)
    def returned(place):
        def target(chip, core, layer):
            chip = (chip + distance(layer, core)) % chips
            step = 1 - place if (chip, core) in CHANGED and place < 2 <= layers else place
            return chip, core, layer + step

        return target

    parts = [move(outs[place], returned(place)) for place in range(layers)]
    own = pl.pallas_call(
        functools.partial(own_kernel, stations, windows),
        out_shape=jax.ShapeDtypeStruct((block_rows, freq), f32),
        in_specs=[VMEM] * 3,
        out_specs=VMEM,
        scratch_shapes=[pltpu.VMEM(((block_rows + 1) * chunks, LANES), f32)],
        compiler_params=grant(8),
        name="own",
    )(outs[layers], outs[layers + 1], spec)
    share = (block_rows, freq // layers)
    own = pl.pallas_call(
        functools.partial(share_kernel, layers),
        out_shape=[jax.ShapeDtypeStruct(share, f32)]
        + [jax.ShapeDtypeStruct(share, bf16)] * (layers - 1),
        in_specs=[VMEM] * 2,
        out_specs=[VMEM] * layers,
        compiler_params=grant(2),
        name="share",
    )(own, swap_cores(outs[layers + 2]))
    own = [own[0]] + [
        move(own[step], lambda chip, core, layer: (chip, core, layer + step))
        for step in range(1, layers)
    ]
    firsts = list(range(min(2, layers) - 1, -1, -1)) + list(range(2, layers))
    keep, send = pl.pallas_call(
        add_kernel,
        out_shape=[jax.ShapeDtypeStruct(share, f32)] * 2,
        in_specs=[VMEM] * layers,
        out_specs=[VMEM] * 2,
        compiler_params=grant(2),
        name="arrived",
    )(*[parts[place] for place in firsts])
    keep, send = pl.pallas_call(
        gather_kernel,
        out_shape=[jax.ShapeDtypeStruct(share, f32)] * 2,
        in_specs=[VMEM] * (2 + layers),
        out_specs=[VMEM] * 2,
        compiler_params=grant(2),
        name="gather",
    )(keep, send, *own)
    return pl.pallas_call(
        functools.partial(place_kernel, 1.0 / math.sqrt(blocks * stations)),
        out_shape=jax.ShapeDtypeStruct((2, stations, windows, freq // layers), f32),
        in_specs=[VMEM] * 3,
        out_specs=VMEM,
        compiler_params=grant(2),
        name="place",
    )(placing, keep, swap_cores(send))


def solution(mesh):
    in_specs = (
        P(None, "blk", None, None),
        P("blk", "lay", None, None, None),
        P("blk", "lay"),
        P("blk", "lay"),
        P("blk", None),
    )
    out_specs = P(None, "blk", None, "lay")
    return jax.shard_map(local, mesh=mesh, in_specs=in_specs, out_specs=out_specs, check_vma=False)
```
